128 devices in a mesh: cls: 4 (over x_hi, core), prt: 32 (over x_lo, z, y).
Axes of the slice: x: 4 (x_hi: 2, x_lo: 2; x = x_hi * 2 + x_lo), y: 4, z: 4, core: 2. Of those that a mesh axis runs over, the one named last changes fastest.
Arguments:
- images: bfloat16 [16384, 7168], P(('cls', 'prt')), may hold values from -48 to 48
- projections: bfloat16 [8, 144, 7168], P('cls', None, 'prt'), may hold values from -5 to 5
- noise_weights: float32 [7168], replicated, may hold values from 0.005 to 0.03
- class_prior: float32 [8], replicated, may hold values from 0.05 to 1
- class_lists: int32 [16384, 2], P(('cls', 'prt')), may hold values from 0 to 7, all different within a row; in each aligned block of 128 rows (0 to 127, 128 to 255, ...) at most 40 rows name the same one
Outputs:
- class_sums: float32 [8, 144, 7168], P('cls', None, 'prt')
- class_weights: float32 [8, 144], P('cls')
- evidence: float32 [16384], P(('cls', 'prt'))
The draws below stay inside these ranges and needn't reach their ends.
Inputs may be any that keep to these rules, and one draw needn't show every extreme that they name: `class_lists`: each row names 2 different classes; in the rows of one device no class is named by more than 40 rows, a bound that some block reaches.
All inputs are finite; a program needn't handle non-finite values.
Results may differ from the reference program's by a relative error of at most 0.0066.
Values may be sent and summed in bfloat16 or wider, within the bound.
A program may use at most 128 MiB of HBM per device.

```python
import math
import jax
import jax.numpy as jnp
import numpy as np
from jax import lax

K = 8
R = 144
C = 2
ROWS = 128
COEF2 = 7168
MOST = 40
NPART = 16384


def stack_of(key):
    return jnp.clip(jax.random.normal(jax.random.fold_in(key, 7), (K, R, COEF2), jnp.float32), -5.0, 5.0)


def draw_projections(key, part):
    return stack_of(key).astype(jnp.bfloat16)


def draw_images(key, part):
    values = jax.random.normal(jax.random.fold_in(key, 11), (NPART, COEF2), jnp.float32)
    return jnp.clip(values, -48.0, 48.0).astype(jnp.bfloat16)


def shared_out(rng, own, number, rows, amount, top, reach, skew):
    sequence = jax.random.permutation(rng, amount)
    heavy_load, ordinary = load_shares(amount, rows * top, reach, skew, True), load_shares(amount, rows * top, reach, skew, False)
    places = jnp.arange(amount)

    def named(tallies, rotation):
        used = int((tallies > 0).sum())
        fixed = max(1, used // 4)
        moved = fixed + (places - fixed + rotation * (used - fixed)) % max(1, amount - fixed)
        return jnp.zeros((amount,), jnp.int32).at[sequence[jnp.where(places < fixed, places, moved)]].set(jnp.asarray(tallies, jnp.int32))

    tallies = jnp.where(number % 4 == 0, named(heavy_load, number // 4), named(ordinary, number - number // 4 - 1))
    mixed = jax.random.permutation(jax.random.fold_in(own, 3), amount)
    source_of, sink = mixed[0:amount // 2 * 2:2], mixed[1:amount // 2 * 2:2]
    margin = jnp.minimum(tallies[source_of] - 1, reach - tallies[sink]) // 2
    margin = jnp.where((source_of == sequence[0]) | (sink == sequence[0]) | (tallies[sink] == 0), 0, jnp.maximum(margin, 0))
    moved = jax.random.randint(jax.random.fold_in(own, 4), (amount // 2,), 0, 1 << 20) % (margin + 1)
    tallies = tallies.at[source_of].add(-moved).at[sink].add(moved)
    items = jnp.searchsorted(jnp.cumsum(tallies), jnp.arange(rows * top), side="right").astype(jnp.int32)
    table = items.reshape(top, rows).T
    table = table[jax.random.permutation(jax.random.fold_in(own, 1), rows)]
    rotation = jax.random.randint(jax.random.fold_in(own, 2), (rows, 1), 0, top)
    return jnp.take_along_axis(table, (jnp.arange(top)[None, :] + rotation) % top, axis=1)


def load_shares(number_of, total, limit, slope, full):
    loads = [(1 << 20) // math.isqrt(rank ** slope) + 1 for rank in range(1, number_of + 1)]
    largest = limit if full else min(limit, max(-(-total // number_of), total * loads[0] // sum(loads)))
    least = 1 if total - largest >= number_of - 1 else 0
    holding, rest = [largest] + [least] * (number_of - 1), total - largest - least * (number_of - 1)
    while rest > 0:
        movable = [i for i in range(1, number_of) if holding[i] < largest] or [i for i in range(1, number_of) if holding[i] < limit]
        whole, remaining = sum([loads[i] for i in movable]), rest
        for i in movable:
            addition = min(limit - holding[i], max(1, remaining * loads[i] // whole), rest)
            holding[i] = holding[i] + addition
            rest = rest - addition
    return np.array(holding)


def setup_inputs(seed: int = 0) -> dict:
    splits = jax.random.split(jax.random.key(seed), 6)
    images = draw_images(jax.random.fold_in(splits[5], 71), 0)
    projections = draw_projections(jax.random.fold_in(splits[5], 71), 0)
    noise_weights = jnp.clip(jnp.exp(jax.random.uniform(splits[2], (COEF2,), jnp.float32, math.log(0.005), math.log(0.03))), 0.005, 0.03)
    class_prior = jnp.clip(jnp.exp(jax.random.uniform(splits[3], (K,), jnp.float32, math.log(0.05), math.log(1.0))), 0.05, 1.0)
    class_lists_keys = jax.random.split(jax.random.fold_in(splits[4], 1), NPART // ROWS)
    class_lists_turns = jax.random.permutation(jax.random.fold_in(splits[4], 3), NPART // ROWS)
    class_lists = jax.vmap(lambda own, number: shared_out(jax.random.fold_in(splits[4], 2), own, number, ROWS, K, C, MOST, 2))(class_lists_keys, class_lists_turns).reshape((NPART, C))
    return {"images": images, "projections": projections, "noise_weights": noise_weights, "class_prior": class_prior, "class_lists": class_lists}


def reference(images, projections, noise_weights, class_prior, class_lists):
    proj_float = projections.astype(jnp.float32)
    norms = 0.5 * jnp.sum(proj_float * proj_float * noise_weights[None, None, :], axis=2)
    weighted = (images.astype(jnp.float32) * noise_weights[None, :]).astype(jnp.bfloat16)
    flat = projections.reshape(K * R, COEF2)
    listed = jnp.any(class_lists[:, :, None] == jnp.arange(K, dtype=jnp.int32)[None, None, :], axis=1)
    log_prior = jnp.log(class_prior)
    blk = 1024 if NPART % 1024 == 0 else NPART
    count = NPART // blk

    def block(args):
        wrows, lrows = args
        cross = lax.dot_general(wrows, flat, (((1,), (1,)), ((), ())), preferred_element_type=jnp.float32).reshape(blk, K, R)
        score = cross - norms[None, :, :] + log_prior[None, :, None]
        score = jnp.where(lrows[:, :, None], score, -jnp.inf)
        top = jnp.max(score, axis=(1, 2))
        total = jnp.sum(jnp.exp(score - top[:, None, None]), axis=(1, 2))
        evid = top + jnp.log(total)
        post = jnp.exp(score - evid[:, None, None]).astype(jnp.bfloat16)
        return evid, post

    evid, post = lax.map(block, (weighted.reshape(count, blk, COEF2), listed.reshape(count, blk, K)))
    evidence = evid.reshape(NPART)
    post = post.reshape(NPART, K, R)
    sums = []
    for k in range(K):
        sums.append(jnp.dot(post[:, k, :].T, images, preferred_element_type=jnp.float32))
    class_sums = jnp.stack(sums, axis=0)
    class_weights = jnp.sum(post.astype(jnp.float32), axis=0)
    return class_sums, class_weights, evidence
```

```python
import jax
import jax.numpy as jnp
from jax import lax
from jax.experimental import pallas as pl
from jax.experimental.pallas import tpu as pltpu
from jax.sharding import Mesh
from jax.sharding import PartitionSpec as P

AXES = ("xh", "c", "xl", "z", "y")
MESH = pl.DeviceIdType.MESH
R = 144
ROWS = 128
CH = 224
PAD = 256
PIECE = 4 * CH
F32 = jnp.float32
BF16 = jnp.bfloat16


def kernel(
    img_ref, proj_ref, nw_ref, prior_ref, list_ref,
    out_ref, evid_ref,
    img, lists, xb, wb, nwp, pb, norm, cross, sbuf, srecv, post, pt,
    mb, mr, sb, ra, rb, t2a, t2b, ga, gb, fa, fb,
    own_sem, img_ss, img_rs, list_ss, list_rs, p1_ss, p1_rs, p2_ss, p2_rs, pm_ss, pm_rs,
    s_ss, s_rs, q_ss, q_rs, m_ss, m_rs, r1_ss, r1_rs, r2_ss, r2_rs,
):
    xh, c, xl = lax.axis_index("xh"), lax.axis_index("c"), lax.axis_index("xl")
    z, y = lax.axis_index("z"), lax.axis_index("y")
    x = 2 * xh + xl
    mate = (xh, 1 - c, xl, z, y)

    def at_x(s):
        t = lax.rem(x + s, 4)
        return (lax.div(t, 2), c, lax.rem(t, 2), z, y)

    def at_y(s):
        return (xh, c, xl, z, lax.rem(y + s, 4))

    def at_z(s):
        return (xh, c, xl, lax.rem(z + s, 4), y)

    def remote(src, dst, ss, rs, dev):
        return pltpu.make_async_remote_copy(
            src_ref=src, dst_ref=dst, send_sem=ss, recv_sem=rs, device_id=dev, device_id_type=MESH
        )

    barrier = pltpu.get_barrier_semaphore()
    pl.semaphore_signal(barrier, inc=1, device_id=mate, device_id_type=MESH)
    for s in (1, 2, 3):
        for dev in (at_x(s), at_y(s), at_z(s)):
            pl.semaphore_signal(barrier, inc=1, device_id=dev, device_id_type=MESH)

    for q in range(2):
        pb[xl, y, xh, c, q] = jnp.zeros((R, PAD), BF16)
        pb[xl, y, xh, c, q, :, 0:CH] = proj_ref[q]
    lists[0] = list_ref[...]

    own = []
    for p in range(2):
        own.append(
            pltpu.make_async_copy(
                img_ref.at[:, pl.ds(pl.multiple_of((p * 4 + z) * PIECE, 128), PIECE)],
                img.at[0, :, pl.ds(p * PIECE, PIECE)],
                own_sem.at[p],
            )
        )
        own[p].start()

    pl.semaphore_wait(barrier, 10)

    p1 = {}
    for s in (1, 2, 3):
        block = pb.at[xl, y, xh, c, 0]
        p1["a", s] = remote(block, block, p1_ss.at[0, s - 1], p1_rs.at[0, s - 1], at_y(s))
        p1["a", s].start()
        block = pb.at[xl, y, xh, c, 1]
        p1["b", s] = remote(block, block, p1_ss.at[1, s - 1], p1_rs.at[1, s - 1], at_x(s))
        p1["b", s].start()
    lcp, icp = {}, {}
    for s in (1, 3, 2):
        lcp[s] = remote(lists.at[0], lists.at[s], list_ss.at[s - 1], list_rs.at[s - 1], at_z(s))
        lcp[s].start()
        for p in range(2):
            to = lax.rem(z + s, 4)
            icp[s, p] = remote(
                img_ref.at[:, pl.ds(pl.multiple_of((p * 4 + to) * PIECE, 128), PIECE)],
                img.at[s, :, pl.ds(p * PIECE, PIECE)],
                img_ss.at[s - 1, p], img_rs.at[s - 1, p], at_z(s),
            )
            icp[s, p].start()

    nwp[...] = jnp.zeros_like(nwp)
    for p in range(2):
        row = (p * 4 + z) * 7
        flat = jnp.concatenate([nw_ref[pl.ds(row + t, 1), :] for t in range(7)], axis=1)
        for k in range(4):
            j = p * 4 + k
            nwp[:, j * PAD : j * PAD + CH] = flat[:, k * CH : (k + 1) * CH]

    def spread(s):
        ones = jnp.where(lax.broadcasted_iota(jnp.int32, (ROWS, 128), 1) == CH - 128, 1.0, 0.0)
        for p in range(2):
            piece = img[s, :, p * PIECE : (p + 1) * PIECE].astype(F32)
            for k in range(4):
                j = p * 4 + k
                chunk = piece[:, k * CH : (k + 1) * CH]
                xb[j, s * ROWS : (s + 1) * ROWS, 128:PAD] = ones.astype(BF16)
                xb[j, s * ROWS : (s + 1) * ROWS, 0:CH] = chunk.astype(BF16)
                full = xb[j, s * ROWS : (s + 1) * ROWS, :].astype(F32)
                wb[s, :, j * PAD : (j + 1) * PAD] = (
                    full * nwp[:, j * PAD : (j + 1) * PAD]
                ).astype(BF16)

    own[0].wait()
    own[1].wait()
    spread(0)

    p2, pm = {}, {}

    def mate_copy(half, s):
        if half == 0:
            t = lax.rem(x + 4 - s, 4)
            block = pb.at[lax.rem(t, 2), :, lax.div(t, 2), c, 0]
        else:
            block = pb.at[:, lax.rem(y + 4 - s, 4), :, c, 1]
        pm[half, s] = remote(block, block, pm_ss.at[half, s], pm_rs.at[half, s], mate)
        pm[half, s].start()

    for half in range(2):
        for s in (1, 2, 3):
            p1["ab"[half], s].wait_recv()
        for s in (1, 2, 3):
            block = pb.at[xl, :, xh, c, 0] if half == 0 else pb.at[:, y, :, c, 1]
            p2[half, s] = remote(
                block, block, p2_ss.at[half, s - 1], p2_rs.at[half, s - 1],
                at_x(s) if half == 0 else at_y(s),
            )
            p2[half, s].start()
        mate_copy(half, 0)

    for s in (1, 3):
        icp[s, 0].wait_recv()
        icp[s, 1].wait_recv()
        spread(s)

    for s in (1, 3, 2):
        for half in range(2):
            p2[half, s].wait_recv()
            mate_copy(half, s)
    for s in range(4):
        for half in range(2):
            pm[half, s].wait_recv()
    for s in (1, 2, 3):
        lcp[s].wait_recv()

    def norm_body(k, carry):
        kh, kc, kq = lax.div(k, 4), lax.rem(lax.div(k, 2), 2), lax.rem(k, 2)
        acc = jnp.zeros((R, PAD), F32)
        for j in range(8):
            v = pb[j // 4, j % 4, kh, kc, kq].astype(F32)
            acc = acc + v * v * nwp[:, j * PAD : (j + 1) * PAD]
        norm[k] = jnp.broadcast_to(0.5 * jnp.sum(acc, axis=1, keepdims=True), (R, ROWS))
        return carry

    lax.fori_loop(0, 8, norm_body, 0)

    scp = {}

    def scores(s):
        def body(k, carry):
            kh, kc, kq = lax.div(k, 4), lax.rem(lax.div(k, 2), 2), lax.rem(k, 2)
            left = jnp.concatenate([pb[j // 4, j % 4, kh, kc, kq] for j in range(8)], axis=1)
            part = lax.dot_general(
                left, wb[s], (((1,), (1,)), ((), ())), preferred_element_type=F32
            )
            part = part - norm[k]
            for slot in range(2):
                hit = jnp.broadcast_to(lists[s, slot : slot + 1, :] == k, (R, ROWS))
                sbuf[s, slot] = jnp.where(hit, part, sbuf[s, slot])
            return carry

        lax.fori_loop(0, 8, body, 0)
        if s:
            scp[s] = remote(
                sbuf.at[s], srecv.at[s - 1], s_ss.at[s - 1], s_rs.at[s - 1], at_z(4 - s)
            )
            scp[s].start()

    sbuf[...] = jnp.zeros_like(sbuf)
    for s in (1, 3, 0):
        scores(s)
    icp[2, 0].wait_recv()
    icp[2, 1].wait_recv()
    spread(2)
    scores(2)

    for s in (1, 3, 2):
        scp[s].wait_recv()
    score = []
    for slot in range(2):
        prior = jnp.ones((1, ROWS), F32)
        for k in range(8):
            prior = jnp.where(lists[0, slot : slot + 1, :] == k, prior_ref[k], prior)
        total = (sbuf[0, slot] + srecv[0, slot]) + (srecv[1, slot] + srecv[2, slot])
        score.append(total + jnp.log(prior))
    top = jnp.maximum(
        jnp.max(score[0], axis=0, keepdims=True), jnp.max(score[1], axis=0, keepdims=True)
    )
    mass = jnp.sum(jnp.exp(score[0] - top), axis=0, keepdims=True) + jnp.sum(
        jnp.exp(score[1] - top), axis=0, keepdims=True
    )
    evid = top + jnp.log(mass)
    evid_ref[...] = evid
    for slot in range(2):
        post[0, slot] = jnp.exp(score[slot] - evid).astype(BF16)

    qcp = {}
    for s in (2, 1, 3):
        qcp[s] = remote(post.at[0], post.at[s], q_ss.at[s - 1], q_rs.at[s - 1], at_z(s))
        qcp[s].start()

    def expand(s):
        def body(k, carry):
            kh, kc, kq = lax.div(k, 4), lax.rem(lax.div(k, 2), 2), lax.rem(k, 2)
            value = jnp.zeros((R, ROWS), F32)
            for slot in range(2):
                hit = jnp.broadcast_to(lists[s, slot : slot + 1, :] == k, (R, ROWS))
                value = jnp.where(hit, post[s, slot].astype(F32), value)
            pt[kc, kh, kq, :, s * ROWS : (s + 1) * ROWS] = value.astype(BF16)
            return carry

        lax.fori_loop(0, 8, body, 0)

    expand(0)
    for s in (1, 3, 2):
        qcp[s].wait_recv()
        expand(s)

    def mate_sum(j):
        jl, jy = lax.div(j, 4), lax.rem(j, 4)
        return remote(mb.at[jl, jy], mr.at[jl, jy], m_ss.at[j], m_rs.at[j], mate)

    def product(which, j):
        left = pt[which].reshape(4 * R, 4 * ROWS)
        return jnp.dot(left, xb[j], preferred_element_type=F32).reshape(2, 2, R, PAD)

    def other_body(j, carry):
        mb[lax.div(j, 4), lax.rem(j, 4)] = product(1 - c, j).astype(BF16)
        mate_sum(j).start()
        return carry

    lax.fori_loop(0, 8, other_body, 0)

    def own_body(j, carry):
        jl, jy = lax.div(j, 4), lax.rem(j, 4)
        mine = product(c, j)
        mate_sum(j).wait_recv()
        sb[jl, jy] = (mine + mr[jl, jy].astype(F32)).astype(BF16)
        return carry

    lax.fori_loop(0, 8, own_body, 0)

    r1, r2 = {}, {}
    for s in (2, 1, 3):
        t = lax.rem(x + s, 4)
        r1[0, s] = remote(
            sb.at[lax.rem(t, 2), :, lax.div(t, 2), 0], ra.at[s - 1],
            r1_ss.at[0, s - 1], r1_rs.at[0, s - 1], at_x(s),
        )
        r1[0, s].start()
        r1[1, s] = remote(
            sb.at[:, lax.rem(y + s, 4), :, 1], rb.at[s - 1],
            r1_ss.at[1, s - 1], r1_rs.at[1, s - 1], at_y(s),
        )
        r1[1, s].start()
    for s in (1, 2, 3):
        r1[0, s].wait_recv()
    ga[...] = sb[xl, :, xh, 0].astype(F32)
    for s in range(3):
        ga[...] += ra[s].astype(F32)
    t2a[...] = ga[...].astype(BF16)
    for s in (2, 1, 3):
        r2[0, s] = remote(
            t2a.at[lax.rem(y + s, 4)], fa.at[s - 1], r2_ss.at[0, s - 1], r2_rs.at[0, s - 1], at_y(s)
        )
        r2[0, s].start()
    for s in (1, 2, 3):
        r1[1, s].wait_recv()
    gb[...] = sb[:, y, :, 1].astype(F32)
    for s in range(3):
        gb[...] += rb[s].astype(F32)
    t2b[...] = gb[...].astype(BF16)
    for s in (2, 1, 3):
        t = lax.rem(x + s, 4)
        r2[1, s] = remote(
            t2b.at[lax.rem(t, 2), lax.div(t, 2)], fb.at[s - 1],
            r2_ss.at[1, s - 1], r2_rs.at[1, s - 1], at_x(s),
        )
        r2[1, s].start()

    for half, kept, came in ((0, ga.at[y], fa), (1, gb.at[xl, xh], fb)):
        for s in (1, 2, 3):
            r2[half, s].wait_recv()
        out_ref[half] = (kept[...] + came[0].astype(F32)) + (
            came[1].astype(F32) + came[2].astype(F32)
        )

    for group in (p1, lcp, icp, p2, pm, scp, qcp, r1, r2):
        for cp in group.values():
            cp.wait_send()

    def mate_done(j, carry):
        mate_sum(j).wait_send()
        return carry

    lax.fori_loop(0, 8, mate_done, 0)


def local(images, projections, noise_weights, class_prior, class_lists):
    dma = pltpu.SemaphoreType.DMA
    vmem = pl.BlockSpec(memory_space=pltpu.VMEM)
    sums, evidence = pl.pallas_call(
        kernel,
        name="estep",
        out_shape=(
            jax.ShapeDtypeStruct((2, R, PAD), F32),
            jax.ShapeDtypeStruct((1, ROWS), F32),
        ),
        in_specs=[
            pl.BlockSpec(memory_space=pl.ANY), vmem, vmem,
            pl.BlockSpec(memory_space=pltpu.SMEM), vmem,
        ],
        out_specs=(vmem, vmem),
        scratch_shapes=[
            pltpu.VMEM((4, ROWS, 2 * PIECE), BF16),
            pltpu.VMEM((4, 2, ROWS), jnp.int32),
            pltpu.VMEM((8, 4 * ROWS, PAD), BF16),
            pltpu.VMEM((4, ROWS, 8 * PAD), BF16),
            pltpu.VMEM((1, 8 * PAD), F32),
            pltpu.VMEM((2, 4, 2, 2, 2, R, PAD), BF16),
            pltpu.VMEM((8, R, ROWS), F32),
            pltpu.VMEM((8, 128), F32),
            pltpu.VMEM((4, 2, R, ROWS), F32),
            pltpu.VMEM((3, 2, R, ROWS), F32),
            pltpu.VMEM((4, 2, R, ROWS), BF16),
            pltpu.VMEM((2, 2, 2, R, 4 * ROWS), BF16),
            pltpu.VMEM((2, 4, 2, 2, R, PAD), BF16),
            pltpu.VMEM((2, 4, 2, 2, R, PAD), BF16),
            pltpu.VMEM((2, 4, 2, 2, R, PAD), BF16),
            pltpu.VMEM((3, 4, R, PAD), BF16),
            pltpu.VMEM((3, 2, 2, R, PAD), BF16),
            pltpu.VMEM((4, R, PAD), BF16),
            pltpu.VMEM((2, 2, R, PAD), BF16),
            pltpu.VMEM((4, R, PAD), F32),
            pltpu.VMEM((2, 2, R, PAD), F32),
            pltpu.VMEM((3, R, PAD), BF16),
            pltpu.VMEM((3, R, PAD), BF16),
            dma((2,)),
            dma((3, 2)), dma((3, 2)),
            dma((3,)), dma((3,)),
            dma((2, 3)), dma((2, 3)),
            dma((2, 3)), dma((2, 3)),
            dma((2, 4)), dma((2, 4)),
            dma((3,)), dma((3,)),
            dma((3,)), dma((3,)),
            dma((8,)), dma((8,)),
            dma((2, 3)), dma((2, 3)),
            dma((2, 3)), dma((2, 3)),
        ],
        compiler_params=pltpu.CompilerParams(
            collective_id=0, has_side_effects=True, vmem_limit_bytes=56 * 2**20
        ),
    )(images, projections, noise_weights.reshape(56, 128), class_prior, class_lists.T)
    return sums[:, :, :CH], sums[:, :, CH], evidence.reshape(ROWS)


def solution(mesh):
    finer = Mesh(mesh.devices.reshape(2, 2, 2, 4, 4), AXES)
    rows, cls, prt = P(AXES, None), ("xh", "c"), ("xl", "z", "y")
    return jax.shard_map(
        local,
        mesh=finer,
        in_specs=(rows, P(cls, None, prt), P(), P(), rows),
        out_specs=(P(cls, None, prt), P(cls, None), P(AXES)),
        check_vma=False,
    )
```

```python
import jax
import jax.numpy as jnp
from jax import lax
from jax.experimental import pallas as pl
from jax.experimental.pallas import tpu as pltpu
from jax.sharding import Mesh
from jax.sharding import PartitionSpec as P

AXES = ("xh", "c", "xl", "z", "y")
MESH = pl.DeviceIdType.MESH
R = 144
ROWS = 128
CH = 224
PAD = 256
PIECE = 4 * CH
PLACE = {0: 0, 1: 1, 3: 2, 2: 3}
F32 = jnp.float32
BF16 = jnp.bfloat16


def kernel(
    img_ref, proj_ref, nw_ref, prior_ref, list_ref,
    out_ref, evid_ref,
    img, lists, xb, wb, nwp, pb, norm, cross, sbuf, srecv, post, pt,
    mb, mr, sb, ra, rb, t2a, t2b, ga, gb, fa, fb,
    own_sem, img_ss, img_rs, list_ss, list_rs, p1_ss, p1_rs, p2_ss, p2_rs, pm_ss, pm_rs,
    s_ss, s_rs, q_ss, q_rs, m_ss, m_rs, xa_ss, xa_rs, yb_ss, yb_rs, r2_ss, r2_rs,
):
    xh, c, xl = lax.axis_index("xh"), lax.axis_index("c"), lax.axis_index("xl")
    z, y = lax.axis_index("z"), lax.axis_index("y")
    x = 2 * xh + xl
    mate = (xh, 1 - c, xl, z, y)

    def at_x(s):
        t = lax.rem(x + s, 4)
        return (lax.div(t, 2), c, lax.rem(t, 2), z, y)

    def at_y(s):
        return (xh, c, xl, z, lax.rem(y + s, 4))

    def at_z(s):
        return (xh, c, xl, lax.rem(z + s, 4), y)

    def remote(src, dst, ss, rs, dev):
        return pltpu.make_async_remote_copy(
            src_ref=src, dst_ref=dst, send_sem=ss, recv_sem=rs, device_id=dev, device_id_type=MESH
        )

    barrier = pltpu.get_barrier_semaphore()
    pl.semaphore_signal(barrier, inc=1, device_id=mate, device_id_type=MESH)
    for s in (1, 2, 3):
        for dev in (at_x(s), at_y(s), at_z(s)):
            pl.semaphore_signal(barrier, inc=1, device_id=dev, device_id_type=MESH)

    for q in range(2):
        pb[xl, y, xh, c, q] = jnp.zeros((R, PAD), BF16)
        pb[xl, y, xh, c, q, :, 0:CH] = proj_ref[q]
    lists[0] = list_ref[...]

    own = []
    for p in range(2):
        own.append(
            pltpu.make_async_copy(
                img_ref.at[:, pl.ds(pl.multiple_of((p * 4 + z) * PIECE, 128), PIECE)],
                img.at[0, :, pl.ds(p * PIECE, PIECE)],
                own_sem.at[p],
            )
        )
        own[p].start()

    pl.semaphore_wait(barrier, 10)

    p1 = {}
    for s in (1, 2, 3):
        block = pb.at[xl, y, xh, c, 0]
        p1["a", s] = remote(block, block, p1_ss.at[0, s - 1], p1_rs.at[0, s - 1], at_y(s))
        p1["a", s].start()
        block = pb.at[xl, y, xh, c, 1]
        p1["b", s] = remote(block, block, p1_ss.at[1, s - 1], p1_rs.at[1, s - 1], at_x(s))
        p1["b", s].start()
    lcp, icp = {}, {}
    for s in (1, 3, 2):
        lcp[s] = remote(lists.at[0], lists.at[s], list_ss.at[s - 1], list_rs.at[s - 1], at_z(s))
        lcp[s].start()
        for p in range(2):
            to = lax.rem(z + s, 4)
            icp[s, p] = remote(
                img_ref.at[:, pl.ds(pl.multiple_of((p * 4 + to) * PIECE, 128), PIECE)],
                img.at[s, :, pl.ds(p * PIECE, PIECE)],
                img_ss.at[s - 1, p], img_rs.at[s - 1, p], at_z(s),
            )
            icp[s, p].start()

    nwp[...] = jnp.zeros_like(nwp)
    for p in range(2):
        row = (p * 4 + z) * 7
        flat = jnp.concatenate([nw_ref[pl.ds(row + t, 1), :] for t in range(7)], axis=1)
        for k in range(4):
            j = p * 4 + k
            nwp[:, j * PAD : j * PAD + CH] = flat[:, k * CH : (k + 1) * CH]

    def spread(s):
        ones = jnp.where(lax.broadcasted_iota(jnp.int32, (ROWS, 128), 1) == CH - 128, 1.0, 0.0)
        rows = slice(PLACE[s] * ROWS, (PLACE[s] + 1) * ROWS)
        for p in range(2):
            piece = img[s, :, p * PIECE : (p + 1) * PIECE].astype(F32)
            for k in range(4):
                j = p * 4 + k
                chunk = piece[:, k * CH : (k + 1) * CH]
                xb[j, rows, 128:PAD] = ones.astype(BF16)
                xb[j, rows, 0:CH] = chunk.astype(BF16)
                full = xb[j, rows, :].astype(F32)
                wb[j, rows, :] = (full * nwp[:, j * PAD : (j + 1) * PAD]).astype(BF16)

    own[0].wait()
    own[1].wait()
    spread(0)

    p2, pm = {}, {}

    def mate_copy(half, s):
        if half == 0:
            t = lax.rem(x + 4 - s, 4)
            block = pb.at[lax.rem(t, 2), :, lax.div(t, 2), c, 0]
        else:
            block = pb.at[:, lax.rem(y + 4 - s, 4), :, c, 1]
        pm[half, s] = remote(block, block, pm_ss.at[half, s], pm_rs.at[half, s], mate)
        pm[half, s].start()

    for half in range(2):
        for s in (1, 2, 3):
            p1["ab"[half], s].wait_recv()
        for s in (1, 2, 3):
            block = pb.at[xl, :, xh, c, 0] if half == 0 else pb.at[:, y, :, c, 1]
            p2[half, s] = remote(
                block, block, p2_ss.at[half, s - 1], p2_rs.at[half, s - 1],
                at_x(s) if half == 0 else at_y(s),
            )
            p2[half, s].start()
        mate_copy(half, 0)

    for s in (1, 3):
        icp[s, 0].wait_recv()
        icp[s, 1].wait_recv()
        spread(s)

    for s in (1, 3, 2):
        for half in range(2):
            p2[half, s].wait_recv()
            mate_copy(half, s)
    for s in range(4):
        for half in range(2):
            pm[half, s].wait_recv()
    for s in (1, 2, 3):
        lcp[s].wait_recv()

    def norm_body(k, carry):
        kh, kc, kq = lax.div(k, 4), lax.rem(lax.div(k, 2), 2), lax.rem(k, 2)
        acc = jnp.zeros((R, PAD), F32)
        for j in range(8):
            v = pb[j // 4, j % 4, kh, kc, kq].astype(F32)
            acc = acc + v * v * nwp[:, j * PAD : (j + 1) * PAD]
        norm[k] = jnp.broadcast_to(0.5 * jnp.sum(acc, axis=1, keepdims=True), (R, ROWS))
        return carry

    lax.fori_loop(0, 8, norm_body, 0)

    def products(first, last):
        rows = slice(first * ROWS, last * ROWS)
        left = jnp.concatenate([pb[j // 4, j % 4].reshape(8 * R, PAD) for j in range(8)], axis=1)
        right = jnp.concatenate([wb[j, rows, :] for j in range(8)], axis=1)
        cross[:, rows] = lax.dot_general(
            left, right, (((1,), (1,)), ((), ())), preferred_element_type=F32
        )

    scp = {}

    def scores(s):
        lanes = slice(PLACE[s] * ROWS, (PLACE[s] + 1) * ROWS)

        def body(i, carry):
            start = pl.multiple_of(i * 16, 16)
            listed = [jnp.broadcast_to(lists[s, t : t + 1, :], (16, ROWS)) for t in range(2)]
            chosen = [jnp.zeros((16, ROWS), F32)] * 2
            for k in range(8):
                part = cross[pl.ds(k * R + start, 16), lanes] - norm[k, pl.ds(start, 16), :]
                for t in range(2):
                    chosen[t] = jnp.where(listed[t] == k, part, chosen[t])
            for t in range(2):
                sbuf[s, t, pl.ds(start, 16), :] = chosen[t]
            return carry

        lax.fori_loop(0, R // 16, body, 0)
        if s:
            scp[s] = remote(
                sbuf.at[s], srecv.at[s - 1], s_ss.at[s - 1], s_rs.at[s - 1], at_z(4 - s)
            )
            scp[s].start()

    products(0, 3)
    for s in (1, 3, 0):
        scores(s)
    icp[2, 0].wait_recv()
    icp[2, 1].wait_recv()
    spread(2)
    products(3, 4)
    scores(2)

    for s in (1, 3, 2):
        scp[s].wait_recv()
    score = []
    for slot in range(2):
        prior = jnp.ones((1, ROWS), F32)
        for k in range(8):
            prior = jnp.where(lists[0, slot : slot + 1, :] == k, prior_ref[k], prior)
        total = (sbuf[0, slot] + srecv[0, slot]) + (srecv[1, slot] + srecv[2, slot])
        score.append(total + jnp.log(prior))
    top = jnp.maximum(
        jnp.max(score[0], axis=0, keepdims=True), jnp.max(score[1], axis=0, keepdims=True)
    )
    mass = jnp.sum(jnp.exp(score[0] - top), axis=0, keepdims=True) + jnp.sum(
        jnp.exp(score[1] - top), axis=0, keepdims=True
    )
    evid = top + jnp.log(mass)
    evid_ref[...] = evid
    for slot in range(2):
        post[0, slot] = jnp.exp(score[slot] - evid).astype(BF16)

    qcp = {}
    for s in (2, 1, 3):
        qcp[s] = remote(post.at[0], post.at[s], q_ss.at[s - 1], q_rs.at[s - 1], at_z(s))
        qcp[s].start()

    def expand(s):
        def body(k, carry):
            kh, kc, kq = lax.div(k, 4), lax.rem(lax.div(k, 2), 2), lax.rem(k, 2)
            value = jnp.zeros((R, ROWS), F32)
            for slot in range(2):
                hit = jnp.broadcast_to(lists[s, slot : slot + 1, :] == k, (R, ROWS))
                value = jnp.where(hit, post[s, slot].astype(F32), value)
            pt[kc, kh, kq, :, PLACE[s] * ROWS : (PLACE[s] + 1) * ROWS] = value.astype(BF16)
            return carry

        lax.fori_loop(0, 8, body, 0)

    expand(0)
    for s in (1, 3, 2):
        qcp[s].wait_recv()
        expand(s)

    def chunk_of(i):
        return lax.rem(i, 2), lax.rem(y + lax.div(i, 2), 4)

    def mate_sum(i):
        jl, jy = chunk_of(i)
        return remote(mb.at[jl, jy], mr.at[jl, jy], m_ss.at[i], m_rs.at[i], mate)

    def product(which, j):
        left = pt[which].reshape(4 * R, 4 * ROWS)
        return jnp.dot(left, xb[j], preferred_element_type=F32).reshape(2, 2, R, PAD)

    def along_x(i, s):
        jy = lax.rem(y + i, 4)
        t = lax.rem(x + s, 4)
        return remote(
            sb.at[lax.rem(t, 2), jy, lax.div(t, 2), 0], ra.at[s - 1, i],
            xa_ss.at[s - 1, i], xa_rs.at[s - 1, i], at_x(s),
        )

    def along_y(i, jl):
        return remote(
            sb.at[jl, lax.rem(y + i, 4), :, 1], rb.at[i - 1, jl],
            yb_ss.at[i - 1, jl], yb_rs.at[i - 1, jl], at_y(i),
        )

    def other(i):
        jl, jy = chunk_of(i)
        mb[jl, jy] = product(1 - c, jl * 4 + jy).astype(BF16)
        mate_sum(i).start()

    def mine(i):
        jl, jy = chunk_of(i)
        value = product(c, jl * 4 + jy)
        mate_sum(i).wait_recv()
        sb[jl, jy] = (value + mr[jl, jy].astype(F32)).astype(BF16)

    def leave(i):
        for s in (2, 1, 3):
            along_x(i, s).start()

    def ahead(i, carry):
        other(i)
        return carry

    def steady(i, carry):
        for u in range(2):
            other(2 * i + 2 + u)
            mine(2 * i + u)
        leave(i)

        @pl.when(i > 0)
        def _():
            along_y(i, 0).start()
            along_y(i, 1).start()

        return carry

    lax.fori_loop(0, 2, ahead, 0)
    lax.fori_loop(0, 3, steady, 0)
    mine(6)
    mine(7)
    leave(3)
    along_y(3, 0).start()
    along_y(3, 1).start()

    def last_y(i):
        return remote(t2a.at[i], fa.at[i - 1], r2_ss.at[0, i - 1], r2_rs.at[0, i - 1], at_y(i))

    def last_x(s):
        t = lax.rem(x + s, 4)
        return remote(
            t2b.at[lax.rem(t, 2), lax.div(t, 2)], fb.at[s - 1],
            r2_ss.at[1, s - 1], r2_rs.at[1, s - 1], at_x(s),
        )

    def add_x(i):
        for s in (1, 2, 3):
            along_x(i, s).wait_recv()
        total = sb[xl, lax.rem(y + i, 4), xh, 0].astype(F32)
        return total + ((ra[0, i].astype(F32) + ra[1, i].astype(F32)) + ra[2, i].astype(F32))

    ga[...] = add_x(0)

    def pass_y(i, carry):
        t2a[i] = add_x(i).astype(BF16)
        last_y(i).start()
        return carry

    lax.fori_loop(1, 4, pass_y, 0)
    for jl in range(2):
        for i in (1, 2, 3):
            along_y(i, jl).wait_recv()
        total = sb[jl, y, :, 1].astype(F32)
        total = total + (
            (rb[0, jl].astype(F32) + rb[1, jl].astype(F32)) + rb[2, jl].astype(F32)
        )
        gb[jl] = total
        t2b[jl] = total.astype(BF16)
    for s in (2, 1, 3):
        last_x(s).start()

    for i in (1, 2, 3):
        last_y(i).wait_recv()
    out_ref[0] = (ga[...] + fa[0].astype(F32)) + (fa[1].astype(F32) + fa[2].astype(F32))
    for s in (1, 2, 3):
        last_x(s).wait_recv()
    out_ref[1] = (gb[xl, xh] + fb[0].astype(F32)) + (fb[1].astype(F32) + fb[2].astype(F32))

    for group in (p1, lcp, icp, p2, pm, scp, qcp):
        for cp in group.values():
            cp.wait_send()

    def mate_done(i, carry):
        mate_sum(i).wait_send()
        return carry

    lax.fori_loop(0, 8, mate_done, 0)
    for i in range(4):
        for s in (1, 2, 3):
            along_x(i, s).wait_send()
    for i in (1, 2, 3):
        for jl in range(2):
            along_y(i, jl).wait_send()
        last_y(i).wait_send()
        last_x(i).wait_send()


def finish(sums_ref, evid_ref, out_ref, total_ref, out_evid_ref):
    for q in range(2):
        out_ref[q] = sums_ref[q, :, 0:CH]
        total_ref[q : q + 1, :] = sums_ref[q, :, 128:PAD].T[CH - 128 : CH - 127, :]
    out_evid_ref[...] = evid_ref[...]


def local(images, projections, noise_weights, class_prior, class_lists):
    dma = pltpu.SemaphoreType.DMA
    vmem = pl.BlockSpec(memory_space=pltpu.VMEM)
    sums, evidence = pl.pallas_call(
        kernel,
        name="estep",
        out_shape=(
            jax.ShapeDtypeStruct((2, R, PAD), F32),
            jax.ShapeDtypeStruct((1, ROWS), F32),
        ),
        in_specs=[
            pl.BlockSpec(memory_space=pl.ANY), vmem, vmem,
            pl.BlockSpec(memory_space=pltpu.SMEM), vmem,
        ],
        out_specs=(vmem, vmem),
        scratch_shapes=[
            pltpu.VMEM((4, ROWS, 2 * PIECE), BF16),
            pltpu.VMEM((4, 2, ROWS), jnp.int32),
            pltpu.VMEM((8, 4 * ROWS, PAD), BF16),
            pltpu.VMEM((8, 4 * ROWS, PAD), BF16),
            pltpu.VMEM((1, 8 * PAD), F32),
            pltpu.VMEM((2, 4, 2, 2, 2, R, PAD), BF16),
            pltpu.VMEM((8, R, ROWS), F32),
            pltpu.VMEM((8 * R, 4 * ROWS), F32),
            pltpu.VMEM((4, 2, R, ROWS), F32),
            pltpu.VMEM((3, 2, R, ROWS), F32),
            pltpu.VMEM((4, 2, R, ROWS), BF16),
            pltpu.VMEM((2, 2, 2, R, 4 * ROWS), BF16),
            pltpu.VMEM((2, 4, 2, 2, R, PAD), BF16),
            pltpu.VMEM((2, 4, 2, 2, R, PAD), BF16),
            pltpu.VMEM((2, 4, 2, 2, R, PAD), BF16),
            pltpu.VMEM((3, 4, R, PAD), BF16),
            pltpu.VMEM((3, 2, 2, R, PAD), BF16),
            pltpu.VMEM((4, R, PAD), BF16),
            pltpu.VMEM((2, 2, R, PAD), BF16),
            pltpu.VMEM((R, PAD), F32),
            pltpu.VMEM((2, 2, R, PAD), F32),
            pltpu.VMEM((3, R, PAD), BF16),
            pltpu.VMEM((3, R, PAD), BF16),
            dma((2,)),
            dma((3, 2)), dma((3, 2)),
            dma((3,)), dma((3,)),
            dma((2, 3)), dma((2, 3)),
            dma((2, 3)), dma((2, 3)),
            dma((2, 4)), dma((2, 4)),
            dma((3,)), dma((3,)),
            dma((3,)), dma((3,)),
            dma((8,)), dma((8,)),
            dma((3, 4)), dma((3, 4)),
            dma((3, 2)), dma((3, 2)),
            dma((2, 3)), dma((2, 3)),
        ],
        compiler_params=pltpu.CompilerParams(
            collective_id=0, has_side_effects=True, vmem_limit_bytes=56 * 2**20
        ),
    )(images, projections, noise_weights.reshape(56, 128), class_prior, class_lists.T)
    sums, totals, evidence = pl.pallas_call(
        finish,
        name="finish",
        out_shape=(
            jax.ShapeDtypeStruct((2, R, CH), F32),
            jax.ShapeDtypeStruct((2, R), F32),
            jax.ShapeDtypeStruct((1, ROWS), F32),
        ),
        in_specs=[vmem] * 2,
        out_specs=(vmem,) * 3,
    )(sums, evidence)
    return sums, totals, evidence.reshape(ROWS)


def solution(mesh):
    finer = Mesh(mesh.devices.reshape(2, 2, 2, 4, 4), AXES)
    rows, cls, prt = P(AXES, None), ("xh", "c"), ("xl", "z", "y")
    return jax.shard_map(
        local,
        mesh=finer,
        in_specs=(rows, P(cls, None, prt), P(), P(), rows),
        out_specs=(P(cls, None, prt), P(cls, None), P(AXES)),
        check_vma=False,
    )
```

```python
import jax
import jax.numpy as jnp
from jax import lax
from jax.experimental import pallas as pl
from jax.experimental.pallas import tpu as pltpu
from jax.sharding import Mesh
from jax.sharding import PartitionSpec as P

AXES = ("xh", "c", "xl", "z", "y")
MESH = pl.DeviceIdType.MESH
R = 144
ROWS = 128
CH = 224
PAD = 256
PIECE = 4 * CH
PLACE = {0: 0, 1: 1, 3: 2, 2: 3}
F32 = jnp.float32
BF16 = jnp.bfloat16


def kernel(
    img_ref, proj_ref, nw_ref, prior_ref, list_ref,
    out_ref, evid_ref,
    img, lists, xb, wb, nwp, pb, cross, sbuf, srecv, post, pt,
    mb, mr, sb, ra, rb, t2a, t2b, ga, gb, fa, fb,
    own_sem, img_ss, img_rs, list_ss, list_rs, p1_ss, p1_rs, p2_ss, p2_rs, pm_ss, pm_rs,
    s_ss, s_rs, q_ss, q_rs, m_ss, m_rs, xa_ss, xa_rs, yb_ss, yb_rs, r2_ss, r2_rs,
):
    xh, c, xl = lax.axis_index("xh"), lax.axis_index("c"), lax.axis_index("xl")
    z, y = lax.axis_index("z"), lax.axis_index("y")
    x = 2 * xh + xl
    mate = (xh, 1 - c, xl, z, y)

    def at_x(s):
        t = lax.rem(x + s, 4)
        return (lax.div(t, 2), c, lax.rem(t, 2), z, y)

    def at_y(s):
        return (xh, c, xl, z, lax.rem(y + s, 4))

    def at_z(s):
        return (xh, c, xl, lax.rem(z + s, 4), y)

    def remote(src, dst, ss, rs, dev):
        return pltpu.make_async_remote_copy(
            src_ref=src, dst_ref=dst, send_sem=ss, recv_sem=rs, device_id=dev, device_id_type=MESH
        )

    barrier = pltpu.get_barrier_semaphore()
    pl.semaphore_signal(barrier, inc=1, device_id=mate, device_id_type=MESH)
    for s in (1, 2, 3):
        for dev in (at_x(s), at_y(s), at_z(s)):
            pl.semaphore_signal(barrier, inc=1, device_id=dev, device_id_type=MESH)

    for p in range(2):
        row = (p * 4 + z) * 7
        flat = jnp.concatenate([nw_ref[pl.ds(row + t, 1), :] for t in range(7)], axis=1)
        for k in range(4):
            j = p * 4 + k
            nwp[:, j * PAD : (j + 1) * PAD] = jnp.full((1, PAD), -1.0, F32)
            nwp[:, j * PAD : j * PAD + CH] = flat[:, k * CH : (k + 1) * CH]

    lane = lax.broadcasted_iota(jnp.int32, (R, 128), 1) - (CH - 128)
    weights = nwp[:, pl.ds(pl.multiple_of((xl * 4 + y) * PAD, PAD), PAD)]
    for q in range(2):
        pb[xl, y, xh, c, q] = jnp.zeros((R, PAD), BF16)
        pb[xl, y, xh, c, q, :, 0:CH] = proj_ref[q]
        value = pb[xl, y, xh, c, q].astype(F32)
        left = 0.5 * jnp.sum(value * value * weights, axis=1, keepdims=True)
        tail = value[:, 128:PAD]
        for t in range(3):
            term = left.astype(BF16).astype(F32)
            left = left - term
            tail = jnp.where(lane == t, term, tail)
        pb[xl, y, xh, c, q, :, 128:PAD] = tail.astype(BF16)
    lists[0] = list_ref[...]

    own = []
    for p in range(2):
        own.append(
            pltpu.make_async_copy(
                img_ref.at[:, pl.ds(pl.multiple_of((p * 4 + z) * PIECE, 128), PIECE)],
                img.at[0, :, pl.ds(p * PIECE, PIECE)],
                own_sem.at[p],
            )
        )
        own[p].start()

    pl.semaphore_wait(barrier, 10)

    p1, p2, pm = {}, {}, {}

    def origin(half, s, t):
        u, v = (t, s) if half == 0 else (s, t)
        u = lax.rem(x + 4 - u, 4)
        return pb.at[lax.rem(u, 2), lax.rem(y + 4 - v, 4), lax.div(u, 2), c, half]

    def second(half, s):
        block = origin(half, s, 0)
        for t in (1, 3, 2):
            p2[half, s, t] = remote(
                block, block, p2_ss.at[half, s, t - 1], p2_rs.at[half, s, t - 1],
                at_x(t) if half == 0 else at_y(t),
            )
            p2[half, s, t].start()

    for half in range(2):
        for s in (1, 3, 2):
            block = origin(half, 0, 0)
            p1[half, s] = remote(
                block, block, p1_ss.at[half, s - 1], p1_rs.at[half, s - 1],
                at_y(s) if half == 0 else at_x(s),
            )
            p1[half, s].start()
    for half in range(2):
        second(half, 0)
    lcp, icp = {}, {}
    for s in (1, 3, 2):
        lcp[s] = remote(lists.at[0], lists.at[s], list_ss.at[s - 1], list_rs.at[s - 1], at_z(s))
        lcp[s].start()
        for p in range(2):
            to = lax.rem(z + s, 4)
            icp[s, p] = remote(
                img_ref.at[:, pl.ds(pl.multiple_of((p * 4 + to) * PIECE, 128), PIECE)],
                img.at[s, :, pl.ds(p * PIECE, PIECE)],
                img_ss.at[s - 1, p], img_rs.at[s - 1, p], at_z(s),
            )
            icp[s, p].start()

    def spread(s):
        past = lax.broadcasted_iota(jnp.int32, (ROWS, 128), 1) - (CH - 128)
        ones = jnp.where((past >= 0) & (past < 3), 1.0, 0.0)
        rows = slice(PLACE[s] * ROWS, (PLACE[s] + 1) * ROWS)
        for p in range(2):
            piece = img[s, :, p * PIECE : (p + 1) * PIECE].astype(F32)
            for k in range(4):
                j = p * 4 + k
                chunk = piece[:, k * CH : (k + 1) * CH]
                xb[j, rows, 128:PAD] = ones.astype(BF16)
                xb[j, rows, 0:CH] = chunk.astype(BF16)
                full = xb[j, rows, :].astype(F32)
                wb[j, rows, :] = (full * nwp[:, j * PAD : (j + 1) * PAD]).astype(BF16)

    own[0].wait()
    own[1].wait()
    spread(0)

    def mate_copy(half, t):
        u = lax.rem((x if half == 0 else y) + 4 - t, 4)
        if half == 0:
            block = pb.at[lax.rem(u, 2), :, lax.div(u, 2), c, 0]
        else:
            block = pb.at[:, u, :, c, 1]
        pm[half, t] = remote(block, block, pm_ss.at[half, t], pm_rs.at[half, t], mate)
        pm[half, t].start()

    for s in (1, 3, 2):
        for half in range(2):
            p1[half, s].wait_recv()
            second(half, s)
    for half in range(2):
        mate_copy(half, 0)

    for s in (1, 3):
        icp[s, 0].wait_recv()
        icp[s, 1].wait_recv()
        spread(s)
    for t in (1, 3, 2):
        for half in range(2):
            for s in range(4):
                p2[half, s, t].wait_recv()
            mate_copy(half, t)
    for s in (1, 2, 3):
        lcp[s].wait_recv()
    for t in range(4):
        for half in range(2):
            pm[half, t].wait_recv()

    def products(first, last):
        rows = slice(first * ROWS, last * ROWS)
        left = jnp.concatenate([pb[j // 4, j % 4].reshape(8 * R, PAD) for j in range(8)], axis=1)
        right = jnp.concatenate([wb[j, rows, :] for j in range(8)], axis=1)
        cross[:, rows] = lax.dot_general(
            left, right, (((1,), (1,)), ((), ())), preferred_element_type=F32
        )

    scp = {}

    def scores(s):
        lanes = slice(PLACE[s] * ROWS, (PLACE[s] + 1) * ROWS)

        def body(i, carry):
            start = pl.multiple_of(i * 16, 16)
            listed = [jnp.broadcast_to(lists[s, t : t + 1, :], (16, ROWS)) for t in range(2)]
            chosen = [jnp.zeros((16, ROWS), F32)] * 2
            for k in range(8):
                part = cross[pl.ds(k * R + start, 16), lanes]
                for t in range(2):
                    chosen[t] = jnp.where(listed[t] == k, part, chosen[t])
            for t in range(2):
                sbuf[s, t, pl.ds(start, 16), :] = chosen[t]
            return carry

        lax.fori_loop(0, R // 16, body, 0)
        if s:
            scp[s] = remote(
                sbuf.at[s], srecv.at[s - 1], s_ss.at[s - 1], s_rs.at[s - 1], at_z(4 - s)
            )
            scp[s].start()

    products(0, 3)
    for s in (1, 3, 0):
        scores(s)
    icp[2, 0].wait_recv()
    icp[2, 1].wait_recv()
    spread(2)
    products(3, 4)
    scores(2)

    for s in (1, 3, 2):
        scp[s].wait_recv()
    score = []
    for slot in range(2):
        prior = jnp.ones((1, ROWS), F32)
        for k in range(8):
            prior = jnp.where(lists[0, slot : slot + 1, :] == k, prior_ref[k], prior)
        total = (sbuf[0, slot] + srecv[0, slot]) + (srecv[1, slot] + srecv[2, slot])
        score.append(total + jnp.log(prior))
    top = jnp.maximum(
        jnp.max(score[0], axis=0, keepdims=True), jnp.max(score[1], axis=0, keepdims=True)
    )
    mass = jnp.sum(jnp.exp(score[0] - top), axis=0, keepdims=True) + jnp.sum(
        jnp.exp(score[1] - top), axis=0, keepdims=True
    )
    evid = top + jnp.log(mass)
    evid_ref[...] = evid
    for slot in range(2):
        post[0, slot] = jnp.exp(score[slot] - evid).astype(BF16)

    qcp = {}
    for s in (2, 1, 3):
        qcp[s] = remote(post.at[0], post.at[s], q_ss.at[s - 1], q_rs.at[s - 1], at_z(s))
        qcp[s].start()

    def expand(s):
        def body(k, carry):
            kh, kc, kq = lax.div(k, 4), lax.rem(lax.div(k, 2), 2), lax.rem(k, 2)
            value = jnp.zeros((R, ROWS), F32)
            for slot in range(2):
                hit = jnp.broadcast_to(lists[s, slot : slot + 1, :] == k, (R, ROWS))
                value = jnp.where(hit, post[s, slot].astype(F32), value)
            pt[kc, kh, kq, :, PLACE[s] * ROWS : (PLACE[s] + 1) * ROWS] = value.astype(BF16)
            return carry

        lax.fori_loop(0, 8, body, 0)

    expand(0)
    for s in (1, 3, 2):
        qcp[s].wait_recv()
        expand(s)

    def far(i):
        i = lax.div(i, 2)
        t = lax.rem(3 * i + 2, 4)
        return lax.select(i < 2, t, 3 - t)

    def chunk_of(i):
        return lax.rem(xl + 1 + lax.rem(i, 2), 2), lax.rem(y + far(i), 4)

    def mate_sum(i):
        jl, jy = chunk_of(i)
        return remote(mb.at[jl, jy], mr.at[jl, jy], m_ss.at[i], m_rs.at[i], mate)

    def product(which, j):
        left = pt[which].reshape(4 * R, 4 * ROWS)
        return jnp.dot(left, xb[j], preferred_element_type=F32).reshape(2, 2, R, PAD)

    def along_x(v, s):
        t = lax.rem(x + s, 4)
        return remote(
            sb.at[lax.rem(t, 2), lax.rem(y + v, 4), lax.div(t, 2), 0], ra.at[s - 1, v],
            xa_ss.at[s - 1, v], xa_rs.at[s - 1, v], at_x(s),
        )

    def along_y(v, jl):
        return remote(
            sb.at[jl, lax.rem(y + v, 4), :, 1], rb.at[v - 1, jl],
            yb_ss.at[v - 1, jl], yb_rs.at[v - 1, jl], at_y(v),
        )

    def other(i):
        jl, jy = chunk_of(i)
        mb[jl, jy] = product(1 - c, jl * 4 + jy).astype(BF16)
        mate_sum(i).start()

    def mine(i, shifts):
        jl, jy = chunk_of(i)
        value = product(c, jl * 4 + jy)
        mate_sum(i).wait_recv()
        sb[jl, jy] = (value + mr[jl, jy].astype(F32)).astype(BF16)
        for s in shifts:
            along_x(far(i), s).start()

    def ahead(i, carry):
        other(i)
        return carry

    def steady(i, carry):
        for u, shifts in enumerate(((1, 3), (2,))):
            other(2 * i + 2 + u)
            mine(2 * i + u, shifts)
            along_y(far(2 * i + u), chunk_of(2 * i + u)[0]).start()
        return carry

    lax.fori_loop(0, 2, ahead, 0)
    lax.fori_loop(0, 3, steady, 0)
    mine(6, (1, 3))
    mine(7, (2,))

    def last_y(v):
        return remote(t2a.at[v], fa.at[v - 1], r2_ss.at[0, v - 1], r2_rs.at[0, v - 1], at_y(v))

    def last_x(s):
        t = lax.rem(x + s, 4)
        return remote(
            t2b.at[lax.rem(t, 2), lax.div(t, 2)], fb.at[s - 1],
            r2_ss.at[1, s - 1], r2_rs.at[1, s - 1], at_x(s),
        )

    def add_x(v):
        for s in (1, 2, 3):
            along_x(v, s).wait_recv()
        total = sb[xl, lax.rem(y + v, 4), xh, 0].astype(F32)
        return total + ((ra[0, v].astype(F32) + ra[1, v].astype(F32)) + ra[2, v].astype(F32))

    def pass_y(i, carry):
        v = far(2 * i)
        t2a[v] = add_x(v).astype(BF16)
        last_y(v).start()
        return carry

    lax.fori_loop(0, 3, pass_y, 0)
    for u, shifts in enumerate(((1, 3), (2,))):
        jl = lax.rem(xl + 1 + u, 2)
        for v in (2, 1, 3):
            along_y(v, jl).wait_recv()
        total = sb[jl, y, :, 1].astype(F32)
        total = total + (
            (rb[0, jl].astype(F32) + rb[1, jl].astype(F32)) + rb[2, jl].astype(F32)
        )
        gb[jl] = total
        t2b[jl] = total.astype(BF16)
        for s in shifts:
            last_x(s).start()
    ga[...] = add_x(0)

    for v in (1, 2, 3):
        last_y(v).wait_recv()
    out_ref[0] = (ga[...] + fa[0].astype(F32)) + (fa[1].astype(F32) + fa[2].astype(F32))
    for s in (1, 2, 3):
        last_x(s).wait_recv()
    out_ref[1] = (gb[xl, xh] + fb[0].astype(F32)) + (fb[1].astype(F32) + fb[2].astype(F32))

    for group in (p1, lcp, icp, p2, pm, scp, qcp):
        for cp in group.values():
            cp.wait_send()

    def mate_done(i, carry):
        mate_sum(i).wait_send()
        return carry

    lax.fori_loop(0, 8, mate_done, 0)
    for i in range(4):
        for s in (1, 2, 3):
            along_x(i, s).wait_send()
    for i in (1, 2, 3):
        for jl in range(2):
            along_y(i, jl).wait_send()
        last_y(i).wait_send()
        last_x(i).wait_send()


def finish(sums_ref, evid_ref, out_ref, total_ref, out_evid_ref):
    for q in range(2):
        out_ref[q] = sums_ref[q, :, 0:CH]
        total_ref[q : q + 1, :] = sums_ref[q, :, 128:PAD].T[CH - 128 : CH - 127, :]
    out_evid_ref[...] = evid_ref[...]


def local(images, projections, noise_weights, class_prior, class_lists):
    dma = pltpu.SemaphoreType.DMA
    vmem = pl.BlockSpec(memory_space=pltpu.VMEM)
    sums, evidence = pl.pallas_call(
        kernel,
        name="estep",
        out_shape=(
            jax.ShapeDtypeStruct((2, R, PAD), F32),
            jax.ShapeDtypeStruct((1, ROWS), F32),
        ),
        in_specs=[
            pl.BlockSpec(memory_space=pl.ANY), vmem, vmem,
            pl.BlockSpec(memory_space=pltpu.SMEM), vmem,
        ],
        out_specs=(vmem, vmem),
        scratch_shapes=[
            pltpu.VMEM((4, ROWS, 2 * PIECE), BF16),
            pltpu.VMEM((4, 2, ROWS), jnp.int32),
            pltpu.VMEM((8, 4 * ROWS, PAD), BF16),
            pltpu.VMEM((8, 4 * ROWS, PAD), BF16),
            pltpu.VMEM((1, 8 * PAD), F32),
            pltpu.VMEM((2, 4, 2, 2, 2, R, PAD), BF16),
            pltpu.VMEM((8 * R, 4 * ROWS), F32),
            pltpu.VMEM((4, 2, R, ROWS), F32),
            pltpu.VMEM((3, 2, R, ROWS), F32),
            pltpu.VMEM((4, 2, R, ROWS), BF16),
            pltpu.VMEM((2, 2, 2, R, 4 * ROWS), BF16),
            pltpu.VMEM((2, 4, 2, 2, R, PAD), BF16),
            pltpu.VMEM((2, 4, 2, 2, R, PAD), BF16),
            pltpu.VMEM((2, 4, 2, 2, R, PAD), BF16),
            pltpu.VMEM((3, 4, R, PAD), BF16),
            pltpu.VMEM((3, 2, 2, R, PAD), BF16),
            pltpu.VMEM((4, R, PAD), BF16),
            pltpu.VMEM((2, 2, R, PAD), BF16),
            pltpu.VMEM((R, PAD), F32),
            pltpu.VMEM((2, 2, R, PAD), F32),
            pltpu.VMEM((3, R, PAD), BF16),
            pltpu.VMEM((3, R, PAD), BF16),
            dma((2,)),
            dma((3, 2)), dma((3, 2)),
            dma((3,)), dma((3,)),
            dma((2, 3)), dma((2, 3)),
            dma((2, 4, 3)), dma((2, 4, 3)),
            dma((2, 4)), dma((2, 4)),
            dma((3,)), dma((3,)),
            dma((3,)), dma((3,)),
            dma((8,)), dma((8,)),
            dma((3, 4)), dma((3, 4)),
            dma((3, 2)), dma((3, 2)),
            dma((2, 3)), dma((2, 3)),
        ],
        compiler_params=pltpu.CompilerParams(
            collective_id=0, has_side_effects=True, vmem_limit_bytes=56 * 2**20
        ),
    )(images, projections, noise_weights.reshape(56, 128), class_prior, class_lists.T)
    sums, totals, evidence = pl.pallas_call(
        finish,
        name="finish",
        out_shape=(
            jax.ShapeDtypeStruct((2, R, CH), F32),
            jax.ShapeDtypeStruct((2, R), F32),
            jax.ShapeDtypeStruct((1, ROWS), F32),
        ),
        in_specs=[vmem] * 2,
        out_specs=(vmem,) * 3,
    )(sums, evidence)
    return sums, totals, evidence.reshape(ROWS)


def solution(mesh):
    finer = Mesh(mesh.devices.reshape(2, 2, 2, 4, 4), AXES)
    rows, cls, prt = P(AXES, None), ("xh", "c"), ("xl", "z", "y")
    return jax.shard_map(
        local,
        mesh=finer,
        in_specs=(rows, P(cls, None, prt), P(), P(), rows),
        out_specs=(P(cls, None, prt), P(cls, None), P(AXES)),
        check_vma=False,
    )
```

```python
import jax
import jax.numpy as jnp
from jax import lax
from jax.experimental import pallas as pl
from jax.experimental.pallas import tpu as pltpu
from jax.sharding import Mesh
from jax.sharding import PartitionSpec as P

AXES = ("xh", "c", "xl", "z", "y")
MESH = pl.DeviceIdType.MESH
R = 144
ROWS = 128
CH = 224
PAD = 256
PIECE = 4 * CH
PLACE = {0: 0, 1: 1, 3: 2, 2: 3}
F32 = jnp.float32
BF16 = jnp.bfloat16


def kernel(
    img_ref, proj_ref, nw_ref, prior_ref, list_ref,
    out_ref, evid_ref,
    img, lists, xb, wb, nwp, pb, cross, sbuf, srecv, post, pt,
    mb, mr, sb, ra, rb, t2a, t2b, ga, gb, fa, fb,
    own_sem, img_ss, img_rs, list_ss, list_rs, p1_ss, p1_rs, p2_ss, p2_rs, pm_ss, pm_rs,
    s_ss, s_rs, q_ss, q_rs, m_ss, m_rs, xa_ss, xa_rs, yb_ss, yb_rs, r2_ss, r2_rs,
):
    xh, c, xl = lax.axis_index("xh"), lax.axis_index("c"), lax.axis_index("xl")
    z, y = lax.axis_index("z"), lax.axis_index("y")
    x = 2 * xh + xl
    mate = (xh, 1 - c, xl, z, y)

    def at_x(s):
        t = lax.rem(x + s, 4)
        return (lax.div(t, 2), c, lax.rem(t, 2), z, y)

    def at_y(s):
        return (xh, c, xl, z, lax.rem(y + s, 4))

    def at_z(s):
        return (xh, c, xl, lax.rem(z + s, 4), y)

    def remote(src, dst, ss, rs, dev):
        return pltpu.make_async_remote_copy(
            src_ref=src, dst_ref=dst, send_sem=ss, recv_sem=rs, device_id=dev, device_id_type=MESH
        )

    barrier = pltpu.get_barrier_semaphore()
    pl.semaphore_signal(barrier, inc=1, device_id=mate, device_id_type=MESH)
    for s in (1, 2, 3):
        for dev in (at_x(s), at_y(s), at_z(s)):
            pl.semaphore_signal(barrier, inc=1, device_id=dev, device_id_type=MESH)

    for p in range(2):
        row = (p * 4 + z) * 7
        flat = jnp.concatenate([nw_ref[pl.ds(row + t, 1), :] for t in range(7)], axis=1)
        for k in range(4):
            j = p * 4 + k
            nwp[:, j * PAD : (j + 1) * PAD] = jnp.full((1, PAD), -1.0, F32)
            nwp[:, j * PAD : j * PAD + CH] = flat[:, k * CH : (k + 1) * CH]

    lane = lax.broadcasted_iota(jnp.int32, (R, 128), 1) - (CH - 128)
    weights = nwp[:, pl.ds(pl.multiple_of((xl * 4 + y) * PAD, PAD), PAD)]
    for q in range(2):
        pb[xl, y, xh, c, q] = jnp.zeros((R, PAD), BF16)
        pb[xl, y, xh, c, q, :, 0:CH] = proj_ref[q]
        value = pb[xl, y, xh, c, q].astype(F32)
        left = 0.5 * jnp.sum(value * value * weights, axis=1, keepdims=True)
        tail = value[:, 128:PAD]
        for t in range(3):
            term = left.astype(BF16).astype(F32)
            left = left - term
            tail = jnp.where(lane == t, term, tail)
        pb[xl, y, xh, c, q, :, 128:PAD] = tail.astype(BF16)
    lists[0] = list_ref[...]

    own = []
    for p in range(2):
        own.append(
            pltpu.make_async_copy(
                img_ref.at[:, pl.ds(pl.multiple_of((p * 4 + z) * PIECE, 128), PIECE)],
                img.at[0, :, pl.ds(p * PIECE, PIECE)],
                own_sem.at[p],
            )
        )
        own[p].start()

    pl.semaphore_wait(barrier, 10)

    p1, p2, pm = {}, {}, {}

    def origin(half, s, t):
        u, v = (t, s) if half == 0 else (s, t)
        u = lax.rem(x + 4 - u, 4)
        return pb.at[lax.rem(u, 2), lax.rem(y + 4 - v, 4), lax.div(u, 2), c, half]

    def hop(half, s, t, to):
        block, k = origin(half, s, t), (t + to) % 4
        p2[half, s, k] = remote(
            block, block, p2_ss.at[half, s, k - 1], p2_rs.at[half, s, k - 1],
            at_x(to) if half == 0 else at_y(to),
        )
        p2[half, s, k].start()

    def second(half, s):
        for to in (1, 3):
            hop(half, s, 0, to)

    for half in range(2):
        for s in (1, 3, 2):
            block = origin(half, 0, 0)
            p1[half, s] = remote(
                block, block, p1_ss.at[half, s - 1], p1_rs.at[half, s - 1],
                at_y(s) if half == 0 else at_x(s),
            )
            p1[half, s].start()
    for half in range(2):
        second(half, 0)
    lcp, icp = {}, {}
    for s in (1, 3, 2):
        lcp[s] = remote(lists.at[0], lists.at[s], list_ss.at[s - 1], list_rs.at[s - 1], at_z(s))
        lcp[s].start()
        for p in range(2):
            to = lax.rem(z + s, 4)
            icp[s, p] = remote(
                img_ref.at[:, pl.ds(pl.multiple_of((p * 4 + to) * PIECE, 128), PIECE)],
                img.at[s, :, pl.ds(p * PIECE, PIECE)],
                img_ss.at[s - 1, p], img_rs.at[s - 1, p], at_z(s),
            )
            icp[s, p].start()

    def spread(s):
        past = lax.broadcasted_iota(jnp.int32, (ROWS, 128), 1) - (CH - 128)
        ones = jnp.where((past >= 0) & (past < 3), 1.0, 0.0)
        rows = slice(PLACE[s] * ROWS, (PLACE[s] + 1) * ROWS)
        for p in range(2):
            piece = img[s, :, p * PIECE : (p + 1) * PIECE].astype(F32)
            for k in range(4):
                j = p * 4 + k
                chunk = piece[:, k * CH : (k + 1) * CH]
                xb[j, rows, 128:PAD] = ones.astype(BF16)
                xb[j, rows, 0:CH] = chunk.astype(BF16)
                full = xb[j, rows, :].astype(F32)
                wb[j, rows, :] = (full * nwp[:, j * PAD : (j + 1) * PAD]).astype(BF16)

    own[0].wait()
    own[1].wait()
    spread(0)

    def mate_copy(half, t):
        u = lax.rem((x if half == 0 else y) + 4 - t, 4)
        if half == 0:
            block = pb.at[lax.rem(u, 2), :, lax.div(u, 2), c, 0]
        else:
            block = pb.at[:, u, :, c, 1]
        pm[half, t] = remote(block, block, pm_ss.at[half, t], pm_rs.at[half, t], mate)
        pm[half, t].start()

    for s in (1, 3, 2):
        for half in range(2):
            p1[half, s].wait_recv()
            second(half, s)
    for half in range(2):
        mate_copy(half, 0)
    for s in (0, 1, 3, 2):
        for half in range(2):
            way = 1 if s % 2 == 0 else 3
            p2[half, s, way].wait_recv()
            hop(half, s, way, way)

    for s in (1, 3):
        icp[s, 0].wait_recv()
        icp[s, 1].wait_recv()
        spread(s)
    for t in (1, 3, 2):
        for half in range(2):
            for s in range(4):
                if t == 2 or t != (1 if s % 2 == 0 else 3):
                    p2[half, s, t].wait_recv()
            mate_copy(half, t)
    for s in (1, 2, 3):
        lcp[s].wait_recv()
    for t in range(4):
        for half in range(2):
            pm[half, t].wait_recv()

    def products(first, last):
        rows = slice(first * ROWS, last * ROWS)
        left = jnp.concatenate([pb[j // 4, j % 4].reshape(8 * R, PAD) for j in range(8)], axis=1)
        right = jnp.concatenate([wb[j, rows, :] for j in range(8)], axis=1)
        cross[:, rows] = lax.dot_general(
            left, right, (((1,), (1,)), ((), ())), preferred_element_type=F32
        )

    scp = {}

    def scores(s):
        lanes = slice(PLACE[s] * ROWS, (PLACE[s] + 1) * ROWS)

        def body(i, carry):
            start = pl.multiple_of(i * 16, 16)
            listed = [jnp.broadcast_to(lists[s, t : t + 1, :], (16, ROWS)) for t in range(2)]
            chosen = [jnp.zeros((16, ROWS), F32)] * 2
            for k in range(8):
                part = cross[pl.ds(k * R + start, 16), lanes]
                for t in range(2):
                    chosen[t] = jnp.where(listed[t] == k, part, chosen[t])
            for t in range(2):
                sbuf[s, t, pl.ds(start, 16), :] = chosen[t]
            return carry

        lax.fori_loop(0, R // 16, body, 0)
        if s:
            scp[s] = remote(
                sbuf.at[s], srecv.at[s - 1], s_ss.at[s - 1], s_rs.at[s - 1], at_z(4 - s)
            )
            scp[s].start()

    products(0, 3)
    for s in (1, 3, 0):
        scores(s)
    icp[2, 0].wait_recv()
    icp[2, 1].wait_recv()
    spread(2)
    products(3, 4)
    scores(2)

    for s in (1, 3, 2):
        scp[s].wait_recv()
    score = []
    for slot in range(2):
        prior = jnp.ones((1, ROWS), F32)
        for k in range(8):
            prior = jnp.where(lists[0, slot : slot + 1, :] == k, prior_ref[k], prior)
        total = (sbuf[0, slot] + srecv[0, slot]) + (srecv[1, slot] + srecv[2, slot])
        score.append(total + jnp.log(prior))
    top = jnp.maximum(
        jnp.max(score[0], axis=0, keepdims=True), jnp.max(score[1], axis=0, keepdims=True)
    )
    mass = jnp.sum(jnp.exp(score[0] - top), axis=0, keepdims=True) + jnp.sum(
        jnp.exp(score[1] - top), axis=0, keepdims=True
    )
    evid = top + jnp.log(mass)
    evid_ref[...] = evid
    for slot in range(2):
        post[0, slot] = jnp.exp(score[slot] - evid).astype(BF16)

    qcp = {}
    for s in (2, 1, 3):
        qcp[s] = remote(post.at[0], post.at[s], q_ss.at[s - 1], q_rs.at[s - 1], at_z(s))
        qcp[s].start()

    def expand(s):
        def body(k, carry):
            kh, kc, kq = lax.div(k, 4), lax.rem(lax.div(k, 2), 2), lax.rem(k, 2)
            value = jnp.zeros((R, ROWS), F32)
            for slot in range(2):
                hit = jnp.broadcast_to(lists[s, slot : slot + 1, :] == k, (R, ROWS))
                value = jnp.where(hit, post[s, slot].astype(F32), value)
            pt[lax.rem(kc + c, 2), kh, kq, :, PLACE[s] * ROWS : (PLACE[s] + 1) * ROWS] = value.astype(BF16)
            return carry

        lax.fori_loop(0, 8, body, 0)

    expand(0)
    for s in (1, 3, 2):
        qcp[s].wait_recv()
        expand(s)

    def far(i):
        i = lax.div(i, 2)
        t = lax.rem(3 * i + 2, 4)
        return lax.select(i < 2, t, 3 - t)

    def chunk_of(i):
        return lax.rem(xl + lax.rem(i, 2), 2), lax.rem(y + far(i), 4)

    def mate_sum(i):
        jl, jy = chunk_of(i)
        return remote(mb.at[jl, jy], mr.at[jl, jy], m_ss.at[i], m_rs.at[i], mate)

    def block_x(v, s):
        t = lax.rem(x + s, 4)
        return sb.at[lax.rem(t, 2), lax.rem(y + v, 4), lax.div(t, 2), 0]

    def block_y(v, u):
        return sb.at[lax.rem(xl + u, 2), lax.rem(y + v, 4), :, 1]

    def along_x(i, part):
        way = 1 + 2 * lax.rem(i, 2)
        v = far(2 * i)
        shift = (way, 4 - way, 2)[part]
        return remote(
            block_x(v, shift), ra.at[part, i], xa_ss.at[part, i], xa_rs.at[part, i],
            at_x((way, 4 - way, way)[part]),
        )

    def along_y(u, part):
        way = 1 + 2 * u
        shift = (way, 4 - way, 2)[part]
        return remote(
            block_y(shift, u), rb.at[part, u], yb_ss.at[part, u], yb_rs.at[part, u],
            at_y((way, 4 - way, way)[part]),
        )

    def pass_x(i):
        along_x(i, 2).wait_recv()
        block = block_x(far(2 * i), 1 + 2 * lax.rem(i, 2))
        block[...] = (block[...].astype(F32) + ra[2, i].astype(F32)).astype(BF16)
        along_x(i, 0).start()

    def pass_y(u):
        along_y(u, 2).wait_recv()
        block = block_y(1 + 2 * u, u)
        block[...] = (block[...].astype(F32) + rb[2, u].astype(F32)).astype(BF16)
        along_y(u, 0).start()

    def product(i):
        jl, jy = chunk_of(i)
        left = pt[...].reshape(8 * R, 4 * ROWS)
        both = jnp.dot(left, xb[jl * 4 + jy], preferred_element_type=F32)
        both = both.reshape(2, 2, 2, R, PAD).astype(BF16)
        mb[jl, jy] = both[1]
        sb[jl, jy] = both[0]
        mate_sum(i).start()

    def join(i):
        jl, jy = chunk_of(i)
        mate_sum(i).wait_recv()
        sb[jl, jy] = (sb[jl, jy].astype(F32) + mr[jl, jy].astype(F32)).astype(BF16)

    def ahead(i, carry):
        product(i)
        return carry

    def steady(i, carry):
        @pl.when(i < 3)
        def _():
            product(2 * i + 2)

        join(2 * i)
        along_x(i, 2).start()

        @pl.when(i == 0)
        def _():
            along_y(0, 2).start()

        @pl.when(i == 1)
        def _():
            pass_y(0)

        @pl.when(i == 2)
        def _():
            along_y(0, 1).start()

        @pl.when(i < 3)
        def _():
            product(2 * i + 3)

        join(2 * i + 1)
        along_x(i, 1).start()

        @pl.when(i == 0)
        def _():
            along_y(1, 2).start()

        @pl.when(i == 1)
        def _():
            along_y(1, 1).start()

        @pl.when(i == 2)
        def _():
            pass_y(1)

        @pl.when(i > 0)
        def _():
            pass_x(i - 1)

        return carry

    lax.fori_loop(0, 2, ahead, 0)
    lax.fori_loop(0, 4, steady, 0)
    pass_x(3)

    def last_y(v):
        return remote(t2a.at[v], fa.at[v - 1], r2_ss.at[0, v - 1], r2_rs.at[0, v - 1], at_y(v))

    def last_x(s):
        t = lax.rem(x + s, 4)
        return remote(
            t2b.at[lax.rem(t, 2), lax.div(t, 2)], fb.at[s - 1],
            r2_ss.at[1, s - 1], r2_rs.at[1, s - 1], at_x(s),
        )

    def add_x(i):
        along_x(i, 1).wait_recv()
        along_x(i, 0).wait_recv()
        total = block_x(far(2 * i), 0)[...].astype(F32)
        return total + (ra[0, i].astype(F32) + ra[1, i].astype(F32))

    def leave_y(i, carry):
        v = far(2 * i)
        t2a[v] = add_x(i).astype(BF16)
        last_y(v).start()
        return carry

    lax.fori_loop(0, 3, leave_y, 0)
    for u, shifts in enumerate(((2,), (1, 3))):
        jl = lax.rem(xl + u, 2)
        along_y(u, 1).wait_recv()
        along_y(u, 0).wait_recv()
        total = block_y(0, u)[...].astype(F32) + (rb[0, u].astype(F32) + rb[1, u].astype(F32))
        gb[jl] = total
        t2b[jl] = total.astype(BF16)
        for s in shifts:
            last_x(s).start()
    ga[...] = add_x(3)

    for v in (1, 2, 3):
        last_y(v).wait_recv()
    out_ref[0] = (ga[...] + fa[0].astype(F32)) + (fa[1].astype(F32) + fa[2].astype(F32))
    for s in (1, 2, 3):
        last_x(s).wait_recv()
    out_ref[1] = (gb[xl, xh] + fb[0].astype(F32)) + (fb[1].astype(F32) + fb[2].astype(F32))

    for group in (p1, lcp, icp, p2, pm, scp, qcp):
        for cp in group.values():
            cp.wait_send()

    def mate_done(i, carry):
        mate_sum(i).wait_send()
        return carry

    lax.fori_loop(0, 8, mate_done, 0)
    for part in range(3):
        for i in range(4):
            along_x(i, part).wait_send()
        for u in range(2):
            along_y(u, part).wait_send()
    for s in (1, 2, 3):
        last_y(s).wait_send()
        last_x(s).wait_send()


def finish(sums_ref, evid_ref, out_ref, total_ref, out_evid_ref):
    for q in range(2):
        out_ref[q] = sums_ref[q, :, 0:CH]
        total_ref[q : q + 1, :] = sums_ref[q, :, 128:PAD].T[CH - 128 : CH - 127, :]
    out_evid_ref[...] = evid_ref[...]


def local(images, projections, noise_weights, class_prior, class_lists):
    dma = pltpu.SemaphoreType.DMA
    vmem = pl.BlockSpec(memory_space=pltpu.VMEM)
    sums, evidence = pl.pallas_call(
        kernel,
        name="estep",
        out_shape=(
            jax.ShapeDtypeStruct((2, R, PAD), F32),
            jax.ShapeDtypeStruct((1, ROWS), F32),
        ),
        in_specs=[
            pl.BlockSpec(memory_space=pl.ANY), vmem, vmem,
            pl.BlockSpec(memory_space=pltpu.SMEM), vmem,
        ],
        out_specs=(vmem, vmem),
        scratch_shapes=[
            pltpu.VMEM((4, ROWS, 2 * PIECE), BF16),
            pltpu.VMEM((4, 2, ROWS), jnp.int32),
            pltpu.VMEM((8, 4 * ROWS, PAD), BF16),
            pltpu.VMEM((8, 4 * ROWS, PAD), BF16),
            pltpu.VMEM((1, 8 * PAD), F32),
            pltpu.VMEM((2, 4, 2, 2, 2, R, PAD), BF16),
            pltpu.VMEM((8 * R, 4 * ROWS), F32),
            pltpu.VMEM((4, 2, R, ROWS), F32),
            pltpu.VMEM((3, 2, R, ROWS), F32),
            pltpu.VMEM((4, 2, R, ROWS), BF16),
            pltpu.VMEM((2, 2, 2, R, 4 * ROWS), BF16),
            pltpu.VMEM((2, 4, 2, 2, R, PAD), BF16),
            pltpu.VMEM((2, 4, 2, 2, R, PAD), BF16),
            pltpu.VMEM((2, 4, 2, 2, R, PAD), BF16),
            pltpu.VMEM((3, 4, R, PAD), BF16),
            pltpu.VMEM((3, 2, 2, R, PAD), BF16),
            pltpu.VMEM((4, R, PAD), BF16),
            pltpu.VMEM((2, 2, R, PAD), BF16),
            pltpu.VMEM((R, PAD), F32),
            pltpu.VMEM((2, 2, R, PAD), F32),
            pltpu.VMEM((3, R, PAD), BF16),
            pltpu.VMEM((3, R, PAD), BF16),
            dma((2,)),
            dma((3, 2)), dma((3, 2)),
            dma((3,)), dma((3,)),
            dma((2, 3)), dma((2, 3)),
            dma((2, 4, 3)), dma((2, 4, 3)),
            dma((2, 4)), dma((2, 4)),
            dma((3,)), dma((3,)),
            dma((3,)), dma((3,)),
            dma((8,)), dma((8,)),
            dma((3, 4)), dma((3, 4)),
            dma((3, 2)), dma((3, 2)),
            dma((2, 3)), dma((2, 3)),
        ],
        compiler_params=pltpu.CompilerParams(
            collective_id=0, has_side_effects=True, vmem_limit_bytes=56 * 2**20
        ),
    )(images, projections, noise_weights.reshape(56, 128), class_prior, class_lists.T)
    sums, totals, evidence = pl.pallas_call(
        finish,
        name="finish",
        out_shape=(
            jax.ShapeDtypeStruct((2, R, CH), F32),
            jax.ShapeDtypeStruct((2, R), F32),
            jax.ShapeDtypeStruct((1, ROWS), F32),
        ),
        in_specs=[vmem] * 2,
        out_specs=(vmem,) * 3,
    )(sums, evidence)
    return sums, totals, evidence.reshape(ROWS)


def solution(mesh):
    finer = Mesh(mesh.devices.reshape(2, 2, 2, 4, 4), AXES)
    rows, cls, prt = P(AXES, None), ("xh", "c"), ("xl", "z", "y")
    return jax.shard_map(
        local,
        mesh=finer,
        in_specs=(rows, P(cls, None, prt), P(), P(), rows),
        out_specs=(P(cls, None, prt), P(cls, None), P(AXES)),
        check_vma=False,
    )
```

```python
import jax
import jax.numpy as jnp
from jax import lax
from jax.experimental import pallas as pl
from jax.experimental.pallas import tpu as pltpu
from jax.sharding import Mesh
from jax.sharding import PartitionSpec as P

AXES = ("xh", "c", "xl", "z", "y")
MESH = pl.DeviceIdType.MESH
R = 144
ROWS = 128
CH = 224
PAD = 256
PIECE = 4 * CH
F32 = jnp.float32
BF16 = jnp.bfloat16


def kernel(
    img_ref, proj_ref, nw_ref, prior_ref, list_ref,
    out_ref, evid_ref,
    img, lists, xb, wb, nwp, pb, cross, sbuf, srecv, post, pt,
    mb, mr, sb, ra, rb, t2a, t2b, ga, gb, fa, fb,
    own_sem, img_ss, img_rs, list_ss, list_rs, p1_ss, p1_rs, p2_ss, p2_rs, pm_ss, pm_rs,
    s_ss, s_rs, q_ss, q_rs, m_ss, m_rs, xa_ss, xa_rs, yb_ss, yb_rs, r2_ss, r2_rs,
):
    xh, c, xl = lax.axis_index("xh"), lax.axis_index("c"), lax.axis_index("xl")
    z, y = lax.axis_index("z"), lax.axis_index("y")
    x = 2 * xh + xl
    mate = (xh, 1 - c, xl, z, y)

    def at_x(s):
        t = lax.rem(x + s, 4)
        return (lax.div(t, 2), c, lax.rem(t, 2), z, y)

    def at_y(s):
        return (xh, c, xl, z, lax.rem(y + s, 4))

    def at_z(s):
        return (xh, c, xl, lax.rem(z + s, 4), y)

    def remote(src, dst, ss, rs, dev):
        return pltpu.make_async_remote_copy(
            src_ref=src, dst_ref=dst, send_sem=ss, recv_sem=rs, device_id=dev, device_id_type=MESH
        )

    barrier = pltpu.get_barrier_semaphore()
    pl.semaphore_signal(barrier, inc=1, device_id=mate, device_id_type=MESH)
    for s in (1, 2, 3):
        for dev in (at_x(s), at_y(s), at_z(s)):
            pl.semaphore_signal(barrier, inc=1, device_id=dev, device_id_type=MESH)

    for p in range(2):
        row = (p * 4 + z) * 7
        flat = jnp.concatenate([nw_ref[pl.ds(row + t, 1), :] for t in range(7)], axis=1)
        for k in range(4):
            j = p * 4 + k
            nwp[:, j * PAD : (j + 1) * PAD] = jnp.full((1, PAD), -1.0, F32)
            nwp[:, j * PAD : j * PAD + CH] = flat[:, k * CH : (k + 1) * CH]

    lane = lax.broadcasted_iota(jnp.int32, (R, 128), 1) - (CH - 128)
    weights = nwp[:, pl.ds(pl.multiple_of((xl * 4 + y) * PAD, PAD), PAD)]
    for q in range(2):
        pb[xl, y, xh, c, q] = jnp.zeros((R, PAD), BF16)
        pb[xl, y, xh, c, q, :, 0:CH] = proj_ref[q]
        value = pb[xl, y, xh, c, q].astype(F32)
        left = 0.5 * jnp.sum(value * value * weights, axis=1, keepdims=True)
        tail = value[:, 128:PAD]
        for t in range(3):
            term = left.astype(BF16).astype(F32)
            left = left - term
            tail = jnp.where(lane == t, term, tail)
        pb[xl, y, xh, c, q, :, 128:PAD] = tail.astype(BF16)
    lists[0] = list_ref[...]

    own = []
    for p in range(2):
        own.append(
            pltpu.make_async_copy(
                img_ref.at[:, pl.ds(pl.multiple_of((p * 4 + z) * PIECE, 128), PIECE)],
                img.at[0, :, pl.ds(p * PIECE, PIECE)],
                own_sem.at[p],
            )
        )
        own[p].start()

    pl.semaphore_wait(barrier, 10)

    p1, p2, pm = {}, {}, {}

    def origin(half, s, t):
        u, v = (t, s) if half == 0 else (s, t)
        u = lax.rem(x + 4 - u, 4)
        return pb.at[lax.rem(u, 2), lax.rem(y + 4 - v, 4), lax.div(u, 2), c, half]

    def hop(half, s, t, to):
        block, k = origin(half, s, t), (t + to) % 4
        p2[half, s, k] = remote(
            block, block, p2_ss.at[half, s, k - 1], p2_rs.at[half, s, k - 1],
            at_x(to) if half == 0 else at_y(to),
        )
        p2[half, s, k].start()

    def second(half, s):
        for to in (1, 3):
            hop(half, s, 0, to)

    for half in range(2):
        for s in (1, 3, 2):
            block = origin(half, 0, 0)
            p1[half, s] = remote(
                block, block, p1_ss.at[half, s - 1], p1_rs.at[half, s - 1],
                at_y(s) if half == 0 else at_x(s),
            )
            p1[half, s].start()
    for half in range(2):
        second(half, 0)
    lcp = {}

    def image(s, p):
        to = lax.rem(z + s, 4)
        return remote(
            img_ref.at[:, pl.ds(pl.multiple_of((p * 4 + to) * PIECE, 128), PIECE)],
            img.at[s, :, pl.ds(p * PIECE, PIECE)],
            img_ss.at[s - 1, p], img_rs.at[s - 1, p], at_z(s),
        )

    for s in (1, 3, 2):
        lcp[s] = remote(lists.at[0], lists.at[s], list_ss.at[s - 1], list_rs.at[s - 1], at_z(s))
        lcp[s].start()
        for p in range(2):
            image(s, p).start()

    order = (1, 3, 2, 0)

    def spread(place, s):
        past = lax.broadcasted_iota(jnp.int32, (ROWS, 128), 1) - (CH - 128)
        ones = jnp.where((past >= 0) & (past < 3), 1.0, 0.0)
        rows = pl.ds(pl.multiple_of(place * ROWS, ROWS), ROWS)
        for p in range(2):
            piece = img[s, :, p * PIECE : (p + 1) * PIECE].astype(F32)
            for k in range(4):
                j = p * 4 + k
                chunk = piece[:, k * CH : (k + 1) * CH]
                xb[j, rows, 128:PAD] = ones.astype(BF16)
                xb[j, rows, 0:CH] = chunk.astype(BF16)
                full = xb[j, rows, :].astype(F32)
                wb[j, rows, :] = (full * nwp[:, j * PAD : (j + 1) * PAD]).astype(BF16)

    own[0].wait()
    own[1].wait()
    spread(3, 0)

    def mate_copy(half, t):
        u = lax.rem((x if half == 0 else y) + 4 - t, 4)
        if half == 0:
            block = pb.at[lax.rem(u, 2), :, lax.div(u, 2), c, 0]
        else:
            block = pb.at[:, u, :, c, 1]
        pm[half, t] = remote(block, block, pm_ss.at[half, t], pm_rs.at[half, t], mate)
        pm[half, t].start()

    for s in (1, 3, 2):
        for half in range(2):
            p1[half, s].wait_recv()
            second(half, s)
    for half in range(2):
        mate_copy(half, 0)
    for s in (0, 1, 3, 2):
        for half in range(2):
            way = 1 if s % 2 == 0 else 3
            p2[half, s, way].wait_recv()
            hop(half, s, way, way)

    for t in (1, 3, 2):
        for half in range(2):
            for s in range(4):
                if t == 2 or t != (1 if s % 2 == 0 else 3):
                    p2[half, s, t].wait_recv()
            mate_copy(half, t)
    for s in (1, 2, 3):
        lcp[s].wait_recv()
    for t in range(4):
        for half in range(2):
            pm[half, t].wait_recv()

    def score_copy(s):
        return remote(sbuf.at[s], srecv.at[s - 1], s_ss.at[s - 1], s_rs.at[s - 1], at_z(4 - s))

    def scores(s, lanes):
        def body(i, carry):
            start = pl.multiple_of(i * 16, 16)
            listed = [jnp.broadcast_to(lists[s, t : t + 1, :], (16, ROWS)) for t in range(2)]
            chosen = [jnp.zeros((16, ROWS), F32)] * 2
            for k in range(8):
                part = cross[pl.ds(k * R + start, 16), lanes]
                for t in range(2):
                    chosen[t] = jnp.where(listed[t] == k, part, chosen[t])
            for t in range(2):
                sbuf[s, t, pl.ds(start, 16), :] = chosen[t]
            return carry

        lax.fori_loop(0, R // 16, body, 0)

    def pair(i, carry):
        first = lax.select(i == 0, order[0], order[2])
        second = lax.select(i == 0, order[1], order[3])
        for p in range(2):
            image(first, p).wait_recv()
        spread(2 * i, first)

        @pl.when(i == 0)
        def _():
            for p in range(2):
                image(second, p).wait_recv()
            spread(1, second)

        left = jnp.concatenate([pb[j // 4, j % 4].reshape(8 * R, PAD) for j in range(8)], axis=1)
        rows = pl.ds(pl.multiple_of(2 * i * ROWS, ROWS), 2 * ROWS)
        right = jnp.concatenate([wb[j, rows, :] for j in range(8)], axis=1)
        cross[...] = lax.dot_general(
            left, right, (((1,), (1,)), ((), ())), preferred_element_type=F32
        )
        scores(first, slice(0, ROWS))
        score_copy(first).start()
        scores(second, slice(ROWS, 2 * ROWS))

        @pl.when(i == 0)
        def _():
            score_copy(second).start()

        return carry

    lax.fori_loop(0, 2, pair, 0)

    for s in (1, 3, 2):
        score_copy(s).wait_recv()
    score = []
    for slot in range(2):
        prior = jnp.ones((1, ROWS), F32)
        for k in range(8):
            prior = jnp.where(lists[0, slot : slot + 1, :] == k, prior_ref[k], prior)
        total = (sbuf[0, slot] + srecv[0, slot]) + (srecv[1, slot] + srecv[2, slot])
        score.append(total + jnp.log(prior))
    top = jnp.maximum(
        jnp.max(score[0], axis=0, keepdims=True), jnp.max(score[1], axis=0, keepdims=True)
    )
    mass = jnp.sum(jnp.exp(score[0] - top), axis=0, keepdims=True) + jnp.sum(
        jnp.exp(score[1] - top), axis=0, keepdims=True
    )
    evid = top + jnp.log(mass)
    evid_ref[...] = evid
    for slot in range(2):
        post[0, slot] = jnp.exp(score[slot] - evid).astype(BF16)

    qcp = {}
    for s in (2, 1, 3):
        qcp[s] = remote(post.at[0], post.at[s], q_ss.at[s - 1], q_rs.at[s - 1], at_z(s))
        qcp[s].start()

    def expand(place, s):
        lanes = pl.ds(pl.multiple_of(place * ROWS, ROWS), ROWS)

        def body(k, carry):
            kh, kc, kq = lax.div(k, 4), lax.rem(lax.div(k, 2), 2), lax.rem(k, 2)
            value = jnp.zeros((R, ROWS), F32)
            for slot in range(2):
                hit = jnp.broadcast_to(lists[s, slot : slot + 1, :] == k, (R, ROWS))
                value = jnp.where(hit, post[s, slot].astype(F32), value)
            pt[lax.rem(kc + c, 2), kh, kq, :, lanes] = value.astype(BF16)
            return carry

        lax.fori_loop(0, 8, body, 0)

    expand(3, 0)
    for place in range(3):
        qcp[order[place]].wait_recv()
        expand(place, order[place])

    def far(i):
        i = lax.div(i, 2)
        t = lax.rem(3 * i + 2, 4)
        return lax.select(i < 2, t, 3 - t)

    def chunk_of(i):
        return lax.rem(xl + lax.rem(i, 2), 2), lax.rem(y + far(i), 4)

    def mate_sum(i):
        jl, jy = chunk_of(i)
        return remote(mb.at[jl, jy], mr.at[jl, jy], m_ss.at[i], m_rs.at[i], mate)

    def block_x(v, s):
        t = lax.rem(x + s, 4)
        return sb.at[lax.rem(t, 2), lax.rem(y + v, 4), lax.div(t, 2), 0]

    def block_y(v, u):
        return sb.at[lax.rem(xl + u, 2), lax.rem(y + v, 4), :, 1]

    def along_x(i, part):
        way = 1 + 2 * lax.rem(i, 2)
        v = far(2 * i)
        shift = (way, 4 - way, 2)[part]
        return remote(
            block_x(v, shift), ra.at[part, i], xa_ss.at[part, i], xa_rs.at[part, i],
            at_x((way, 4 - way, way)[part]),
        )

    def along_y(u, part):
        way = 1 + 2 * u
        shift = (way, 4 - way, 2)[part]
        return remote(
            block_y(shift, u), rb.at[part, u], yb_ss.at[part, u], yb_rs.at[part, u],
            at_y((way, 4 - way, way)[part]),
        )

    def pass_x(i):
        along_x(i, 2).wait_recv()
        block = block_x(far(2 * i), 1 + 2 * lax.rem(i, 2))
        block[...] = (block[...].astype(F32) + ra[2, i].astype(F32)).astype(BF16)
        along_x(i, 0).start()

    def pass_y(u):
        along_y(u, 2).wait_recv()
        block = block_y(1 + 2 * u, u)
        block[...] = (block[...].astype(F32) + rb[2, u].astype(F32)).astype(BF16)
        along_y(u, 0).start()

    def product(i):
        jl, jy = chunk_of(i)
        left = pt[...].reshape(8 * R, 4 * ROWS)
        both = jnp.dot(left, xb[jl * 4 + jy], preferred_element_type=F32)
        both = both.reshape(2, 2, 2, R, PAD).astype(BF16)
        mb[jl, jy] = both[1]
        sb[jl, jy] = both[0]
        mate_sum(i).start()

    def join(i):
        jl, jy = chunk_of(i)
        mate_sum(i).wait_recv()
        sb[jl, jy] = (sb[jl, jy].astype(F32) + mr[jl, jy].astype(F32)).astype(BF16)

    def ahead(i, carry):
        product(i)
        return carry

    def steady(i, carry):
        @pl.when(i < 3)
        def _():
            product(2 * i + 2)

        join(2 * i)
        along_x(i, 2).start()

        @pl.when(i == 0)
        def _():
            along_y(0, 2).start()

        @pl.when(i == 2)
        def _():
            along_y(0, 1).start()

        @pl.when(i < 3)
        def _():
            product(2 * i + 3)

        join(2 * i + 1)

        @pl.when(i == 0)
        def _():
            along_y(1, 2).start()

        @pl.when(i == 1)
        def _():
            along_y(1, 1).start()

        along_x(i, 1).start()
        return carry

    lax.fori_loop(0, 2, ahead, 0)
    lax.fori_loop(0, 4, steady, 0)
    pass_x(0)
    for u in range(2):
        pass_y(u)
        pass_x(u + 1)
    pass_x(3)

    def last_y(v):
        return remote(t2a.at[v], fa.at[v - 1], r2_ss.at[0, v - 1], r2_rs.at[0, v - 1], at_y(v))

    def last_x(s):
        t = lax.rem(x + s, 4)
        return remote(
            t2b.at[lax.rem(t, 2), lax.div(t, 2)], fb.at[s - 1],
            r2_ss.at[1, s - 1], r2_rs.at[1, s - 1], at_x(s),
        )

    def add_x(i):
        along_x(i, 1).wait_recv()
        along_x(i, 0).wait_recv()
        total = block_x(far(2 * i), 0)[...].astype(F32)
        return total + (ra[0, i].astype(F32) + ra[1, i].astype(F32))

    def leave_y(i, carry):
        v = far(2 * i)
        t2a[v] = add_x(i).astype(BF16)
        last_y(v).start()
        return carry

    lax.fori_loop(0, 3, leave_y, 0)
    for u, shifts in enumerate(((2,), (1, 3))):
        jl = lax.rem(xl + u, 2)
        along_y(u, 1).wait_recv()
        along_y(u, 0).wait_recv()
        total = block_y(0, u)[...].astype(F32) + (rb[0, u].astype(F32) + rb[1, u].astype(F32))
        gb[jl] = total
        t2b[jl] = total.astype(BF16)
        for s in shifts:
            last_x(s).start()
    ga[...] = add_x(3)

    for v in (1, 2, 3):
        last_y(v).wait_recv()
    out_ref[0] = (ga[...] + fa[0].astype(F32)) + (fa[1].astype(F32) + fa[2].astype(F32))
    for s in (1, 2, 3):
        last_x(s).wait_recv()
    out_ref[1] = (gb[xl, xh] + fb[0].astype(F32)) + (fb[1].astype(F32) + fb[2].astype(F32))

    for group in (p1, lcp, p2, pm, qcp):
        for cp in group.values():
            cp.wait_send()
    for s in (1, 2, 3):
        score_copy(s).wait_send()
        for p in range(2):
            image(s, p).wait_send()

    def mate_done(i, carry):
        mate_sum(i).wait_send()
        return carry

    lax.fori_loop(0, 8, mate_done, 0)
    for part in range(3):
        for i in range(4):
            along_x(i, part).wait_send()
        for u in range(2):
            along_y(u, part).wait_send()
    for s in (1, 2, 3):
        last_y(s).wait_send()
        last_x(s).wait_send()


def finish(sums_ref, evid_ref, out_ref, total_ref, out_evid_ref):
    for q in range(2):
        out_ref[q] = sums_ref[q, :, 0:CH]
        total_ref[q : q + 1, :] = sums_ref[q, :, 128:PAD].T[CH - 128 : CH - 127, :]
    out_evid_ref[...] = evid_ref[...]


def local(images, projections, noise_weights, class_prior, class_lists):
    dma = pltpu.SemaphoreType.DMA
    vmem = pl.BlockSpec(memory_space=pltpu.VMEM)
    sums, evidence = pl.pallas_call(
        kernel,
        name="estep",
        out_shape=(
            jax.ShapeDtypeStruct((2, R, PAD), F32),
            jax.ShapeDtypeStruct((1, ROWS), F32),
        ),
        in_specs=[
            pl.BlockSpec(memory_space=pl.ANY), vmem, vmem,
            pl.BlockSpec(memory_space=pltpu.SMEM), vmem,
        ],
        out_specs=(vmem, vmem),
        scratch_shapes=[
            pltpu.VMEM((4, ROWS, 2 * PIECE), BF16),
            pltpu.VMEM((4, 2, ROWS), jnp.int32),
            pltpu.VMEM((8, 4 * ROWS, PAD), BF16),
            pltpu.VMEM((8, 4 * ROWS, PAD), BF16),
            pltpu.VMEM((1, 8 * PAD), F32),
            pltpu.VMEM((2, 4, 2, 2, 2, R, PAD), BF16),
            pltpu.VMEM((8 * R, 2 * ROWS), F32),
            pltpu.VMEM((4, 2, R, ROWS), F32),
            pltpu.VMEM((3, 2, R, ROWS), F32),
            pltpu.VMEM((4, 2, R, ROWS), BF16),
            pltpu.VMEM((2, 2, 2, R, 4 * ROWS), BF16),
            pltpu.VMEM((2, 4, 2, 2, R, PAD), BF16),
            pltpu.VMEM((2, 4, 2, 2, R, PAD), BF16),
            pltpu.VMEM((2, 4, 2, 2, R, PAD), BF16),
            pltpu.VMEM((3, 4, R, PAD), BF16),
            pltpu.VMEM((3, 2, 2, R, PAD), BF16),
            pltpu.VMEM((4, R, PAD), BF16),
            pltpu.VMEM((2, 2, R, PAD), BF16),
            pltpu.VMEM((R, PAD), F32),
            pltpu.VMEM((2, 2, R, PAD), F32),
            pltpu.VMEM((3, R, PAD), BF16),
            pltpu.VMEM((3, R, PAD), BF16),
            dma((2,)),
            dma((3, 2)), dma((3, 2)),
            dma((3,)), dma((3,)),
            dma((2, 3)), dma((2, 3)),
            dma((2, 4, 3)), dma((2, 4, 3)),
            dma((2, 4)), dma((2, 4)),
            dma((3,)), dma((3,)),
            dma((3,)), dma((3,)),
            dma((8,)), dma((8,)),
            dma((3, 4)), dma((3, 4)),
            dma((3, 2)), dma((3, 2)),
            dma((2, 3)), dma((2, 3)),
        ],
        compiler_params=pltpu.CompilerParams(
            collective_id=0, has_side_effects=True, vmem_limit_bytes=56 * 2**20
        ),
    )(images, projections, noise_weights.reshape(56, 128), class_prior, class_lists.T)
    sums, totals, evidence = pl.pallas_call(
        finish,
        name="finish",
        out_shape=(
            jax.ShapeDtypeStruct((2, R, CH), F32),
            jax.ShapeDtypeStruct((2, R), F32),
            jax.ShapeDtypeStruct((1, ROWS), F32),
        ),
        in_specs=[vmem] * 2,
        out_specs=(vmem,) * 3,
    )(sums, evidence)
    return sums, totals, evidence.reshape(ROWS)


def solution(mesh):
    finer = Mesh(mesh.devices.reshape(2, 2, 2, 4, 4), AXES)
    rows, cls, prt = P(AXES, None), ("xh", "c"), ("xl", "z", "y")
    return jax.shard_map(
        local,
        mesh=finer,
        in_specs=(rows, P(cls, None, prt), P(), P(), rows),
        out_specs=(P(cls, None, prt), P(cls, None), P(AXES)),
        check_vma=False,
    )
```

```python
import jax
import jax.numpy as jnp
from jax import lax
from jax.experimental import pallas as pl
from jax.experimental.pallas import tpu as pltpu
from jax.sharding import Mesh
from jax.sharding import PartitionSpec as P

AXES = ("xh", "c", "xl", "z", "y")
MESH = pl.DeviceIdType.MESH
R = 144
ROWS = 128
CH = 224
PAD = 256
PIECE = 4 * CH
F32 = jnp.float32
BF16 = jnp.bfloat16


def kernel(
    img_ref, proj_hbm, nw_hbm, prior_hbm, list_hbm,
    out_ref, evid_ref,
    img, lists, xb, wb, nwp, pb, cross, sbuf, srecv, post, pt,
    mb, mr, sb, ra, rb, t2a, t2b, ga, gb, fa, fb,
    proj_ref, nw_ref, prior_ref, in_sem, own_sem, img_ss, img_rs, list_ss, list_rs, p1_ss, p1_rs, p2_ss, p2_rs, pm_ss, pm_rs,
    s_ss, s_rs, q_ss, q_rs, m_ss, m_rs, xa_ss, xa_rs, yb_ss, yb_rs, r2_ss, r2_rs,
):
    xh, c, xl = lax.axis_index("xh"), lax.axis_index("c"), lax.axis_index("xl")
    z, y = lax.axis_index("z"), lax.axis_index("y")
    x = 2 * xh + xl
    mate = (xh, 1 - c, xl, z, y)

    def at_x(s):
        t = lax.rem(x + s, 4)
        return (lax.div(t, 2), c, lax.rem(t, 2), z, y)

    def at_y(s):
        return (xh, c, xl, z, lax.rem(y + s, 4))

    def at_z(s):
        return (xh, c, xl, lax.rem(z + s, 4), y)

    def remote(src, dst, ss, rs, dev):
        return pltpu.make_async_remote_copy(
            src_ref=src, dst_ref=dst, send_sem=ss, recv_sem=rs, device_id=dev, device_id_type=MESH
        )

    barrier = pltpu.get_barrier_semaphore()
    pl.semaphore_signal(barrier, inc=1, device_id=mate, device_id_type=MESH)
    for s in (1, 2, 3):
        for dev in (at_x(s), at_y(s), at_z(s)):
            pl.semaphore_signal(barrier, inc=1, device_id=dev, device_id_type=MESH)

    inputs = []
    for hbm, ref in (
        (nw_hbm, nw_ref), (proj_hbm, proj_ref), (list_hbm, lists.at[0]), (prior_hbm, prior_ref)
    ):
        inputs.append(pltpu.make_async_copy(hbm, ref, in_sem.at[len(inputs)]))
        inputs[-1].start()
    own = []
    for p in range(2):
        own.append(
            pltpu.make_async_copy(
                img_ref.at[:, pl.ds(pl.multiple_of((p * 4 + z) * PIECE, 128), PIECE)],
                img.at[0, p],
                own_sem.at[p],
            )
        )
        own[p].start()

    inputs[0].wait()
    for p in range(2):
        row = (p * 4 + z) * 7
        flat = jnp.concatenate([nw_ref[pl.ds(row + t, 1), :] for t in range(7)], axis=1)
        for k in range(4):
            j = p * 4 + k
            nwp[j] = jnp.full((1, PAD), -1.0, F32)
            nwp[j, :, 0:CH] = flat[:, k * CH : (k + 1) * CH]

    lane = lax.broadcasted_iota(jnp.int32, (R, 128), 1) - (CH - 128)
    weights = nwp[xl * 4 + y]
    inputs[1].wait()
    for q in range(2):
        pb[xl, y, xh, c, q] = jnp.zeros((R, PAD), BF16)
        pb[xl, y, xh, c, q, :, 0:CH] = proj_ref[q]
        value = pb[xl, y, xh, c, q].astype(F32)
        left = 0.5 * jnp.sum(value * value * weights, axis=1, keepdims=True)
        tail = value[:, 128:PAD]
        for t in range(3):
            term = left.astype(BF16).astype(F32)
            left = left - term
            tail = jnp.where(lane == t, term, tail)
        pb[xl, y, xh, c, q, :, 128:PAD] = tail.astype(BF16)
    inputs[2].wait()
    inputs[3].wait()

    pl.semaphore_wait(barrier, 10)

    p1, p2, pm = {}, {}, {}

    def origin(half, s, t):
        u, v = (t, s) if half == 0 else (s, t)
        u = lax.rem(x + 4 - u, 4)
        return pb.at[lax.rem(u, 2), lax.rem(y + 4 - v, 4), lax.div(u, 2), c, half]

    def hop(half, s, t, to):
        block, k = origin(half, s, t), (t + to) % 4
        p2[half, s, k] = remote(
            block, block, p2_ss.at[half, s, k - 1], p2_rs.at[half, s, k - 1],
            at_x(to) if half == 0 else at_y(to),
        )
        p2[half, s, k].start()

    def second(half, s):
        for to in (1, 3):
            hop(half, s, 0, to)

    for half in range(2):
        for s in (1, 3, 2):
            block = origin(half, 0, 0)
            p1[half, s] = remote(
                block, block, p1_ss.at[half, s - 1], p1_rs.at[half, s - 1],
                at_y(s) if half == 0 else at_x(s),
            )
            p1[half, s].start()
    for half in range(2):
        second(half, 0)
    lcp = {}

    def image(s, p):
        to = lax.rem(z + s, 4)
        return remote(
            img_ref.at[:, pl.ds(pl.multiple_of((p * 4 + to) * PIECE, 128), PIECE)],
            img.at[s, p],
            img_ss.at[s - 1, p], img_rs.at[s - 1, p], at_z(s),
        )

    for s in (1, 3, 2):
        lcp[s] = remote(lists.at[0], lists.at[s], list_ss.at[s - 1], list_rs.at[s - 1], at_z(s))
        lcp[s].start()
        for p in range(2):
            image(s, p).start()

    late = (z == 0) & (c == 0)
    order = (3, lax.select(late, 2, 1), lax.select(late, 1, 2), 0)

    def spread(place, s, p):
        past = lax.broadcasted_iota(jnp.int32, (ROWS, 128), 1) - (CH - 128)
        ones = jnp.where((past >= 0) & (past < 3), 1.0, 0.0)
        rows = pl.ds(pl.multiple_of(place * ROWS, ROWS), ROWS)
        piece = img[s, p].astype(F32)
        for k in range(4):
            j = p * 4 + k
            chunk = piece[:, k * CH : (k + 1) * CH]
            xb[j, rows, 128:PAD] = ones.astype(BF16)
            xb[j, rows, 0:CH] = chunk.astype(BF16)
            full = xb[j, rows, :].astype(F32)
            wb[j, rows, :] = (full * nwp[j]).astype(BF16)

    for p in range(2):
        own[p].wait()
        spread(3, 0, p)

    def mate_copy(half, t):
        u = lax.rem((x if half == 0 else y) + 4 - t, 4)
        if half == 0:
            block = pb.at[lax.rem(u, 2), :, lax.div(u, 2), c, 0]
        else:
            block = pb.at[:, u, :, c, 1]
        pm[half, t] = remote(block, block, pm_ss.at[half, t], pm_rs.at[half, t], mate)
        pm[half, t].start()

    for s in (1, 3, 2):
        for half in range(2):
            p1[half, s].wait_recv()
            second(half, s)
    for half in range(2):
        mate_copy(half, 0)
    for s in (0, 1, 3, 2):
        for half in range(2):
            way = 1 if s % 2 == 0 else 3
            p2[half, s, way].wait_recv()
            hop(half, s, way, way)

    for t in (1, 3, 2):
        for half in range(2):
            for s in range(4):
                if t == 2 or t != (1 if s % 2 == 0 else 3):
                    p2[half, s, t].wait_recv()
            mate_copy(half, t)
    for s in (1, 2, 3):
        lcp[s].wait_recv()
    for t in range(4):
        for half in range(2):
            pm[half, t].wait_recv()

    def score_copy(s):
        return remote(sbuf.at[s], srecv.at[s - 1], s_ss.at[s - 1], s_rs.at[s - 1], at_z(4 - s))

    def scores(s, lanes):
        def body(i, carry):
            start = pl.multiple_of(i * 16, 16)
            listed = [jnp.broadcast_to(lists[s, t : t + 1, :], (16, ROWS)) for t in range(2)]
            chosen = [jnp.zeros((16, ROWS), F32)] * 2
            for k in range(8):
                rows = pl.ds(k * R + start, 16)
                part = cross[0, rows, lanes] + cross[1, rows, lanes]
                for t in range(2):
                    chosen[t] = jnp.where(listed[t] == k, part, chosen[t])
            for t in range(2):
                sbuf[s, t, pl.ds(start, 16), :] = chosen[t]
            return carry

        lax.fori_loop(0, R // 16, body, 0)

    def pair(k, carry):
        i, p = lax.div(k, 2), lax.rem(k, 2)
        first = lax.select(i == 0, order[0], order[2])
        second = lax.select(i == 0, order[1], order[3])
        image(first, p).wait_recv()
        spread(2 * i, first, p)

        @pl.when(i == 0)
        def _():
            image(second, p).wait_recv()
            spread(1, second, p)

        left = jnp.concatenate([pb[p, t].reshape(8 * R, PAD) for t in range(4)], axis=1)
        rows = pl.ds(pl.multiple_of(2 * i * ROWS, ROWS), 2 * ROWS)
        right = jnp.concatenate([wb[p * 4 + t, rows, :] for t in range(4)], axis=1)
        cross[p] = lax.dot_general(
            left, right, (((1,), (1,)), ((), ())), preferred_element_type=F32
        )

        @pl.when(p == 1)
        def _():
            scores(first, slice(0, ROWS))
            score_copy(first).start()
            scores(second, slice(ROWS, 2 * ROWS))

        @pl.when((p == 1) & (i == 0))
        def _():
            score_copy(second).start()

        return carry

    lax.fori_loop(0, 4, pair, 0)

    for s in (1, 3, 2):
        score_copy(s).wait_recv()
    score = []
    for slot in range(2):
        prior = jnp.ones((1, ROWS), F32)
        for k in range(8):
            prior = jnp.where(lists[0, slot : slot + 1, :] == k, prior_ref[k], prior)
        total = (sbuf[0, slot] + srecv[0, slot]) + (srecv[1, slot] + srecv[2, slot])
        score.append(total + jnp.log(prior))
    top = jnp.maximum(
        jnp.max(score[0], axis=0, keepdims=True), jnp.max(score[1], axis=0, keepdims=True)
    )
    mass = jnp.sum(jnp.exp(score[0] - top), axis=0, keepdims=True) + jnp.sum(
        jnp.exp(score[1] - top), axis=0, keepdims=True
    )
    evid = top + jnp.log(mass)
    evid_ref[...] = evid
    for slot in range(2):
        post[0, slot] = jnp.exp(score[slot] - evid).astype(BF16)

    def post_copy(s):
        return remote(post.at[0], post.at[s], q_ss.at[s - 1], q_rs.at[s - 1], at_z(s))

    for s in (2, 1, 3):
        post_copy(s).start()

    def expand(place, s):
        lanes = pl.ds(pl.multiple_of(place * ROWS, ROWS), ROWS)

        def body(k, carry):
            kh, kc, kq = lax.div(k, 4), lax.rem(lax.div(k, 2), 2), lax.rem(k, 2)
            value = jnp.zeros((R, ROWS), F32)
            for slot in range(2):
                hit = jnp.broadcast_to(lists[s, slot : slot + 1, :] == k, (R, ROWS))
                value = jnp.where(hit, post[s, slot].astype(F32), value)
            pt[lax.rem(kc + c, 2), kh, kq, :, lanes] = value.astype(BF16)
            return carry

        lax.fori_loop(0, 8, body, 0)

    expand(3, 0)

    def take(place, carry):
        s = lax.select(place == 0, order[0], lax.select(place == 1, order[1], order[2]))
        post_copy(s).wait_recv()
        expand(place, s)
        return carry

    lax.fori_loop(0, 3, take, 0)

    def far(i):
        i = lax.div(i, 2)
        t = lax.rem(3 * i + 2, 4)
        return lax.select(i < 2, t, 3 - t)

    def chunk_of(i):
        return lax.rem(xl + lax.rem(i, 2), 2), lax.rem(y + far(i), 4)

    def mate_sum(i):
        jl, jy = chunk_of(i)
        return remote(mb.at[jl, jy], mr.at[jl, jy], m_ss.at[i], m_rs.at[i], mate)

    def block_x(v, s):
        t = lax.rem(x + s, 4)
        return sb.at[lax.rem(t, 2), lax.rem(y + v, 4), lax.div(t, 2), 0]

    def block_y(v, u):
        return sb.at[lax.rem(xl + u, 2), lax.rem(y + v, 4), :, 1]

    def along_x(i, part):
        way = 1 + 2 * lax.rem(i, 2)
        v = far(2 * i)
        shift = (way, 4 - way, 2)[part]
        return remote(
            block_x(v, shift), ra.at[part, i], xa_ss.at[part, i], xa_rs.at[part, i],
            at_x((way, 4 - way, way)[part]),
        )

    def along_y(u, part):
        way = 1 + 2 * u
        shift = (way, 4 - way, 2)[part]
        return remote(
            block_y(shift, u), rb.at[part, u], yb_ss.at[part, u], yb_rs.at[part, u],
            at_y((way, 4 - way, way)[part]),
        )

    def pass_x(i):
        along_x(i, 2).wait_recv()
        block = block_x(far(2 * i), 1 + 2 * lax.rem(i, 2))
        block[...] = (block[...].astype(F32) + ra[2, i].astype(F32)).astype(BF16)
        along_x(i, 0).start()

    def pass_y(u):
        along_y(u, 2).wait_recv()
        block = block_y(1 + 2 * u, u)
        block[...] = (block[...].astype(F32) + rb[2, u].astype(F32)).astype(BF16)
        along_y(u, 0).start()

    def product(i):
        jl, jy = chunk_of(i)
        left = pt[...].reshape(8 * R, 4 * ROWS)
        both = jnp.dot(left, xb[jl * 4 + jy], preferred_element_type=F32)
        both = both.reshape(2, 2, 2, R, PAD).astype(BF16)
        mb[jl, jy] = both[1]
        sb[jl, jy] = both[0]
        mate_sum(i).start()

    def join(i):
        jl, jy = chunk_of(i)
        mate_sum(i).wait_recv()
        sb[jl, jy] = (sb[jl, jy].astype(F32) + mr[jl, jy].astype(F32)).astype(BF16)

    def ahead(i, carry):
        product(i)
        return carry

    def steady(i, carry):
        @pl.when(i < 3)
        def _():
            product(2 * i + 2)

        join(2 * i)
        along_x(i, 2).start()

        @pl.when(i == 0)
        def _():
            along_y(0, 2).start()

        @pl.when(i == 2)
        def _():
            along_y(0, 1).start()

        @pl.when(i < 3)
        def _():
            product(2 * i + 3)

        join(2 * i + 1)

        @pl.when(i == 0)
        def _():
            along_y(1, 2).start()

        @pl.when(i == 1)
        def _():
            along_y(1, 1).start()

        along_x(i, 1).start()

        @pl.when(i == 2)
        def _():
            pass_x(0)

        @pl.when(i == 3)
        def _():
            pass_y(0)

        return carry

    lax.fori_loop(0, 2, ahead, 0)
    lax.fori_loop(0, 4, steady, 0)
    pass_x(1)
    pass_y(1)
    pass_x(2)
    pass_x(3)

    def last_y(v):
        return remote(t2a.at[v], fa.at[v - 1], r2_ss.at[0, v - 1], r2_rs.at[0, v - 1], at_y(v))

    def last_x(s):
        t = lax.rem(x + s, 4)
        return remote(
            t2b.at[lax.rem(t, 2), lax.div(t, 2)], fb.at[s - 1],
            r2_ss.at[1, s - 1], r2_rs.at[1, s - 1], at_x(s),
        )

    def add_x(i):
        along_x(i, 1).wait_recv()
        along_x(i, 0).wait_recv()
        total = block_x(far(2 * i), 0)[...].astype(F32)
        return total + (ra[0, i].astype(F32) + ra[1, i].astype(F32))

    def leave_y(i, carry):
        v = far(2 * i)
        t2a[v] = add_x(i).astype(BF16)
        last_y(v).start()
        return carry

    lax.fori_loop(0, 3, leave_y, 0)
    for u, shifts in enumerate(((2,), (1, 3))):
        jl = lax.rem(xl + u, 2)
        along_y(u, 1).wait_recv()
        along_y(u, 0).wait_recv()
        total = block_y(0, u)[...].astype(F32) + (rb[0, u].astype(F32) + rb[1, u].astype(F32))
        gb[jl] = total
        t2b[jl] = total.astype(BF16)
        for s in shifts:
            last_x(s).start()
    ga[...] = add_x(3)

    for v in (1, 2, 3):
        last_y(v).wait_recv()
    out_ref[0] = (ga[...] + fa[0].astype(F32)) + (fa[1].astype(F32) + fa[2].astype(F32))
    for s in (1, 2, 3):
        last_x(s).wait_recv()
    out_ref[1] = (gb[xl, xh] + fb[0].astype(F32)) + (fb[1].astype(F32) + fb[2].astype(F32))

    for group in (p1, lcp, p2, pm):
        for cp in group.values():
            cp.wait_send()
    for s in (1, 2, 3):
        score_copy(s).wait_send()
        post_copy(s).wait_send()
        for p in range(2):
            image(s, p).wait_send()

    def mate_done(i, carry):
        mate_sum(i).wait_send()
        return carry

    lax.fori_loop(0, 8, mate_done, 0)
    for part in range(3):
        for i in range(4):
            along_x(i, part).wait_send()
        for u in range(2):
            along_y(u, part).wait_send()
    for s in (1, 2, 3):
        last_y(s).wait_send()
        last_x(s).wait_send()


def finish(sums_ref, evid_ref, out_ref, total_ref, out_evid_ref):
    for q in range(2):
        out_ref[q] = sums_ref[q, :, 0:CH]
        total_ref[q : q + 1, :] = sums_ref[q, :, 128:PAD].T[CH - 128 : CH - 127, :]
    out_evid_ref[...] = evid_ref[...]


def local(images, projections, noise_weights, class_prior, class_lists):
    dma = pltpu.SemaphoreType.DMA
    vmem = pl.BlockSpec(memory_space=pltpu.VMEM)
    sums, evidence = pl.pallas_call(
        kernel,
        name="estep",
        out_shape=(
            jax.ShapeDtypeStruct((2, R, PAD), F32),
            jax.ShapeDtypeStruct((1, ROWS), F32),
        ),
        in_specs=[pl.BlockSpec(memory_space=pl.ANY)] * 5,
        out_specs=(vmem, vmem),
        scratch_shapes=[
            pltpu.VMEM((4, 2, ROWS, PIECE), BF16),
            pltpu.VMEM((4, 2, ROWS), jnp.int32),
            pltpu.VMEM((8, 4 * ROWS, PAD), BF16),
            pltpu.VMEM((8, 4 * ROWS, PAD), BF16),
            pltpu.VMEM((8, 1, PAD), F32),
            pltpu.VMEM((2, 4, 2, 2, 2, R, PAD), BF16),
            pltpu.VMEM((2, 8 * R, 2 * ROWS), F32),
            pltpu.VMEM((4, 2, R, ROWS), F32),
            pltpu.VMEM((3, 2, R, ROWS), F32),
            pltpu.VMEM((4, 2, R, ROWS), BF16),
            pltpu.VMEM((2, 2, 2, R, 4 * ROWS), BF16),
            pltpu.VMEM((2, 4, 2, 2, R, PAD), BF16),
            pltpu.VMEM((2, 4, 2, 2, R, PAD), BF16),
            pltpu.VMEM((2, 4, 2, 2, R, PAD), BF16),
            pltpu.VMEM((3, 4, R, PAD), BF16),
            pltpu.VMEM((3, 2, 2, R, PAD), BF16),
            pltpu.VMEM((4, R, PAD), BF16),
            pltpu.VMEM((2, 2, R, PAD), BF16),
            pltpu.VMEM((R, PAD), F32),
            pltpu.VMEM((2, 2, R, PAD), F32),
            pltpu.VMEM((3, R, PAD), BF16),
            pltpu.VMEM((3, R, PAD), BF16),
            pltpu.VMEM((2, R, CH), BF16),
            pltpu.VMEM((56, 128), F32),
            pltpu.SMEM((8,), F32),
            dma((4,)),
            dma((2,)),
            dma((3, 2)), dma((3, 2)),
            dma((3,)), dma((3,)),
            dma((2, 3)), dma((2, 3)),
            dma((2, 4, 3)), dma((2, 4, 3)),
            dma((2, 4)), dma((2, 4)),
            dma((3,)), dma((3,)),
            dma((3,)), dma((3,)),
            dma((8,)), dma((8,)),
            dma((3, 4)), dma((3, 4)),
            dma((3, 2)), dma((3, 2)),
            dma((2, 3)), dma((2, 3)),
        ],
        compiler_params=pltpu.CompilerParams(
            collective_id=0, has_side_effects=True, vmem_limit_bytes=56 * 2**20
        ),
    )(images, projections, noise_weights.reshape(56, 128), class_prior, class_lists.T)
    sums, totals, evidence = pl.pallas_call(
        finish,
        name="finish",
        out_shape=(
            jax.ShapeDtypeStruct((2, R, CH), F32),
            jax.ShapeDtypeStruct((2, R), F32),
            jax.ShapeDtypeStruct((1, ROWS), F32),
        ),
        in_specs=[vmem] * 2,
        out_specs=(vmem,) * 3,
    )(sums, evidence)
    return sums, totals, evidence.reshape(ROWS)


def solution(mesh):
    finer = Mesh(mesh.devices.reshape(2, 2, 2, 4, 4), AXES)
    rows, cls, prt = P(AXES, None), ("xh", "c"), ("xl", "z", "y")
    return jax.shard_map(
        local,
        mesh=finer,
        in_specs=(rows, P(cls, None, prt), P(), P(), rows),
        out_specs=(P(cls, None, prt), P(cls, None), P(AXES)),
        check_vma=False,
    )
```

```python
import jax
import jax.numpy as jnp
from jax import lax
from jax.experimental import pallas as pl
from jax.experimental.pallas import tpu as pltpu
from jax.sharding import Mesh
from jax.sharding import PartitionSpec as P

AXES = ("xh", "c", "xl", "z", "y")
MESH = pl.DeviceIdType.MESH
R = 144
ROWS = 128
CH = 224
PAD = 256
PIECE = 4 * CH
F32 = jnp.float32
BF16 = jnp.bfloat16


def kernel(
    img_ref, proj_hbm, nw_hbm, prior_hbm, list_hbm,
    out_ref, evid_ref,
    img, lists, xb, wb, nwp, pb, cross, sbuf, srecv, post, pt,
    mb, mr, sb, ra, rb, t2a, t2b, ga, gb, fa, fb,
    proj_ref, nw_ref, prior_ref, in_sem, own_sem, img_ss, img_rs, list_ss, list_rs, p1_ss, p1_rs, p2_ss, p2_rs, pm_ss, pm_rs,
    s_ss, s_rs, q_ss, q_rs, m_ss, m_rs, xa_ss, xa_rs, yb_ss, yb_rs, r2_ss, r2_rs,
):
    xh, c, xl = lax.axis_index("xh"), lax.axis_index("c"), lax.axis_index("xl")
    z, y = lax.axis_index("z"), lax.axis_index("y")
    x = 2 * xh + xl
    mate = (xh, 1 - c, xl, z, y)

    def at_x(s):
        t = lax.rem(x + s, 4)
        return (lax.div(t, 2), c, lax.rem(t, 2), z, y)

    def at_y(s):
        return (xh, c, xl, z, lax.rem(y + s, 4))

    def at_z(s):
        return (xh, c, xl, lax.rem(z + s, 4), y)

    def remote(src, dst, ss, rs, dev):
        return pltpu.make_async_remote_copy(
            src_ref=src, dst_ref=dst, send_sem=ss, recv_sem=rs, device_id=dev, device_id_type=MESH
        )

    barrier = pltpu.get_barrier_semaphore()
    pl.semaphore_signal(barrier, inc=1, device_id=mate, device_id_type=MESH)
    for s in (1, 2, 3):
        for dev in (at_x(s), at_y(s), at_z(s)):
            pl.semaphore_signal(barrier, inc=1, device_id=dev, device_id_type=MESH)

    inputs = []
    for hbm, ref in (
        (nw_hbm, nw_ref), (proj_hbm, proj_ref), (list_hbm, lists.at[0]), (prior_hbm, prior_ref)
    ):
        inputs.append(pltpu.make_async_copy(hbm, ref, in_sem.at[len(inputs)]))
        inputs[-1].start()
    own = []
    for p in range(2):
        own.append(
            pltpu.make_async_copy(
                img_ref.at[:, pl.ds(pl.multiple_of((p * 4 + z) * PIECE, 128), PIECE)],
                img.at[0, p],
                own_sem.at[p],
            )
        )
        own[p].start()

    pl.semaphore_wait(barrier, 10)

    def image(s, p):
        to = lax.rem(z + s, 4)
        return remote(
            img_ref.at[:, pl.ds(pl.multiple_of((p * 4 + to) * PIECE, 128), PIECE)],
            img.at[s, p],
            img_ss.at[s - 1, p], img_rs.at[s - 1, p], at_z(s),
        )

    image(1, 0).start()
    image(3, 0).start()

    inputs[0].wait()
    for p in range(2):
        row = (p * 4 + z) * 7
        flat = jnp.concatenate([nw_ref[pl.ds(row + t, 1), :] for t in range(7)], axis=1)
        for k in range(4):
            j = p * 4 + k
            nwp[j] = jnp.full((1, PAD), -1.0, F32)
            nwp[j, :, 0:CH] = flat[:, k * CH : (k + 1) * CH]

    lane = lax.broadcasted_iota(jnp.int32, (R, 128), 1) - (CH - 128)
    weights = nwp[xl * 4 + y]
    inputs[1].wait()
    for q in range(2):
        pb[xl, y, xh, c, q] = jnp.zeros((R, PAD), BF16)
        pb[xl, y, xh, c, q, :, 0:CH] = proj_ref[q]
        value = pb[xl, y, xh, c, q].astype(F32)
        left = 0.5 * jnp.sum(value * value * weights, axis=1, keepdims=True)
        tail = value[:, 128:PAD]
        for t in range(3):
            term = left.astype(BF16).astype(F32)
            left = left - term
            tail = jnp.where(lane == t, term, tail)
        pb[xl, y, xh, c, q, :, 128:PAD] = tail.astype(BF16)
    inputs[2].wait()
    inputs[3].wait()

    p1, p2, pm = {}, {}, {}

    def origin(half, s, t):
        u, v = (t, s) if half == 0 else (s, t)
        u = lax.rem(x + 4 - u, 4)
        return pb.at[lax.rem(u, 2), lax.rem(y + 4 - v, 4), lax.div(u, 2), c, half]

    def hop(half, s, t, to):
        block, k = origin(half, s, t), (t + to) % 4
        p2[half, s, k] = remote(
            block, block, p2_ss.at[half, s, k - 1], p2_rs.at[half, s, k - 1],
            at_x(to) if half == 0 else at_y(to),
        )
        p2[half, s, k].start()

    def second(half, s):
        for to in (1, 3):
            hop(half, s, 0, to)

    for half in range(2):
        for s in (1, 3, 2):
            block = origin(half, 0, 0)
            p1[half, s] = remote(
                block, block, p1_ss.at[half, s - 1], p1_rs.at[half, s - 1],
                at_y(s) if half == 0 else at_x(s),
            )
            p1[half, s].start()
    for half in range(2):
        second(half, 0)
    lcp = {}
    for s in (1, 3, 2):
        lcp[s] = remote(lists.at[0], lists.at[s], list_ss.at[s - 1], list_rs.at[s - 1], at_z(s))
        lcp[s].start()

    late = (z == 0) & (c == 0)
    order = (3, lax.select(late, 2, 1), lax.select(late, 1, 2), 0)

    def spread(place, s, p):
        past = lax.broadcasted_iota(jnp.int32, (ROWS, 128), 1) - (CH - 128)
        ones = jnp.where((past >= 0) & (past < 3), 1.0, 0.0)
        rows = pl.ds(pl.multiple_of(place * ROWS, ROWS), ROWS)
        piece = img[s, p].astype(F32)
        for k in range(4):
            j = p * 4 + k
            chunk = piece[:, k * CH : (k + 1) * CH]
            xb[j, rows, 128:PAD] = ones.astype(BF16)
            xb[j, rows, 0:CH] = chunk.astype(BF16)
            full = xb[j, rows, :].astype(F32)
            wb[j, rows, :] = (full * nwp[j]).astype(BF16)

    for p in range(2):
        own[p].wait()
        spread(3, 0, p)

    def mate_copy(half, t):
        u = lax.rem((x if half == 0 else y) + 4 - t, 4)
        if half == 0:
            block = pb.at[lax.rem(u, 2), :, lax.div(u, 2), c, 0]
        else:
            block = pb.at[:, u, :, c, 1]
        pm[half, t] = remote(block, block, pm_ss.at[half, t], pm_rs.at[half, t], mate)
        pm[half, t].start()

    for s in (1, 3, 2):
        for half in range(2):
            p1[half, s].wait_recv()
            second(half, s)
        if s == 1:
            image(1, 1).start()
            image(3, 1).start()
    image(2, 0).start()
    for half in range(2):
        mate_copy(half, 0)
    for s in (0, 1, 3, 2):
        for half in range(2):
            way = 1 if s % 2 == 0 else 3
            p2[half, s, way].wait_recv()
            hop(half, s, way, way)
    image(2, 1).start()

    for t in (1, 3, 2):
        for half in range(2):
            for s in range(4):
                if t == 2 or t != (1 if s % 2 == 0 else 3):
                    p2[half, s, t].wait_recv()
            mate_copy(half, t)
    for s in (1, 2, 3):
        lcp[s].wait_recv()

    def early(k, carry):
        s, p = lax.select(k == 1, order[1], order[0]), lax.div(k, 2)
        image(s, p).wait_recv()
        spread(lax.rem(k, 2), s, p)
        return carry

    lax.fori_loop(0, 3, early, 0)
    for t in range(4):
        for half in range(2):
            pm[half, t].wait_recv()

    def score_copy(s):
        return remote(sbuf.at[s], srecv.at[s - 1], s_ss.at[s - 1], s_rs.at[s - 1], at_z(4 - s))

    def scores(s, n, lanes):
        def body(i, carry):
            start = pl.multiple_of(i * 16, 16)
            listed = [jnp.broadcast_to(lists[s, t : t + 1, :], (16, ROWS)) for t in range(2)]
            chosen = [jnp.zeros((16, ROWS), F32)] * 2
            for k in range(8):
                rows = pl.ds(k * R + start, 16)
                part = cross[n, 0, rows, lanes] + cross[n, 1, rows, lanes]
                for t in range(2):
                    chosen[t] = jnp.where(listed[t] == k, part, chosen[t])
            for t in range(2):
                sbuf[s, t, pl.ds(start, 16), :] = chosen[t]
            return carry

        lax.fori_loop(0, R // 16, body, 0)

    def pair(k, carry):
        i, p = lax.div(k, 2), lax.rem(k, 2)

        @pl.when(k > 0)
        def _():
            s = lax.select(i == 0, order[1], order[2])
            image(s, p).wait_recv()
            spread(1 + i, s, p)

        left = jnp.concatenate([pb[p, t].reshape(8 * R, PAD) for t in range(4)], axis=1)
        rows = pl.ds(pl.multiple_of(2 * i * ROWS, ROWS), 2 * ROWS)
        right = jnp.concatenate([wb[p * 4 + t, rows, :] for t in range(4)], axis=1)
        cross[i, p] = lax.dot_general(
            left, right, (((1,), (1,)), ((), ())), preferred_element_type=F32
        )

        @pl.when(p == 1)
        def _():
            first = lax.select(i == 0, order[0], order[2])
            second = lax.select(i == 0, order[1], order[3])
            scores(first, i, slice(0, ROWS))
            score_copy(first).start()
            scores(second, i, slice(ROWS, 2 * ROWS))

            @pl.when(i == 0)
            def _():
                score_copy(second).start()

        return carry

    lax.fori_loop(0, 4, pair, 0)

    for s in (1, 3, 2):
        score_copy(s).wait_recv()
    score = []
    for slot in range(2):
        prior = jnp.ones((1, ROWS), F32)
        for k in range(8):
            prior = jnp.where(lists[0, slot : slot + 1, :] == k, prior_ref[k], prior)
        total = (sbuf[0, slot] + srecv[0, slot]) + (srecv[1, slot] + srecv[2, slot])
        score.append(total + jnp.log(prior))
    top = jnp.maximum(
        jnp.max(score[0], axis=0, keepdims=True), jnp.max(score[1], axis=0, keepdims=True)
    )
    mass = jnp.sum(jnp.exp(score[0] - top), axis=0, keepdims=True) + jnp.sum(
        jnp.exp(score[1] - top), axis=0, keepdims=True
    )
    evid = top + jnp.log(mass)
    evid_ref[...] = evid
    for slot in range(2):
        post[0, slot] = jnp.exp(score[slot] - evid).astype(BF16)

    def post_copy(s):
        return remote(post.at[0], post.at[s], q_ss.at[s - 1], q_rs.at[s - 1], at_z(s))

    for s in (2, 1, 3):
        post_copy(s).start()

    def expand(place, s):
        lanes = pl.ds(pl.multiple_of(place * ROWS, ROWS), ROWS)

        def body(k, carry):
            kh, kc, kq = lax.div(k, 4), lax.rem(lax.div(k, 2), 2), lax.rem(k, 2)
            value = jnp.zeros((R, ROWS), F32)
            for slot in range(2):
                hit = jnp.broadcast_to(lists[s, slot : slot + 1, :] == k, (R, ROWS))
                value = jnp.where(hit, post[s, slot].astype(F32), value)
            pt[lax.rem(kc + c, 2), kh, kq, :, lanes] = value.astype(BF16)
            return carry

        lax.fori_loop(0, 8, body, 0)

    expand(3, 0)

    def take(place, carry):
        s = lax.select(place == 0, order[0], lax.select(place == 1, order[1], order[2]))
        post_copy(s).wait_recv()
        expand(place, s)
        return carry

    lax.fori_loop(0, 3, take, 0)

    def far(i):
        i = lax.div(i, 2)
        t = lax.rem(3 * i + 2, 4)
        return lax.select(i < 2, t, 3 - t)

    def chunk_of(i):
        return lax.rem(xl + lax.rem(i, 2), 2), lax.rem(y + far(i), 4)

    def mate_sum(i):
        jl, jy = chunk_of(i)
        return remote(mb.at[jl, jy], mr.at[jl, jy], m_ss.at[i], m_rs.at[i], mate)

    def block_x(v, s):
        t = lax.rem(x + s, 4)
        return sb.at[lax.rem(t, 2), lax.rem(y + v, 4), lax.div(t, 2), 0]

    def block_y(v, u):
        return sb.at[lax.rem(xl + u, 2), lax.rem(y + v, 4), :, 1]

    def along_x(i, part):
        way = 1 + 2 * lax.rem(i, 2)
        v = far(2 * i)
        shift = (way, 4 - way, 2)[part]
        return remote(
            block_x(v, shift), ra.at[part, i], xa_ss.at[part, i], xa_rs.at[part, i],
            at_x((way, 4 - way, way)[part]),
        )

    def along_y(u, part):
        way = 1 + 2 * u
        shift = (way, 4 - way, 2)[part]
        return remote(
            block_y(shift, u), rb.at[part, u], yb_ss.at[part, u], yb_rs.at[part, u],
            at_y((way, 4 - way, way)[part]),
        )

    def pass_x(i):
        along_x(i, 2).wait_recv()
        block = block_x(far(2 * i), 1 + 2 * lax.rem(i, 2))
        block[...] = (block[...].astype(F32) + ra[2, i].astype(F32)).astype(BF16)
        along_x(i, 0).start()

    def pass_y(u):
        along_y(u, 2).wait_recv()
        block = block_y(1 + 2 * u, u)
        block[...] = (block[...].astype(F32) + rb[2, u].astype(F32)).astype(BF16)
        along_y(u, 0).start()

    def product(i):
        jl, jy = chunk_of(i)
        left = pt[...].reshape(8 * R, 4 * ROWS)
        both = jnp.dot(left, xb[jl * 4 + jy], preferred_element_type=F32)
        both = both.reshape(2, 2, 2, R, PAD).astype(BF16)
        mb[jl, jy] = both[1]
        sb[jl, jy] = both[0]
        mate_sum(i).start()

    def join(i):
        jl, jy = chunk_of(i)
        mate_sum(i).wait_recv()
        sb[jl, jy] = (sb[jl, jy].astype(F32) + mr[jl, jy].astype(F32)).astype(BF16)

    def ahead(i, carry):
        product(i)
        return carry

    def steady(i, carry):
        for u in range(2):

            @pl.when(i < 3)
            def _():
                product(2 * i + 2 + u)

            join(2 * i + u)
            for step, part in ((0, 2), (1 + u, u), (2 - u, 1 - u)):
                if part:

                    @pl.when(i == step)
                    def _():
                        along_y(u, part).start()

            along_x(i, 2 - u).start()
        return carry

    lax.fori_loop(0, 2, ahead, 0)
    lax.fori_loop(0, 4, steady, 0)

    def last_y(v):
        return remote(t2a.at[v], fa.at[v - 1], r2_ss.at[0, v - 1], r2_rs.at[0, v - 1], at_y(v))

    def last_x(s):
        t = lax.rem(x + s, 4)
        return remote(
            t2b.at[lax.rem(t, 2), lax.div(t, 2)], fb.at[s - 1],
            r2_ss.at[1, s - 1], r2_rs.at[1, s - 1], at_x(s),
        )

    def add_x(i):
        along_x(i, 1).wait_recv()
        along_x(i, 0).wait_recv()
        total = block_x(far(2 * i), 0)[...].astype(F32)
        return total + (ra[0, i].astype(F32) + ra[1, i].astype(F32))

    def leave_y(i):
        v = far(2 * i)
        t2a[v] = add_x(i).astype(BF16)
        last_y(v).start()

    def leave_x(u, shifts):
        jl = lax.rem(xl + u, 2)
        along_y(u, 1).wait_recv()
        along_y(u, 0).wait_recv()
        total = block_y(0, u)[...].astype(F32) + (rb[0, u].astype(F32) + rb[1, u].astype(F32))
        gb[jl] = total
        t2b[jl] = total.astype(BF16)
        for s in shifts:
            last_x(s).start()

    pass_y(0)
    pass_y(1)
    for i in range(4):
        pass_x(i)
    leave_y(0)
    leave_x(0, (2,))
    leave_y(1)
    leave_x(1, (1, 3))
    leave_y(2)
    ga[...] = add_x(3)

    for v in (1, 2, 3):
        last_y(v).wait_recv()
    out_ref[0] = (ga[...] + fa[0].astype(F32)) + (fa[1].astype(F32) + fa[2].astype(F32))
    for s in (1, 2, 3):
        last_x(s).wait_recv()
    out_ref[1] = (gb[xl, xh] + fb[0].astype(F32)) + (fb[1].astype(F32) + fb[2].astype(F32))

    for group in (p1, lcp, p2, pm):
        for cp in group.values():
            cp.wait_send()
    for s in (1, 2, 3):
        score_copy(s).wait_send()
        post_copy(s).wait_send()
        for p in range(2):
            image(s, p).wait_send()

    def mate_done(i, carry):
        mate_sum(i).wait_send()
        return carry

    lax.fori_loop(0, 8, mate_done, 0)
    for part in range(3):
        for i in range(4):
            along_x(i, part).wait_send()
        for u in range(2):
            along_y(u, part).wait_send()
    for s in (1, 2, 3):
        last_y(s).wait_send()
        last_x(s).wait_send()


def finish(sums_ref, evid_ref, out_ref, total_ref, out_evid_ref):
    for q in range(2):
        out_ref[q] = sums_ref[q, :, 0:CH]
        total_ref[q : q + 1, :] = sums_ref[q, :, 128:PAD].T[CH - 128 : CH - 127, :]
    out_evid_ref[...] = evid_ref[...]


def local(images, projections, noise_weights, class_prior, class_lists):
    dma = pltpu.SemaphoreType.DMA
    vmem = pl.BlockSpec(memory_space=pltpu.VMEM)
    sums, evidence = pl.pallas_call(
        kernel,
        name="estep",
        out_shape=(
            jax.ShapeDtypeStruct((2, R, PAD), F32),
            jax.ShapeDtypeStruct((1, ROWS), F32),
        ),
        in_specs=[pl.BlockSpec(memory_space=pl.ANY)] * 5,
        out_specs=(vmem, vmem),
        scratch_shapes=[
            pltpu.VMEM((4, 2, ROWS, PIECE), BF16),
            pltpu.VMEM((4, 2, ROWS), jnp.int32),
            pltpu.VMEM((8, 4 * ROWS, PAD), BF16),
            pltpu.VMEM((8, 4 * ROWS, PAD), BF16),
            pltpu.VMEM((8, 1, PAD), F32),
            pltpu.VMEM((2, 4, 2, 2, 2, R, PAD), BF16),
            pltpu.VMEM((2, 2, 8 * R, 2 * ROWS), F32),
            pltpu.VMEM((4, 2, R, ROWS), F32),
            pltpu.VMEM((3, 2, R, ROWS), F32),
            pltpu.VMEM((4, 2, R, ROWS), BF16),
            pltpu.VMEM((2, 2, 2, R, 4 * ROWS), BF16),
            pltpu.VMEM((2, 4, 2, 2, R, PAD), BF16),
            pltpu.VMEM((2, 4, 2, 2, R, PAD), BF16),
            pltpu.VMEM((2, 4, 2, 2, R, PAD), BF16),
            pltpu.VMEM((3, 4, R, PAD), BF16),
            pltpu.VMEM((3, 2, 2, R, PAD), BF16),
            pltpu.VMEM((4, R, PAD), BF16),
            pltpu.VMEM((2, 2, R, PAD), BF16),
            pltpu.VMEM((R, PAD), F32),
            pltpu.VMEM((2, 2, R, PAD), F32),
            pltpu.VMEM((3, R, PAD), BF16),
            pltpu.VMEM((3, R, PAD), BF16),
            pltpu.VMEM((2, R, CH), BF16),
            pltpu.VMEM((56, 128), F32),
            pltpu.SMEM((8,), F32),
            dma((4,)),
            dma((2,)),
            dma((3, 2)), dma((3, 2)),
            dma((3,)), dma((3,)),
            dma((2, 3)), dma((2, 3)),
            dma((2, 4, 3)), dma((2, 4, 3)),
            dma((2, 4)), dma((2, 4)),
            dma((3,)), dma((3,)),
            dma((3,)), dma((3,)),
            dma((8,)), dma((8,)),
            dma((3, 4)), dma((3, 4)),
            dma((3, 2)), dma((3, 2)),
            dma((2, 3)), dma((2, 3)),
        ],
        compiler_params=pltpu.CompilerParams(
            collective_id=0, has_side_effects=True, vmem_limit_bytes=56 * 2**20
        ),
    )(images, projections, noise_weights.reshape(56, 128), class_prior, class_lists.T)
    sums, totals, evidence = pl.pallas_call(
        finish,
        name="finish",
        out_shape=(
            jax.ShapeDtypeStruct((2, R, CH), F32),
            jax.ShapeDtypeStruct((2, R), F32),
            jax.ShapeDtypeStruct((1, ROWS), F32),
        ),
        in_specs=[vmem] * 2,
        out_specs=(vmem,) * 3,
    )(sums, evidence)
    return sums, totals, evidence.reshape(ROWS)


def solution(mesh):
    finer = Mesh(mesh.devices.reshape(2, 2, 2, 4, 4), AXES)
    rows, cls, prt = P(AXES, None), ("xh", "c"), ("xl", "z", "y")
    return jax.shard_map(
        local,
        mesh=finer,
        in_specs=(rows, P(cls, None, prt), P(), P(), rows),
        out_specs=(P(cls, None, prt), P(cls, None), P(AXES)),
        check_vma=False,
    )
```

```python
import jax
import jax.numpy as jnp
from jax import lax
from jax.experimental import pallas as pl
from jax.experimental.pallas import tpu as pltpu
from jax.sharding import Mesh
from jax.sharding import PartitionSpec as P

AXES = ("xh", "c", "xl", "z", "y")
MESH = pl.DeviceIdType.MESH
R = 144
ROWS = 128
CH = 224
PAD = 256
PIECE = 4 * CH
F32 = jnp.float32
BF16 = jnp.bfloat16


def kernel(
    img_ref, proj_hbm, nw_hbm, prior_hbm, list_hbm,
    out_ref, evid_ref,
    img, lists, xb, wb, nwp, pb, cross, sbuf, srecv, post, pt,
    mb, mr, sb, ra, rb, t2a, t2b, ga, gb, fa, fb,
    proj_ref, nw_ref, prior_ref, in_sem, own_sem, img_ss, img_rs, list_ss, list_rs, p1_ss, p1_rs, p2_ss, p2_rs, pm_ss, pm_rs,
    s_ss, s_rs, q_ss, q_rs, m_ss, m_rs, xa_ss, xa_rs, yb_ss, yb_rs, r2_ss, r2_rs,
):
    xh, c, xl = lax.axis_index("xh"), lax.axis_index("c"), lax.axis_index("xl")
    z, y = lax.axis_index("z"), lax.axis_index("y")
    x = 2 * xh + xl
    mate = (xh, 1 - c, xl, z, y)

    def at_x(s):
        t = lax.rem(x + s, 4)
        return (lax.div(t, 2), c, lax.rem(t, 2), z, y)

    def at_y(s):
        return (xh, c, xl, z, lax.rem(y + s, 4))

    def at_z(s):
        return (xh, c, xl, lax.rem(z + s, 4), y)

    def remote(src, dst, ss, rs, dev):
        return pltpu.make_async_remote_copy(
            src_ref=src, dst_ref=dst, send_sem=ss, recv_sem=rs, device_id=dev, device_id_type=MESH
        )

    barrier = pltpu.get_barrier_semaphore()
    pl.semaphore_signal(barrier, inc=1, device_id=mate, device_id_type=MESH)
    for s in (1, 2, 3):
        for dev in (at_x(s), at_y(s), at_z(s)):
            pl.semaphore_signal(barrier, inc=1, device_id=dev, device_id_type=MESH)

    inputs = []
    for hbm, ref in (
        (nw_hbm, nw_ref), (proj_hbm, proj_ref), (list_hbm, lists.at[0]), (prior_hbm, prior_ref)
    ):
        inputs.append(pltpu.make_async_copy(hbm, ref, in_sem.at[len(inputs)]))
        inputs[-1].start()
    own = []
    for p in range(2):
        own.append(
            pltpu.make_async_copy(
                img_ref.at[:, pl.ds(pl.multiple_of((p * 4 + z) * PIECE, 128), PIECE)],
                img.at[0, p],
                own_sem.at[p],
            )
        )
        own[p].start()

    pl.semaphore_wait(barrier, 10)

    def image(s, p):
        to = lax.rem(z + s, 4)
        return remote(
            img_ref.at[:, pl.ds(pl.multiple_of((p * 4 + to) * PIECE, 128), PIECE)],
            img.at[s, p],
            img_ss.at[s - 1, p], img_rs.at[s - 1, p], at_z(s),
        )

    image(1, 0).start()
    image(3, 0).start()

    inputs[0].wait()
    for p in range(2):
        row = (p * 4 + z) * 7
        flat = jnp.concatenate([nw_ref[pl.ds(row + t, 1), :] for t in range(7)], axis=1)
        for k in range(4):
            j = p * 4 + k
            nwp[j] = jnp.full((1, PAD), -1.0, F32)
            nwp[j, :, 0:CH] = flat[:, k * CH : (k + 1) * CH]

    lane = lax.broadcasted_iota(jnp.int32, (R, 128), 1) - (CH - 128)
    weights = nwp[xl * 4 + y]
    inputs[1].wait()
    for q in range(2):
        pb[xl, y, xh, c, q] = jnp.zeros((R, PAD), BF16)
        pb[xl, y, xh, c, q, :, 0:CH] = proj_ref[q]
        value = pb[xl, y, xh, c, q].astype(F32)
        left = 0.5 * jnp.sum(value * value * weights, axis=1, keepdims=True)
        tail = value[:, 128:PAD]
        for t in range(3):
            term = left.astype(BF16).astype(F32)
            left = left - term
            tail = jnp.where(lane == t, term, tail)
        pb[xl, y, xh, c, q, :, 128:PAD] = tail.astype(BF16)
    inputs[2].wait()
    inputs[3].wait()

    p1, p2, pm = {}, {}, {}

    def origin(half, s, t):
        u, v = (t, s) if half == 0 else (s, t)
        u = lax.rem(x + 4 - u, 4)
        return pb.at[lax.rem(u, 2), lax.rem(y + 4 - v, 4), lax.div(u, 2), c, half]

    def hop(half, s, t, to):
        block, k = origin(half, s, t), (t + to) % 4
        p2[half, s, k] = remote(
            block, block, p2_ss.at[half, s, k - 1], p2_rs.at[half, s, k - 1],
            at_x(to) if half == 0 else at_y(to),
        )
        p2[half, s, k].start()

    def second(half, s):
        for to in (1, 3):
            hop(half, s, 0, to)

    for half in range(2):
        for s in (1, 3, 2):
            block = origin(half, 0, 0)
            p1[half, s] = remote(
                block, block, p1_ss.at[half, s - 1], p1_rs.at[half, s - 1],
                at_y(s) if half == 0 else at_x(s),
            )
            p1[half, s].start()
    for half in range(2):
        second(half, 0)
    lcp = {}
    for s in (1, 3, 2):
        lcp[s] = remote(lists.at[0], lists.at[s], list_ss.at[s - 1], list_rs.at[s - 1], at_z(s))
        lcp[s].start()

    late = (z == 0) & (c == 0)
    order = (3, lax.select(late, 2, 1), lax.select(late, 1, 2), 0)

    def spread(place, s, p):
        past = lax.broadcasted_iota(jnp.int32, (ROWS, 128), 1) - (CH - 128)
        ones = jnp.where((past >= 0) & (past < 3), 1.0, 0.0)
        rows = pl.ds(pl.multiple_of(place * ROWS, ROWS), ROWS)
        piece = img[s, p].astype(F32)
        for k in range(4):
            j = p * 4 + k
            chunk = piece[:, k * CH : (k + 1) * CH]
            xb[j, rows, 128:PAD] = ones.astype(BF16)
            xb[j, rows, 0:CH] = chunk.astype(BF16)
            full = xb[j, rows, :].astype(F32)
            wb[j, rows, :] = (full * nwp[j]).astype(BF16)

    for p in range(2):
        own[p].wait()
        spread(3, 0, p)

    def mate_copy(half, t):
        u = lax.rem((x if half == 0 else y) + 4 - t, 4)
        if half == 0:
            block = pb.at[lax.rem(u, 2), :, lax.div(u, 2), c, 0]
        else:
            block = pb.at[:, u, :, c, 1]
        pm[half, t] = remote(block, block, pm_ss.at[half, t], pm_rs.at[half, t], mate)
        pm[half, t].start()

    for s in (1, 3, 2):
        for half in range(2):
            p1[half, s].wait_recv()
            second(half, s)
        if s == 1:
            image(1, 1).start()
            image(3, 1).start()
    image(2, 0).start()
    for half in range(2):
        mate_copy(half, 0)
    for s in (0, 1, 3, 2):
        for half in range(2):
            way = 1 if s % 2 == 0 else 3
            p2[half, s, way].wait_recv()
            hop(half, s, way, way)
    image(2, 1).start()

    for t in (1, 3, 2):
        for half in range(2):
            for s in range(4):
                if t == 2 or t != (1 if s % 2 == 0 else 3):
                    p2[half, s, t].wait_recv()
            mate_copy(half, t)
    for s in (1, 2, 3):
        lcp[s].wait_recv()

    def early(k, carry):
        s, p = lax.select(k == 1, order[1], order[0]), lax.div(k, 2)
        image(s, p).wait_recv()
        spread(lax.rem(k, 2), s, p)
        return carry

    lax.fori_loop(0, 3, early, 0)
    for t in range(4):
        for half in range(2):
            pm[half, t].wait_recv()

    def score_copy(s):
        return remote(sbuf.at[s], srecv.at[s - 1], s_ss.at[s - 1], s_rs.at[s - 1], at_z(4 - s))

    def scores(s, n, lanes):
        def body(i, carry):
            start = pl.multiple_of(i * 16, 16)
            listed = [jnp.broadcast_to(lists[s, t : t + 1, :], (16, ROWS)) for t in range(2)]
            chosen = [jnp.zeros((16, ROWS), F32)] * 2
            for k in range(8):
                rows = pl.ds(k * R + start, 16)
                part = cross[n, 0, rows, lanes] + cross[n, 1, rows, lanes]
                for t in range(2):
                    chosen[t] = jnp.where(listed[t] == k, part, chosen[t])
            for t in range(2):
                sbuf[s, t, pl.ds(start, 16), :] = chosen[t]
            return carry

        lax.fori_loop(0, R // 16, body, 0)

    def pair(k, carry):
        i, p = lax.div(k, 2), lax.rem(k, 2)

        @pl.when(k > 0)
        def _():
            s = lax.select(i == 0, order[1], order[2])
            image(s, p).wait_recv()
            spread(1 + i, s, p)

        left = jnp.concatenate([pb[p, t].reshape(8 * R, PAD) for t in range(4)], axis=1)
        rows = pl.ds(pl.multiple_of(2 * i * ROWS, ROWS), 2 * ROWS)
        right = jnp.concatenate([wb[p * 4 + t, rows, :] for t in range(4)], axis=1)
        cross[i, p] = lax.dot_general(
            left, right, (((1,), (1,)), ((), ())), preferred_element_type=F32
        )

        @pl.when(p == 1)
        def _():
            first = lax.select(i == 0, order[0], order[2])
            second = lax.select(i == 0, order[1], order[3])
            scores(first, i, slice(0, ROWS))
            score_copy(first).start()
            scores(second, i, slice(ROWS, 2 * ROWS))

            @pl.when(i == 0)
            def _():
                score_copy(second).start()

        return carry

    lax.fori_loop(0, 4, pair, 0)

    for s in (1, 3, 2):
        score_copy(s).wait_recv()
    score = []
    for slot in range(2):
        prior = jnp.ones((1, ROWS), F32)
        for k in range(8):
            prior = jnp.where(lists[0, slot : slot + 1, :] == k, prior_ref[k], prior)
        total = (sbuf[0, slot] + srecv[0, slot]) + (srecv[1, slot] + srecv[2, slot])
        score.append(total + jnp.log(prior))
    top = jnp.maximum(
        jnp.max(score[0], axis=0, keepdims=True), jnp.max(score[1], axis=0, keepdims=True)
    )
    mass = jnp.sum(jnp.exp(score[0] - top), axis=0, keepdims=True) + jnp.sum(
        jnp.exp(score[1] - top), axis=0, keepdims=True
    )
    evid = top + jnp.log(mass)
    evid_ref[...] = evid
    for slot in range(2):
        post[0, slot] = jnp.exp(score[slot] - evid).astype(BF16)

    def post_copy(s):
        return remote(post.at[0], post.at[s], q_ss.at[s - 1], q_rs.at[s - 1], at_z(s))

    for s in (2, 1, 3):
        post_copy(s).start()

    def expand(place, s):
        lanes = pl.ds(pl.multiple_of(place * ROWS, ROWS), ROWS)

        def body(k, carry):
            kh, kc, kq = lax.div(k, 4), lax.rem(lax.div(k, 2), 2), lax.rem(k, 2)
            value = jnp.zeros((R, ROWS), F32)
            for slot in range(2):
                hit = jnp.broadcast_to(lists[s, slot : slot + 1, :] == k, (R, ROWS))
                value = jnp.where(hit, post[s, slot].astype(F32), value)
            pt[lax.rem(kc + c, 2), kh, kq, :, lanes] = value.astype(BF16)
            return carry

        lax.fori_loop(0, 8, body, 0)

    expand(3, 0)

    def take(place, carry):
        s = lax.select(place == 0, order[0], lax.select(place == 1, order[1], order[2]))
        post_copy(s).wait_recv()
        expand(place, s)
        return carry

    lax.fori_loop(0, 3, take, 0)

    def far(i):
        i = lax.div(i, 2)
        t = lax.rem(3 * i + 2, 4)
        return lax.select(i < 2, t, 3 - t)

    def chunk_of(i):
        return lax.rem(xl + lax.rem(i, 2), 2), lax.rem(y + far(i), 4)

    def mate_sum(i):
        jl, jy = chunk_of(i)
        return remote(mb.at[jl, jy], mr.at[jl, jy], m_ss.at[i], m_rs.at[i], mate)

    def block_x(v, s):
        t = lax.rem(x + s, 4)
        return sb.at[lax.rem(t, 2), lax.rem(y + v, 4), lax.div(t, 2), 0]

    def block_y(v, u, h):
        return sb.at[lax.rem(xl + u, 2), lax.rem(y + v, 4), lax.rem(xh + h, 2), 1]

    def along_x(i, part):
        way = 1 + 2 * lax.rem(i, 2)
        v = far(2 * i)
        shift = (way, 4 - way, 2)[part]
        return remote(
            block_x(v, shift), ra.at[part, i], xa_ss.at[part, i], xa_rs.at[part, i],
            at_x((way, 4 - way, way)[part]),
        )

    def along_y(u, h, part):
        way = 1 + 2 * u
        shift = (way, 4 - way, 2)[part]
        return remote(
            block_y(shift, u, h), rb.at[part, u, h], yb_ss.at[part, u, h], yb_rs.at[part, u, h],
            at_y((way, 4 - way, way)[part]),
        )

    def pass_x(i):
        along_x(i, 2).wait_recv()
        block = block_x(far(2 * i), 1 + 2 * lax.rem(i, 2))
        block[...] = (block[...].astype(F32) + ra[2, i].astype(F32)).astype(BF16)
        along_x(i, 0).start()

    def pass_y(u, h):
        along_y(u, h, 2).wait_recv()
        block = block_y(1 + 2 * u, u, h)
        block[...] = (block[...].astype(F32) + rb[2, u, h].astype(F32)).astype(BF16)
        along_y(u, h, 0).start()

    def product(i):
        jl, jy = chunk_of(i)
        left = pt[...].reshape(8 * R, 4 * ROWS)
        both = jnp.dot(left, xb[jl * 4 + jy], preferred_element_type=F32)
        both = both.reshape(2, 2, 2, R, PAD).astype(BF16)
        mb[jl, jy] = both[1]
        sb[jl, jy] = both[0]
        mate_sum(i).start()

    def join(i):
        jl, jy = chunk_of(i)
        mate_sum(i).wait_recv()
        sb[jl, jy] = (sb[jl, jy].astype(F32) + mr[jl, jy].astype(F32)).astype(BF16)

    def ahead(i, carry):
        product(i)
        return carry

    def steady(i, carry):
        for u in range(2):

            @pl.when(i < 3)
            def _():
                product(2 * i + 2 + u)

            join(2 * i + u)
            for step, part in ((0, 2), (1 + u, u), (2 - u, 1 - u)):
                if part:

                    @pl.when(i == step)
                    def _():
                        along_y(u, 1, part).start()
                        along_y(u, 0, part).start()

            along_x(i, 2 - u).start()
        return carry

    lax.fori_loop(0, 2, ahead, 0)
    lax.fori_loop(0, 4, steady, 0)

    def last_y(v):
        return remote(t2a.at[v], fa.at[v - 1], r2_ss.at[0, v - 1], r2_rs.at[0, v - 1], at_y(v))

    def last_x(s):
        return remote(
            t2b.at[s - 1], fb.at[s - 1], r2_ss.at[1, s - 1], r2_rs.at[1, s - 1], at_x(s)
        )

    def add_x(i):
        along_x(i, 1).wait_recv()
        along_x(i, 0).wait_recv()
        total = block_x(far(2 * i), 0)[...].astype(F32)
        return total + (ra[0, i].astype(F32) + ra[1, i].astype(F32))

    def leave_y(i):
        v = far(2 * i)
        t2a[v] = add_x(i).astype(BF16)
        last_y(v).start()

    def add_y(u, h):
        along_y(u, h, 1).wait_recv()
        along_y(u, h, 0).wait_recv()
        total = block_y(0, u, h)[...].astype(F32)
        return total + (rb[0, u, h].astype(F32) + rb[1, u, h].astype(F32))

    def leave_x(u, h):
        s = 2 if u == 0 else 1 + 2 * lax.rem(xl + h, 2)
        t2b[s - 1] = add_y(u, h).astype(BF16)
        last_x(s).start()

    pass_y(0, 1)
    pass_y(1, 1)
    pass_x(0)
    pass_y(1, 0)
    pass_x(1)
    pass_y(0, 0)
    pass_x(2)
    pass_x(3)
    leave_y(0)
    leave_x(0, 1)
    leave_x(1, 1)
    leave_y(1)
    leave_x(1, 0)
    leave_y(2)
    gb[...] = add_y(0, 0)
    ga[...] = add_x(3)

    for v in (1, 2, 3):
        last_y(v).wait_recv()
    out_ref[0] = (ga[...] + fa[0].astype(F32)) + (fa[1].astype(F32) + fa[2].astype(F32))
    for s in (1, 2, 3):
        last_x(s).wait_recv()
    out_ref[1] = (gb[...] + fb[0].astype(F32)) + (fb[1].astype(F32) + fb[2].astype(F32))

    for group in (p1, lcp, p2, pm):
        for cp in group.values():
            cp.wait_send()
    for s in (1, 2, 3):
        score_copy(s).wait_send()
        post_copy(s).wait_send()
        for p in range(2):
            image(s, p).wait_send()

    def mate_done(i, carry):
        mate_sum(i).wait_send()
        return carry

    lax.fori_loop(0, 8, mate_done, 0)
    for part in range(3):
        for i in range(4):
            along_x(i, part).wait_send()
        for u in range(2):
            for h in range(2):
                along_y(u, h, part).wait_send()
    for s in (1, 2, 3):
        last_y(s).wait_send()
        last_x(s).wait_send()


def finish(sums_ref, evid_ref, out_ref, total_ref, out_evid_ref):
    for q in range(2):
        out_ref[q] = sums_ref[q, :, 0:CH]
        total_ref[q : q + 1, :] = sums_ref[q, :, 128:PAD].T[CH - 128 : CH - 127, :]
    out_evid_ref[...] = evid_ref[...]


def local(images, projections, noise_weights, class_prior, class_lists):
    dma = pltpu.SemaphoreType.DMA
    vmem = pl.BlockSpec(memory_space=pltpu.VMEM)
    sums, evidence = pl.pallas_call(
        kernel,
        name="estep",
        out_shape=(
            jax.ShapeDtypeStruct((2, R, PAD), F32),
            jax.ShapeDtypeStruct((1, ROWS), F32),
        ),
        in_specs=[pl.BlockSpec(memory_space=pl.ANY)] * 5,
        out_specs=(vmem, vmem),
        scratch_shapes=[
            pltpu.VMEM((4, 2, ROWS, PIECE), BF16),
            pltpu.VMEM((4, 2, ROWS), jnp.int32),
            pltpu.VMEM((8, 4 * ROWS, PAD), BF16),
            pltpu.VMEM((8, 4 * ROWS, PAD), BF16),
            pltpu.VMEM((8, 1, PAD), F32),
            pltpu.VMEM((2, 4, 2, 2, 2, R, PAD), BF16),
            pltpu.VMEM((2, 2, 8 * R, 2 * ROWS), F32),
            pltpu.VMEM((4, 2, R, ROWS), F32),
            pltpu.VMEM((3, 2, R, ROWS), F32),
            pltpu.VMEM((4, 2, R, ROWS), BF16),
            pltpu.VMEM((2, 2, 2, R, 4 * ROWS), BF16),
            pltpu.VMEM((2, 4, 2, 2, R, PAD), BF16),
            pltpu.VMEM((2, 4, 2, 2, R, PAD), BF16),
            pltpu.VMEM((2, 4, 2, 2, R, PAD), BF16),
            pltpu.VMEM((3, 4, R, PAD), BF16),
            pltpu.VMEM((3, 2, 2, R, PAD), BF16),
            pltpu.VMEM((4, R, PAD), BF16),
            pltpu.VMEM((3, R, PAD), BF16),
            pltpu.VMEM((R, PAD), F32),
            pltpu.VMEM((R, PAD), F32),
            pltpu.VMEM((3, R, PAD), BF16),
            pltpu.VMEM((3, R, PAD), BF16),
            pltpu.VMEM((2, R, CH), BF16),
            pltpu.VMEM((56, 128), F32),
            pltpu.SMEM((8,), F32),
            dma((4,)),
            dma((2,)),
            dma((3, 2)), dma((3, 2)),
            dma((3,)), dma((3,)),
            dma((2, 3)), dma((2, 3)),
            dma((2, 4, 3)), dma((2, 4, 3)),
            dma((2, 4)), dma((2, 4)),
            dma((3,)), dma((3,)),
            dma((3,)), dma((3,)),
            dma((8,)), dma((8,)),
            dma((3, 4)), dma((3, 4)),
            dma((3, 2, 2)), dma((3, 2, 2)),
            dma((2, 3)), dma((2, 3)),
        ],
        compiler_params=pltpu.CompilerParams(
            collective_id=0, has_side_effects=True, vmem_limit_bytes=56 * 2**20
        ),
    )(images, projections, noise_weights.reshape(56, 128), class_prior, class_lists.T)
    sums, totals, evidence = pl.pallas_call(
        finish,
        name="finish",
        out_shape=(
            jax.ShapeDtypeStruct((2, R, CH), F32),
            jax.ShapeDtypeStruct((2, R), F32),
            jax.ShapeDtypeStruct((1, ROWS), F32),
        ),
        in_specs=[vmem] * 2,
        out_specs=(vmem,) * 3,
    )(sums, evidence)
    return sums, totals, evidence.reshape(ROWS)


def solution(mesh):
    finer = Mesh(mesh.devices.reshape(2, 2, 2, 4, 4), AXES)
    rows, cls, prt = P(AXES, None), ("xh", "c"), ("xl", "z", "y")
    return jax.shard_map(
        local,
        mesh=finer,
        in_specs=(rows, P(cls, None, prt), P(), P(), rows),
        out_specs=(P(cls, None, prt), P(cls, None), P(AXES)),
        check_vma=False,
    )
```

```python
import jax
import jax.numpy as jnp
from jax import lax
from jax.experimental import pallas as pl
from jax.experimental.pallas import tpu as pltpu
from jax.sharding import Mesh
from jax.sharding import PartitionSpec as P

AXES = ("xh", "c", "xl", "z", "y")
MESH = pl.DeviceIdType.MESH
R = 144
ROWS = 128
CH = 224
PAD = 256
PIECE = 4 * CH
F32 = jnp.float32
BF16 = jnp.bfloat16


def kernel(
    img_ref, proj_hbm, nw_hbm, prior_hbm, list_hbm,
    out_ref, evid_ref,
    img, lists, xb, wb, nwp, pb, cross, sbuf, srecv, post, pt,
    mb, mr, sb, ra, rb, t2a, t2b, ga, gb, fa, fb,
    proj_ref, nw_ref, prior_ref, in_sem, own_sem, img_ss, img_rs, list_ss, list_rs, p1_ss, p1_rs, p2_ss, p2_rs, pm_ss, pm_rs,
    s_ss, s_rs, q_ss, q_rs, m_ss, m_rs, xa_ss, xa_rs, yb_ss, yb_rs, r2_ss, r2_rs,
):
    xh, c, xl = lax.axis_index("xh"), lax.axis_index("c"), lax.axis_index("xl")
    z, y = lax.axis_index("z"), lax.axis_index("y")
    x = 2 * xh + xl
    mate = (xh, 1 - c, xl, z, y)

    def at_x(s):
        t = lax.rem(x + s, 4)
        return (lax.div(t, 2), c, lax.rem(t, 2), z, y)

    def at_y(s):
        return (xh, c, xl, z, lax.rem(y + s, 4))

    def at_z(s):
        return (xh, c, xl, lax.rem(z + s, 4), y)

    def remote(src, dst, ss, rs, dev):
        return pltpu.make_async_remote_copy(
            src_ref=src, dst_ref=dst, send_sem=ss, recv_sem=rs, device_id=dev, device_id_type=MESH
        )

    barrier = pltpu.get_barrier_semaphore()
    pl.semaphore_signal(barrier, inc=1, device_id=mate, device_id_type=MESH)
    for s in (1, 2, 3):
        for dev in (at_x(s), at_y(s), at_z(s)):
            pl.semaphore_signal(barrier, inc=1, device_id=dev, device_id_type=MESH)

    inputs = []
    for hbm, ref in (
        (nw_hbm, nw_ref), (proj_hbm, proj_ref), (list_hbm, lists.at[0]), (prior_hbm, prior_ref)
    ):
        inputs.append(pltpu.make_async_copy(hbm, ref, in_sem.at[len(inputs)]))
        inputs[-1].start()
    own = []
    for p in range(2):
        own.append(
            pltpu.make_async_copy(
                img_ref.at[:, pl.ds(pl.multiple_of((p * 4 + z) * PIECE, 128), PIECE)],
                img.at[0, p],
                own_sem.at[p],
            )
        )
        own[p].start()

    pl.semaphore_wait(barrier, 10)

    def image(s, p):
        to = lax.rem(z + s, 4)
        return remote(
            img_ref.at[:, pl.ds(pl.multiple_of((p * 4 + to) * PIECE, 128), PIECE)],
            img.at[s, p],
            img_ss.at[s - 1, p], img_rs.at[s - 1, p], at_z(s),
        )

    lead = lax.select(z >= 2, 2, 1)
    image(lead, 0).start()
    image(3, 0).start()

    inputs[0].wait()
    for p in range(2):
        row = (p * 4 + z) * 7
        flat = jnp.concatenate([nw_ref[pl.ds(row + t, 1), :] for t in range(7)], axis=1)
        for k in range(4):
            j = p * 4 + k
            nwp[j] = jnp.full((1, PAD), -1.0, F32)
            nwp[j, :, 0:CH] = flat[:, k * CH : (k + 1) * CH]

    lane = lax.broadcasted_iota(jnp.int32, (R, 128), 1) - (CH - 128)
    weights = nwp[xl * 4 + y]
    inputs[1].wait()
    for q in range(2):
        pb[xl, y, xh, c, q] = jnp.zeros((R, PAD), BF16)
        pb[xl, y, xh, c, q, :, 0:CH] = proj_ref[q]
        value = pb[xl, y, xh, c, q].astype(F32)
        left = 0.5 * jnp.sum(value * value * weights, axis=1, keepdims=True)
        tail = value[:, 128:PAD]
        for t in range(3):
            term = left.astype(BF16).astype(F32)
            left = left - term
            tail = jnp.where(lane == t, term, tail)
        pb[xl, y, xh, c, q, :, 128:PAD] = tail.astype(BF16)
    inputs[2].wait()
    inputs[3].wait()

    p1, p2, pm = {}, {}, {}

    def origin(half, s, t):
        u, v = (t, s) if half == 0 else (s, t)
        u = lax.rem(x + 4 - u, 4)
        return pb.at[lax.rem(u, 2), lax.rem(y + 4 - v, 4), lax.div(u, 2), c, half]

    def hop(half, s, t, to):
        block, k = origin(half, s, t), (t + to) % 4
        p2[half, s, k] = remote(
            block, block, p2_ss.at[half, s, k - 1], p2_rs.at[half, s, k - 1],
            at_x(to) if half == 0 else at_y(to),
        )
        p2[half, s, k].start()

    def second(half, s):
        for to in (1, 3):
            hop(half, s, 0, to)

    for half in range(2):
        for s in (1, 3, 2):
            block = origin(half, 0, 0)
            p1[half, s] = remote(
                block, block, p1_ss.at[half, s - 1], p1_rs.at[half, s - 1],
                at_y(s) if half == 0 else at_x(s),
            )
            p1[half, s].start()
    for half in range(2):
        second(half, 0)
    lcp = {}
    for s in (1, 3, 2):
        lcp[s] = remote(lists.at[0], lists.at[s], list_ss.at[s - 1], list_rs.at[s - 1], at_z(s))
        lcp[s].start()

    late = z == 0
    order = (3, lax.select(late, 2, 1), lax.select(late, 1, 2), 0)

    def spread(place, s, p):
        past = lax.broadcasted_iota(jnp.int32, (ROWS, 128), 1) - (CH - 128)
        ones = jnp.where((past >= 0) & (past < 3), 1.0, 0.0)
        rows = pl.ds(pl.multiple_of(place * ROWS, ROWS), ROWS)
        piece = img[s, p].astype(F32)
        for k in range(4):
            j = p * 4 + k
            chunk = piece[:, k * CH : (k + 1) * CH]
            xb[j, rows, 128:PAD] = ones.astype(BF16)
            xb[j, rows, 0:CH] = chunk.astype(BF16)
            full = xb[j, rows, :].astype(F32)
            wb[j, rows, :] = (full * nwp[j]).astype(BF16)

    for p in range(2):
        own[p].wait()
        spread(3, 0, p)

    def mate_copy(half, t):
        u = lax.rem((x if half == 0 else y) + 4 - t, 4)
        if half == 0:
            block = pb.at[lax.rem(u, 2), :, lax.div(u, 2), c, 0]
        else:
            block = pb.at[:, u, :, c, 1]
        pm[half, t] = remote(block, block, pm_ss.at[half, t], pm_rs.at[half, t], mate)
        pm[half, t].start()

    for s in (1, 3, 2):
        for half in range(2):
            p1[half, s].wait_recv()
            second(half, s)
        if s == 1:
            image(lead, 1).start()
            image(3, 1).start()
    image(3 - lead, 0).start()
    for half in range(2):
        mate_copy(half, 0)
    for s in (0, 1, 3, 2):
        for half in range(2):
            way = 1 if s % 2 == 0 else 3
            p2[half, s, way].wait_recv()
            hop(half, s, way, way)
    image(3 - lead, 1).start()

    for t in (1, 3, 2):
        for half in range(2):
            for s in range(4):
                if t == 2 or t != (1 if s % 2 == 0 else 3):
                    p2[half, s, t].wait_recv()
            mate_copy(half, t)
    for s in (1, 2, 3):
        lcp[s].wait_recv()

    def early(k, carry):
        s, p = lax.select(k == 1, order[1], order[0]), lax.div(k, 2)
        image(s, p).wait_recv()
        spread(lax.rem(k, 2), s, p)
        return carry

    lax.fori_loop(0, 3, early, 0)
    for t in range(4):
        for half in range(2):
            pm[half, t].wait_recv()

    def score_copy(s):
        return remote(sbuf.at[s], srecv.at[s - 1], s_ss.at[s - 1], s_rs.at[s - 1], at_z(4 - s))

    def scores(s, n, lanes):
        def body(i, carry):
            start = pl.multiple_of(i * 16, 16)
            listed = [jnp.broadcast_to(lists[s, t : t + 1, :], (16, ROWS)) for t in range(2)]
            chosen = [jnp.zeros((16, ROWS), F32)] * 2
            for k in range(8):
                rows = pl.ds(k * R + start, 16)
                part = cross[n, 0, rows, lanes] + cross[n, 1, rows, lanes]
                for t in range(2):
                    chosen[t] = jnp.where(listed[t] == k, part, chosen[t])
            for t in range(2):
                sbuf[s, t, pl.ds(start, 16), :] = chosen[t]
            return carry

        lax.fori_loop(0, R // 16, body, 0)

    def pair(k, carry):
        i, p = lax.div(k, 2), lax.rem(k, 2)

        @pl.when(k > 0)
        def _():
            s = lax.select(i == 0, order[1], order[2])
            image(s, p).wait_recv()
            spread(1 + i, s, p)

        left = jnp.concatenate([pb[p, t].reshape(8 * R, PAD) for t in range(4)], axis=1)
        rows = pl.ds(pl.multiple_of(2 * i * ROWS, ROWS), 2 * ROWS)
        right = jnp.concatenate([wb[p * 4 + t, rows, :] for t in range(4)], axis=1)
        cross[i, p] = lax.dot_general(
            left, right, (((1,), (1,)), ((), ())), preferred_element_type=F32
        )

        @pl.when(p == 1)
        def _():
            first = lax.select(i == 0, order[0], order[2])
            second = lax.select(i == 0, order[1], order[3])
            scores(first, i, slice(0, ROWS))
            score_copy(first).start()
            scores(second, i, slice(ROWS, 2 * ROWS))

            @pl.when(i == 0)
            def _():
                score_copy(second).start()

        return carry

    lax.fori_loop(0, 4, pair, 0)

    for s in (1, 3, 2):
        score_copy(s).wait_recv()
    score = []
    for slot in range(2):
        prior = jnp.ones((1, ROWS), F32)
        for k in range(8):
            prior = jnp.where(lists[0, slot : slot + 1, :] == k, prior_ref[k], prior)
        total = (sbuf[0, slot] + srecv[0, slot]) + (srecv[1, slot] + srecv[2, slot])
        score.append(total + jnp.log(prior))
    top = jnp.maximum(
        jnp.max(score[0], axis=0, keepdims=True), jnp.max(score[1], axis=0, keepdims=True)
    )
    mass = jnp.sum(jnp.exp(score[0] - top), axis=0, keepdims=True) + jnp.sum(
        jnp.exp(score[1] - top), axis=0, keepdims=True
    )
    evid = top + jnp.log(mass)
    evid_ref[...] = evid
    for slot in range(2):
        post[0, slot] = jnp.exp(score[slot] - evid).astype(BF16)

    def post_copy(s):
        return remote(post.at[0], post.at[s], q_ss.at[s - 1], q_rs.at[s - 1], at_z(s))

    for s in (2, 1, 3):
        post_copy(s).start()

    def expand(place, s):
        lanes = pl.ds(pl.multiple_of(place * ROWS, ROWS), ROWS)

        def body(k, carry):
            kh, kc, kq = lax.div(k, 4), lax.rem(lax.div(k, 2), 2), lax.rem(k, 2)
            value = jnp.zeros((R, ROWS), F32)
            for slot in range(2):
                hit = jnp.broadcast_to(lists[s, slot : slot + 1, :] == k, (R, ROWS))
                value = jnp.where(hit, post[s, slot].astype(F32), value)
            pt[lax.rem(kc + c, 2), kh, kq, :, lanes] = value.astype(BF16)
            return carry

        lax.fori_loop(0, 8, body, 0)

    expand(3, 0)

    def take(place, carry):
        s = lax.select(place == 0, order[0], lax.select(place == 1, order[1], order[2]))
        post_copy(s).wait_recv()
        expand(place, s)
        return carry

    lax.fori_loop(0, 3, take, 0)

    def far(i):
        i = lax.div(i, 2)
        t = lax.rem(3 * i + 2, 4)
        return lax.select(i < 2, t, 3 - t)

    def chunk_of(i):
        return lax.rem(xl + lax.rem(i, 2), 2), lax.rem(y + far(i), 4)

    def mate_sum(i):
        jl, jy = chunk_of(i)
        return remote(mb.at[jl, jy], mr.at[jl, jy], m_ss.at[i], m_rs.at[i], mate)

    def block_x(v, s):
        t = lax.rem(x + s, 4)
        return sb.at[lax.rem(t, 2), lax.rem(y + v, 4), lax.div(t, 2), 0]

    def block_y(v, u, h):
        return sb.at[lax.rem(xl + u, 2), lax.rem(y + v, 4), lax.rem(xh + h, 2), 1]

    def along_x(i, part):
        way = 1 + 2 * lax.rem(i, 2)
        v = far(2 * i)
        shift = (way, 4 - way, 2)[part]
        return remote(
            block_x(v, shift), ra.at[part, i], xa_ss.at[part, i], xa_rs.at[part, i],
            at_x((way, 4 - way, way)[part]),
        )

    def along_y(u, h, part):
        way = 1 + 2 * u
        shift = (way, 4 - way, 2)[part]
        return remote(
            block_y(shift, u, h), rb.at[part, u, h], yb_ss.at[part, u, h], yb_rs.at[part, u, h],
            at_y((way, 4 - way, way)[part]),
        )

    def pass_x(i):
        along_x(i, 2).wait_recv()
        block = block_x(far(2 * i), 1 + 2 * lax.rem(i, 2))
        block[...] = (block[...].astype(F32) + ra[2, i].astype(F32)).astype(BF16)
        along_x(i, 0).start()

    def pass_y(u, h):
        along_y(u, h, 2).wait_recv()
        block = block_y(1 + 2 * u, u, h)
        block[...] = (block[...].astype(F32) + rb[2, u, h].astype(F32)).astype(BF16)
        along_y(u, h, 0).start()

    def product(i):
        jl, jy = chunk_of(i)
        left = pt[...].reshape(8 * R, 4 * ROWS)
        both = jnp.dot(left, xb[jl * 4 + jy], preferred_element_type=F32)
        both = both.reshape(2, 2, 2, R, PAD).astype(BF16)
        mb[jl, jy] = both[1]
        sb[jl, jy] = both[0]
        mate_sum(i).start()

    def join(i):
        jl, jy = chunk_of(i)
        mate_sum(i).wait_recv()
        sb[jl, jy] = (sb[jl, jy].astype(F32) + mr[jl, jy].astype(F32)).astype(BF16)

    def ahead(i, carry):
        product(i)
        return carry

    def steady(i, carry):
        for u in range(2):

            @pl.when(i < 3)
            def _():
                product(2 * i + 2 + u)

            join(2 * i + u)
            for step, part in ((0, 2), (1 + u, u), (2 - u, 1 - u)):
                if part:

                    @pl.when(i == step)
                    def _():
                        along_y(u, 1, part).start()
                        along_y(u, 0, part).start()

            along_x(i, 2 - u).start()
        return carry

    lax.fori_loop(0, 2, ahead, 0)
    lax.fori_loop(0, 4, steady, 0)

    def last_y(v):
        return remote(t2a.at[v], fa.at[v - 1], r2_ss.at[0, v - 1], r2_rs.at[0, v - 1], at_y(v))

    def last_x(s):
        return remote(
            t2b.at[s - 1], fb.at[s - 1], r2_ss.at[1, s - 1], r2_rs.at[1, s - 1], at_x(s)
        )

    def add_x(i):
        along_x(i, 1).wait_recv()
        along_x(i, 0).wait_recv()
        total = block_x(far(2 * i), 0)[...].astype(F32)
        return total + (ra[0, i].astype(F32) + ra[1, i].astype(F32))

    def leave_y(i):
        v = far(2 * i)
        t2a[v] = add_x(i).astype(BF16)
        last_y(v).start()

    def add_y(u, h):
        along_y(u, h, 1).wait_recv()
        along_y(u, h, 0).wait_recv()
        total = block_y(0, u, h)[...].astype(F32)
        return total + (rb[0, u, h].astype(F32) + rb[1, u, h].astype(F32))

    def leave_x(u, h):
        s = 2 if u == 0 else 1 + 2 * lax.rem(xl + h, 2)
        t2b[s - 1] = add_y(u, h).astype(BF16)
        last_x(s).start()

    pass_y(0, 1)
    pass_y(1, 1)
    pass_x(0)
    pass_y(1, 0)
    pass_x(1)
    pass_y(0, 0)
    pass_x(2)
    pass_x(3)
    leave_y(0)
    leave_x(0, 1)
    leave_x(1, 1)
    leave_y(1)
    leave_x(1, 0)
    leave_y(2)
    gb[...] = add_y(0, 0)
    ga[...] = add_x(3)

    for v in (1, 2, 3):
        last_y(v).wait_recv()
    out_ref[0] = (ga[...] + fa[0].astype(F32)) + (fa[1].astype(F32) + fa[2].astype(F32))
    for s in (1, 2, 3):
        last_x(s).wait_recv()
    out_ref[1] = (gb[...] + fb[0].astype(F32)) + (fb[1].astype(F32) + fb[2].astype(F32))

    for group in (p1, lcp, p2, pm):
        for cp in group.values():
            cp.wait_send()
    for s in (1, 2, 3):
        score_copy(s).wait_send()
        post_copy(s).wait_send()
        for p in range(2):
            image(s, p).wait_send()

    def mate_done(i, carry):
        mate_sum(i).wait_send()
        return carry

    lax.fori_loop(0, 8, mate_done, 0)
    for part in range(3):
        for i in range(4):
            along_x(i, part).wait_send()
        for u in range(2):
            for h in range(2):
                along_y(u, h, part).wait_send()
    for s in (1, 2, 3):
        last_y(s).wait_send()
        last_x(s).wait_send()


def finish(sums_ref, evid_ref, out_ref, total_ref, out_evid_ref):
    for q in range(2):
        out_ref[q] = sums_ref[q, :, 0:CH]
        total_ref[q : q + 1, :] = sums_ref[q, :, 128:PAD].T[CH - 128 : CH - 127, :]
    out_evid_ref[...] = evid_ref[...]


def local(images, projections, noise_weights, class_prior, class_lists):
    dma = pltpu.SemaphoreType.DMA
    vmem = pl.BlockSpec(memory_space=pltpu.VMEM)
    sums, evidence = pl.pallas_call(
        kernel,
        name="estep",
        out_shape=(
            jax.ShapeDtypeStruct((2, R, PAD), F32),
            jax.ShapeDtypeStruct((1, ROWS), F32),
        ),
        in_specs=[pl.BlockSpec(memory_space=pl.ANY)] * 5,
        out_specs=(vmem, vmem),
        scratch_shapes=[
            pltpu.VMEM((4, 2, ROWS, PIECE), BF16),
            pltpu.VMEM((4, 2, ROWS), jnp.int32),
            pltpu.VMEM((8, 4 * ROWS, PAD), BF16),
            pltpu.VMEM((8, 4 * ROWS, PAD), BF16),
            pltpu.VMEM((8, 1, PAD), F32),
            pltpu.VMEM((2, 4, 2, 2, 2, R, PAD), BF16),
            pltpu.VMEM((2, 2, 8 * R, 2 * ROWS), F32),
            pltpu.VMEM((4, 2, R, ROWS), F32),
            pltpu.VMEM((3, 2, R, ROWS), F32),
            pltpu.VMEM((4, 2, R, ROWS), BF16),
            pltpu.VMEM((2, 2, 2, R, 4 * ROWS), BF16),
            pltpu.VMEM((2, 4, 2, 2, R, PAD), BF16),
            pltpu.VMEM((2, 4, 2, 2, R, PAD), BF16),
            pltpu.VMEM((2, 4, 2, 2, R, PAD), BF16),
            pltpu.VMEM((3, 4, R, PAD), BF16),
            pltpu.VMEM((3, 2, 2, R, PAD), BF16),
            pltpu.VMEM((4, R, PAD), BF16),
            pltpu.VMEM((3, R, PAD), BF16),
            pltpu.VMEM((R, PAD), F32),
            pltpu.VMEM((R, PAD), F32),
            pltpu.VMEM((3, R, PAD), BF16),
            pltpu.VMEM((3, R, PAD), BF16),
            pltpu.VMEM((2, R, CH), BF16),
            pltpu.VMEM((56, 128), F32),
            pltpu.SMEM((8,), F32),
            dma((4,)),
            dma((2,)),
            dma((3, 2)), dma((3, 2)),
            dma((3,)), dma((3,)),
            dma((2, 3)), dma((2, 3)),
            dma((2, 4, 3)), dma((2, 4, 3)),
            dma((2, 4)), dma((2, 4)),
            dma((3,)), dma((3,)),
            dma((3,)), dma((3,)),
            dma((8,)), dma((8,)),
            dma((3, 4)), dma((3, 4)),
            dma((3, 2, 2)), dma((3, 2, 2)),
            dma((2, 3)), dma((2, 3)),
        ],
        compiler_params=pltpu.CompilerParams(
            collective_id=0, has_side_effects=True, vmem_limit_bytes=56 * 2**20
        ),
    )(images, projections, noise_weights.reshape(56, 128), class_prior, class_lists.T)
    sums, totals, evidence = pl.pallas_call(
        finish,
        name="finish",
        out_shape=(
            jax.ShapeDtypeStruct((2, R, CH), F32),
            jax.ShapeDtypeStruct((2, R), F32),
            jax.ShapeDtypeStruct((1, ROWS), F32),
        ),
        in_specs=[vmem] * 2,
        out_specs=(vmem,) * 3,
    )(sums, evidence)
    return sums, totals, evidence.reshape(ROWS)


def solution(mesh):
    finer = Mesh(mesh.devices.reshape(2, 2, 2, 4, 4), AXES)
    rows, cls, prt = P(AXES, None), ("xh", "c"), ("xl", "z", "y")
    return jax.shard_map(
        local,
        mesh=finer,
        in_specs=(rows, P(cls, None, prt), P(), P(), rows),
        out_specs=(P(cls, None, prt), P(cls, None), P(AXES)),
        check_vma=False,
    )
```

```python
import jax
import jax.numpy as jnp
from jax import lax
from jax.experimental import pallas as pl
from jax.experimental.pallas import tpu as pltpu
from jax.sharding import Mesh
from jax.sharding import PartitionSpec as P

AXES = ("xh", "c", "xl", "z", "y")
MESH = pl.DeviceIdType.MESH
R = 144
ROWS = 128
CH = 224
PAD = 256
PIECE = 4 * CH
F32 = jnp.float32
BF16 = jnp.bfloat16


def kernel(
    img_ref, proj_hbm, nw_hbm, prior_hbm, list_hbm,
    out_ref, evid_ref,
    img, lists, xb, wb, nwp, pb, cross, sbuf, srecv, post, pt,
    mb, mr, sb, ra, rb, t2a, t2b, ga, gb, fa, fb,
    proj_ref, nw_ref, prior_ref, in_sem, own_sem, img_ss, img_rs, list_ss, list_rs, p1_ss, p1_rs, p2_ss, p2_rs, pm_ss, pm_rs,
    s_ss, s_rs, q_ss, q_rs, m_ss, m_rs, xa_ss, xa_rs, yb_ss, yb_rs, r2_ss, r2_rs,
):
    xh, c, xl = lax.axis_index("xh"), lax.axis_index("c"), lax.axis_index("xl")
    z, y = lax.axis_index("z"), lax.axis_index("y")
    x = 2 * xh + xl
    mate = (xh, 1 - c, xl, z, y)

    def at_x(s):
        t = lax.rem(x + s, 4)
        return (lax.div(t, 2), c, lax.rem(t, 2), z, y)

    def at_y(s):
        return (xh, c, xl, z, lax.rem(y + s, 4))

    def at_z(s):
        return (xh, c, xl, lax.rem(z + s, 4), y)

    def remote(src, dst, ss, rs, dev):
        return pltpu.make_async_remote_copy(
            src_ref=src, dst_ref=dst, send_sem=ss, recv_sem=rs, device_id=dev, device_id_type=MESH
        )

    barrier = pltpu.get_barrier_semaphore()
    pl.semaphore_signal(barrier, inc=1, device_id=mate, device_id_type=MESH)
    for s in (1, 2, 3):
        for dev in (at_x(s), at_y(s), at_z(s)):
            pl.semaphore_signal(barrier, inc=1, device_id=dev, device_id_type=MESH)

    inputs = []
    for hbm, ref in (
        (nw_hbm, nw_ref), (proj_hbm, proj_ref), (list_hbm, lists.at[0]), (prior_hbm, prior_ref)
    ):
        inputs.append(pltpu.make_async_copy(hbm, ref, in_sem.at[len(inputs)]))
        inputs[-1].start()
    own = []
    for p in range(2):
        own.append(
            pltpu.make_async_copy(
                img_ref.at[:, pl.ds(pl.multiple_of((p * 4 + z) * PIECE, 128), PIECE)],
                img.at[0, p],
                own_sem.at[p],
            )
        )
        own[p].start()

    pl.semaphore_wait(barrier, 10)

    def image(s, p):
        to = lax.rem(z + s, 4)
        return remote(
            img_ref.at[:, pl.ds(pl.multiple_of((p * 4 + to) * PIECE, 128), PIECE)],
            img.at[s, p],
            img_ss.at[s - 1, p], img_rs.at[s - 1, p], at_z(s),
        )

    lead = lax.select(z >= 2, 2, 1)
    image(lead, 0).start()
    image(3, 0).start()

    inputs[0].wait()
    for p in range(2):
        row = (p * 4 + z) * 7
        flat = jnp.concatenate([nw_ref[pl.ds(row + t, 1), :] for t in range(7)], axis=1)
        for k in range(4):
            j = p * 4 + k
            nwp[j] = jnp.full((1, PAD), -1.0, F32)
            nwp[j, :, 0:CH] = flat[:, k * CH : (k + 1) * CH]

    lane = lax.broadcasted_iota(jnp.int32, (R, 128), 1) - (CH - 128)
    weights = nwp[xl * 4 + y]
    inputs[1].wait()
    for q in range(2):
        pb[xl, y, xh, c, q] = jnp.zeros((R, PAD), BF16)
        pb[xl, y, xh, c, q, :, 0:CH] = proj_ref[q]
        value = pb[xl, y, xh, c, q].astype(F32)
        left = 0.5 * jnp.sum(value * value * weights, axis=1, keepdims=True)
        tail = value[:, 128:PAD]
        for t in range(3):
            term = left.astype(BF16).astype(F32)
            left = left - term
            tail = jnp.where(lane == t, term, tail)
        pb[xl, y, xh, c, q, :, 128:PAD] = tail.astype(BF16)
    inputs[2].wait()
    inputs[3].wait()

    p1, p2, pm = {}, {}, {}

    def origin(half, s, t):
        u, v = (t, s) if half == 0 else (s, t)
        u = lax.rem(x + 4 - u, 4)
        return pb.at[lax.rem(u, 2), lax.rem(y + 4 - v, 4), lax.div(u, 2), c, half]

    def hop(half, s, t, to):
        block, k = origin(half, s, t), (t + to) % 4
        p2[half, s, k] = remote(
            block, block, p2_ss.at[half, s, k - 1], p2_rs.at[half, s, k - 1],
            at_x(to) if half == 0 else at_y(to),
        )
        p2[half, s, k].start()

    def second(half, s):
        for to in (1, 3):
            hop(half, s, 0, to)

    for half in range(2):
        for s in (1, 3, 2):
            block = origin(half, 0, 0)
            p1[half, s] = remote(
                block, block, p1_ss.at[half, s - 1], p1_rs.at[half, s - 1],
                at_y(s) if half == 0 else at_x(s),
            )
            p1[half, s].start()
    for half in range(2):
        second(half, 0)
    lcp = {}
    for s in (1, 3, 2):
        lcp[s] = remote(lists.at[0], lists.at[s], list_ss.at[s - 1], list_rs.at[s - 1], at_z(s))
        lcp[s].start()

    order = (
        lax.select(z == 1, 1, 3),
        lax.select(z < 2, 2, 1),
        lax.select(z == 0, 1, lax.select(z == 1, 3, 2)),
        0,
    )

    def spread(place, s, p):
        past = lax.broadcasted_iota(jnp.int32, (ROWS, 128), 1) - (CH - 128)
        ones = jnp.where((past >= 0) & (past < 3), 1.0, 0.0)
        rows = pl.ds(pl.multiple_of(place * ROWS, ROWS), ROWS)
        piece = img[s, p].astype(F32)
        for k in range(4):
            j = p * 4 + k
            chunk = piece[:, k * CH : (k + 1) * CH]
            xb[j, rows, 128:PAD] = ones.astype(BF16)
            xb[j, rows, 0:CH] = chunk.astype(BF16)
            full = xb[j, rows, :].astype(F32)
            wb[j, rows, :] = (full * nwp[j]).astype(BF16)

    for p in range(2):
        own[p].wait()
        spread(3, 0, p)

    def mate_copy(half, t):
        u = lax.rem((x if half == 0 else y) + 4 - t, 4)
        if half == 0:
            block = pb.at[lax.rem(u, 2), :, lax.div(u, 2), c, 0]
        else:
            block = pb.at[:, u, :, c, 1]
        pm[half, t] = remote(block, block, pm_ss.at[half, t], pm_rs.at[half, t], mate)
        pm[half, t].start()

    for s in (1, 3, 2):
        for half in range(2):
            p1[half, s].wait_recv()
            second(half, s)
        if s == 1:
            image(lead, 1).start()
            image(3, 1).start()
    image(3 - lead, 0).start()
    for half in range(2):
        mate_copy(half, 0)
    for s in (0, 1, 3, 2):
        for half in range(2):
            way = 1 if s % 2 == 0 else 3
            p2[half, s, way].wait_recv()
            hop(half, s, way, way)
    image(3 - lead, 1).start()

    for t in (1, 3, 2):
        for half in range(2):
            for s in range(4):
                if t == 2 or t != (1 if s % 2 == 0 else 3):
                    p2[half, s, t].wait_recv()
            mate_copy(half, t)
    for s in (1, 2, 3):
        lcp[s].wait_recv()

    def early(k, carry):
        s, p = lax.select(k == 1, order[1], order[0]), lax.div(k, 2)
        image(s, p).wait_recv()
        spread(lax.rem(k, 2), s, p)
        return carry

    lax.fori_loop(0, 3, early, 0)
    for t in range(4):
        for half in range(2):
            pm[half, t].wait_recv()

    def score_copy(s):
        return remote(sbuf.at[s], srecv.at[s - 1], s_ss.at[s - 1], s_rs.at[s - 1], at_z(4 - s))

    def scores(s, n, lanes):
        def body(i, carry):
            start = pl.multiple_of(i * 16, 16)
            listed = [jnp.broadcast_to(lists[s, t : t + 1, :], (16, ROWS)) for t in range(2)]
            chosen = [jnp.zeros((16, ROWS), F32)] * 2
            for k in range(8):
                rows = pl.ds(k * R + start, 16)
                part = cross[n, 0, rows, lanes] + cross[n, 1, rows, lanes]
                for t in range(2):
                    chosen[t] = jnp.where(listed[t] == k, part, chosen[t])
            for t in range(2):
                sbuf[s, t, pl.ds(start, 16), :] = chosen[t]
            return carry

        lax.fori_loop(0, R // 16, body, 0)

    def pair(k, carry):
        i, p = lax.div(k, 2), lax.rem(k, 2)

        @pl.when(k > 0)
        def _():
            s = lax.select(i == 0, order[1], order[2])
            image(s, p).wait_recv()
            spread(1 + i, s, p)

        left = jnp.concatenate([pb[p, t].reshape(8 * R, PAD) for t in range(4)], axis=1)
        rows = pl.ds(pl.multiple_of(2 * i * ROWS, ROWS), 2 * ROWS)
        right = jnp.concatenate([wb[p * 4 + t, rows, :] for t in range(4)], axis=1)
        cross[i, p] = lax.dot_general(
            left, right, (((1,), (1,)), ((), ())), preferred_element_type=F32
        )

        @pl.when(p == 1)
        def _():
            first = lax.select(i == 0, order[0], order[2])
            second = lax.select(i == 0, order[1], order[3])
            scores(first, i, slice(0, ROWS))
            score_copy(first).start()
            scores(second, i, slice(ROWS, 2 * ROWS))

            @pl.when(i == 0)
            def _():
                score_copy(second).start()

        return carry

    lax.fori_loop(0, 4, pair, 0)

    for s in (1, 3, 2):
        score_copy(s).wait_recv()
    score = []
    for slot in range(2):
        prior = jnp.ones((1, ROWS), F32)
        for k in range(8):
            prior = jnp.where(lists[0, slot : slot + 1, :] == k, prior_ref[k], prior)
        total = (sbuf[0, slot] + srecv[0, slot]) + (srecv[1, slot] + srecv[2, slot])
        score.append(total + jnp.log(prior))
    top = jnp.maximum(
        jnp.max(score[0], axis=0, keepdims=True), jnp.max(score[1], axis=0, keepdims=True)
    )
    mass = jnp.sum(jnp.exp(score[0] - top), axis=0, keepdims=True) + jnp.sum(
        jnp.exp(score[1] - top), axis=0, keepdims=True
    )
    evid = top + jnp.log(mass)
    evid_ref[...] = evid
    for slot in range(2):
        post[0, slot] = jnp.exp(score[slot] - evid).astype(BF16)

    def post_copy(s):
        return remote(post.at[0], post.at[s], q_ss.at[s - 1], q_rs.at[s - 1], at_z(s))

    for s in (2, 1, 3):
        post_copy(s).start()

    def expand(place, s):
        lanes = pl.ds(pl.multiple_of(place * ROWS, ROWS), ROWS)

        def body(k, carry):
            kh, kc, kq = lax.div(k, 4), lax.rem(lax.div(k, 2), 2), lax.rem(k, 2)
            value = jnp.zeros((R, ROWS), F32)
            for slot in range(2):
                hit = jnp.broadcast_to(lists[s, slot : slot + 1, :] == k, (R, ROWS))
                value = jnp.where(hit, post[s, slot].astype(F32), value)
            pt[lax.rem(kc + c, 2), kh, kq, :, lanes] = value.astype(BF16)
            return carry

        lax.fori_loop(0, 8, body, 0)

    expand(3, 0)

    def take(place, carry):
        s = lax.select(place == 0, order[0], lax.select(place == 1, order[1], order[2]))
        post_copy(s).wait_recv()
        expand(place, s)
        return carry

    lax.fori_loop(0, 3, take, 0)

    def far(i):
        i = lax.div(i, 2)
        t = lax.rem(3 * i + 2, 4)
        return lax.select(i < 2, t, 3 - t)

    def chunk_of(i):
        return lax.rem(xl + lax.rem(i, 2), 2), lax.rem(y + far(i), 4)

    def mate_sum(i):
        jl, jy = chunk_of(i)
        return remote(mb.at[jl, jy], mr.at[jl, jy], m_ss.at[i], m_rs.at[i], mate)

    def block_x(v, s):
        t = lax.rem(x + s, 4)
        return sb.at[lax.rem(t, 2), lax.rem(y + v, 4), lax.div(t, 2), 0]

    def block_y(v, u, h):
        return sb.at[lax.rem(xl + u, 2), lax.rem(y + v, 4), lax.rem(xh + h, 2), 1]

    def along_x(i, part):
        way = 1 + 2 * lax.rem(i, 2)
        v = far(2 * i)
        shift = (way, 4 - way, 2)[part]
        return remote(
            block_x(v, shift), ra.at[part, i], xa_ss.at[part, i], xa_rs.at[part, i],
            at_x((way, 4 - way, way)[part]),
        )

    def along_y(u, h, part):
        way = 1 + 2 * u
        shift = (way, 4 - way, 2)[part]
        return remote(
            block_y(shift, u, h), rb.at[part, u, h], yb_ss.at[part, u, h], yb_rs.at[part, u, h],
            at_y((way, 4 - way, way)[part]),
        )

    def pass_x(i):
        along_x(i, 2).wait_recv()
        block = block_x(far(2 * i), 1 + 2 * lax.rem(i, 2))
        block[...] = (block[...].astype(F32) + ra[2, i].astype(F32)).astype(BF16)
        along_x(i, 0).start()

    def pass_y(u, h):
        along_y(u, h, 2).wait_recv()
        block = block_y(1 + 2 * u, u, h)
        block[...] = (block[...].astype(F32) + rb[2, u, h].astype(F32)).astype(BF16)
        along_y(u, h, 0).start()

    def product(i):
        jl, jy = chunk_of(i)
        left = pt[...].reshape(8 * R, 4 * ROWS)
        both = jnp.dot(left, xb[jl * 4 + jy], preferred_element_type=F32)
        both = both.reshape(2, 2, 2, R, PAD).astype(BF16)
        mb[jl, jy] = both[1]
        sb[jl, jy] = both[0]
        mate_sum(i).start()

    def join(i):
        jl, jy = chunk_of(i)
        mate_sum(i).wait_recv()
        sb[jl, jy] = (sb[jl, jy].astype(F32) + mr[jl, jy].astype(F32)).astype(BF16)

    def ahead(i, carry):
        product(i)
        return carry

    def steady(i, carry):
        for u in range(2):

            @pl.when(i < 3)
            def _():
                product(2 * i + 2 + u)

            join(2 * i + u)
            for step, part in ((0, 2), (1 + u, u), (2 - u, 1 - u)):
                if part:

                    @pl.when(i == step)
                    def _():
                        along_y(u, 1, part).start()
                        along_y(u, 0, part).start()

            along_x(i, 2 - u).start()
        return carry

    lax.fori_loop(0, 2, ahead, 0)
    lax.fori_loop(0, 4, steady, 0)

    def last_y(v):
        return remote(t2a.at[v], fa.at[v - 1], r2_ss.at[0, v - 1], r2_rs.at[0, v - 1], at_y(v))

    def last_x(s):
        return remote(
            t2b.at[s - 1], fb.at[s - 1], r2_ss.at[1, s - 1], r2_rs.at[1, s - 1], at_x(s)
        )

    def add_x(i):
        along_x(i, 1).wait_recv()
        along_x(i, 0).wait_recv()
        total = block_x(far(2 * i), 0)[...].astype(F32)
        return total + (ra[0, i].astype(F32) + ra[1, i].astype(F32))

    def leave_y(i):
        v = far(2 * i)
        t2a[v] = add_x(i).astype(BF16)
        last_y(v).start()

    def add_y(u, h):
        along_y(u, h, 1).wait_recv()
        along_y(u, h, 0).wait_recv()
        total = block_y(0, u, h)[...].astype(F32)
        return total + (rb[0, u, h].astype(F32) + rb[1, u, h].astype(F32))

    def leave_x(u, h):
        s = 2 if u == 0 else 1 + 2 * lax.rem(xl + h, 2)
        t2b[s - 1] = add_y(u, h).astype(BF16)
        last_x(s).start()

    pass_y(0, 1)
    pass_y(1, 1)
    pass_x(0)
    pass_y(1, 0)
    pass_x(1)
    pass_y(0, 0)
    pass_x(2)
    pass_x(3)
    leave_y(0)
    leave_x(0, 1)
    leave_x(1, 1)
    leave_y(1)
    leave_x(1, 0)
    leave_y(2)
    gb[...] = add_y(0, 0)
    ga[...] = add_x(3)

    for v in (1, 2, 3):
        last_y(v).wait_recv()
    out_ref[0] = (ga[...] + fa[0].astype(F32)) + (fa[1].astype(F32) + fa[2].astype(F32))
    for s in (1, 2, 3):
        last_x(s).wait_recv()
    out_ref[1] = (gb[...] + fb[0].astype(F32)) + (fb[1].astype(F32) + fb[2].astype(F32))

    for group in (p1, lcp, p2, pm):
        for cp in group.values():
            cp.wait_send()
    for s in (1, 2, 3):
        score_copy(s).wait_send()
        post_copy(s).wait_send()
        for p in range(2):
            image(s, p).wait_send()

    def mate_done(i, carry):
        mate_sum(i).wait_send()
        return carry

    lax.fori_loop(0, 8, mate_done, 0)
    for part in range(3):
        for i in range(4):
            along_x(i, part).wait_send()
        for u in range(2):
            for h in range(2):
                along_y(u, h, part).wait_send()
    for s in (1, 2, 3):
        last_y(s).wait_send()
        last_x(s).wait_send()


def finish(sums_ref, evid_ref, out_ref, total_ref, out_evid_ref):
    for q in range(2):
        out_ref[q] = sums_ref[q, :, 0:CH]
        total_ref[q : q + 1, :] = sums_ref[q, :, 128:PAD].T[CH - 128 : CH - 127, :]
    out_evid_ref[...] = evid_ref[...]


def local(images, projections, noise_weights, class_prior, class_lists):
    dma = pltpu.SemaphoreType.DMA
    vmem = pl.BlockSpec(memory_space=pltpu.VMEM)
    sums, evidence = pl.pallas_call(
        kernel,
        name="estep",
        out_shape=(
            jax.ShapeDtypeStruct((2, R, PAD), F32),
            jax.ShapeDtypeStruct((1, ROWS), F32),
        ),
        in_specs=[pl.BlockSpec(memory_space=pl.ANY)] * 5,
        out_specs=(vmem, vmem),
        scratch_shapes=[
            pltpu.VMEM((4, 2, ROWS, PIECE), BF16),
            pltpu.VMEM((4, 2, ROWS), jnp.int32),
            pltpu.VMEM((8, 4 * ROWS, PAD), BF16),
            pltpu.VMEM((8, 4 * ROWS, PAD), BF16),
            pltpu.VMEM((8, 1, PAD), F32),
            pltpu.VMEM((2, 4, 2, 2, 2, R, PAD), BF16),
            pltpu.VMEM((2, 2, 8 * R, 2 * ROWS), F32),
            pltpu.VMEM((4, 2, R, ROWS), F32),
            pltpu.VMEM((3, 2, R, ROWS), F32),
            pltpu.VMEM((4, 2, R, ROWS), BF16),
            pltpu.VMEM((2, 2, 2, R, 4 * ROWS), BF16),
            pltpu.VMEM((2, 4, 2, 2, R, PAD), BF16),
            pltpu.VMEM((2, 4, 2, 2, R, PAD), BF16),
            pltpu.VMEM((2, 4, 2, 2, R, PAD), BF16),
            pltpu.VMEM((3, 4, R, PAD), BF16),
            pltpu.VMEM((3, 2, 2, R, PAD), BF16),
            pltpu.VMEM((4, R, PAD), BF16),
            pltpu.VMEM((3, R, PAD), BF16),
            pltpu.VMEM((R, PAD), F32),
            pltpu.VMEM((R, PAD), F32),
            pltpu.VMEM((3, R, PAD), BF16),
            pltpu.VMEM((3, R, PAD), BF16),
            pltpu.VMEM((2, R, CH), BF16),
            pltpu.VMEM((56, 128), F32),
            pltpu.SMEM((8,), F32),
            dma((4,)),
            dma((2,)),
            dma((3, 2)), dma((3, 2)),
            dma((3,)), dma((3,)),
            dma((2, 3)), dma((2, 3)),
            dma((2, 4, 3)), dma((2, 4, 3)),
            dma((2, 4)), dma((2, 4)),
            dma((3,)), dma((3,)),
            dma((3,)), dma((3,)),
            dma((8,)), dma((8,)),
            dma((3, 4)), dma((3, 4)),
            dma((3, 2, 2)), dma((3, 2, 2)),
            dma((2, 3)), dma((2, 3)),
        ],
        compiler_params=pltpu.CompilerParams(
            collective_id=0, has_side_effects=True, vmem_limit_bytes=56 * 2**20
        ),
    )(images, projections, noise_weights.reshape(56, 128), class_prior, class_lists.T)
    sums, totals, evidence = pl.pallas_call(
        finish,
        name="finish",
        out_shape=(
            jax.ShapeDtypeStruct((2, R, CH), F32),
            jax.ShapeDtypeStruct((2, R), F32),
            jax.ShapeDtypeStruct((1, ROWS), F32),
        ),
        in_specs=[vmem] * 2,
        out_specs=(vmem,) * 3,
    )(sums, evidence)
    return sums, totals, evidence.reshape(ROWS)


def solution(mesh):
    finer = Mesh(mesh.devices.reshape(2, 2, 2, 4, 4), AXES)
    rows, cls, prt = P(AXES, None), ("xh", "c"), ("xl", "z", "y")
    return jax.shard_map(
        local,
        mesh=finer,
        in_specs=(rows, P(cls, None, prt), P(), P(), rows),
        out_specs=(P(cls, None, prt), P(cls, None), P(AXES)),
        check_vma=False,
    )
```

```python
import jax
import jax.numpy as jnp
from jax import lax
from jax.experimental import pallas as pl
from jax.experimental.pallas import tpu as pltpu
from jax.sharding import Mesh
from jax.sharding import PartitionSpec as P

AXES = ("xh", "c", "xl", "z", "y")
MESH = pl.DeviceIdType.MESH
R = 144
ROWS = 128
CH = 224
PAD = 256
PIECE = 4 * CH
F32 = jnp.float32
BF16 = jnp.bfloat16


def kernel(
    img_ref, proj_hbm, nw_hbm, prior_hbm, list_hbm,
    out_ref, evid_ref,
    img, lists, xb, wb, nwp, pb, cross, sbuf, srecv, post, pt,
    mb, mr, sb, ra, rb, t2a, t2b, ga, gb, fa, fb,
    proj_ref, nw_ref, prior_ref, in_sem, own_sem, img_ss, img_rs, list_ss, list_rs, p1_ss, p1_rs, p2_ss, p2_rs, pm_ss, pm_rs,
    s_ss, s_rs, q_ss, q_rs, m_ss, m_rs, xa_ss, xa_rs, yb_ss, yb_rs, r2_ss, r2_rs,
):
    xh, c, xl = lax.axis_index("xh"), lax.axis_index("c"), lax.axis_index("xl")
    z, y = lax.axis_index("z"), lax.axis_index("y")
    x = 2 * xh + xl
    mate = (xh, 1 - c, xl, z, y)

    def at_x(s):
        t = lax.rem(x + s, 4)
        return (lax.div(t, 2), c, lax.rem(t, 2), z, y)

    def at_y(s):
        return (xh, c, xl, z, lax.rem(y + s, 4))

    def at_z(s):
        return (xh, c, xl, lax.rem(z + s, 4), y)

    def remote(src, dst, ss, rs, dev):
        return pltpu.make_async_remote_copy(
            src_ref=src, dst_ref=dst, send_sem=ss, recv_sem=rs, device_id=dev, device_id_type=MESH
        )

    barrier = pltpu.get_barrier_semaphore()
    pl.semaphore_signal(barrier, inc=1, device_id=mate, device_id_type=MESH)
    for s in (1, 2, 3):
        for dev in (at_x(s), at_y(s), at_z(s)):
            pl.semaphore_signal(barrier, inc=1, device_id=dev, device_id_type=MESH)

    inputs = []
    for hbm, ref in (
        (nw_hbm, nw_ref), (proj_hbm, proj_ref), (list_hbm, lists.at[0]), (prior_hbm, prior_ref)
    ):
        inputs.append(pltpu.make_async_copy(hbm, ref, in_sem.at[len(inputs)]))
        inputs[-1].start()
    own = []
    for p in range(2):
        own.append(
            pltpu.make_async_copy(
                img_ref.at[:, pl.ds(pl.multiple_of((p * 4 + z) * PIECE, 128), PIECE)],
                img.at[0, p],
                own_sem.at[p],
            )
        )
        own[p].start()

    pl.semaphore_wait(barrier, 10)

    def image(s, p):
        to = lax.rem(z + s, 4)
        return remote(
            img_ref.at[:, pl.ds(pl.multiple_of((p * 4 + to) * PIECE, 128), PIECE)],
            img.at[s, p],
            img_ss.at[s - 1, p], img_rs.at[s - 1, p], at_z(s),
        )

    lead = lax.select((z >= 2) & (c == 0), 2, 1)
    image(lead, 0).start()
    image(3, 0).start()

    inputs[0].wait()
    for p in range(2):
        row = (p * 4 + z) * 7
        flat = jnp.concatenate([nw_ref[pl.ds(row + t, 1), :] for t in range(7)], axis=1)
        for k in range(4):
            j = p * 4 + k
            nwp[j] = jnp.full((1, PAD), -1.0, F32)
            nwp[j, :, 0:CH] = flat[:, k * CH : (k + 1) * CH]

    lane = lax.broadcasted_iota(jnp.int32, (R, 128), 1) - (CH - 128)
    weights = nwp[xl * 4 + y]
    inputs[1].wait()
    for q in range(2):
        pb[xl, y, xh, c, q] = jnp.zeros((R, PAD), BF16)
        pb[xl, y, xh, c, q, :, 0:CH] = proj_ref[q]
        value = pb[xl, y, xh, c, q].astype(F32)
        left = 0.5 * jnp.sum(value * value * weights, axis=1, keepdims=True)
        tail = value[:, 128:PAD]
        for t in range(3):
            term = left.astype(BF16).astype(F32)
            left = left - term
            tail = jnp.where(lane == t, term, tail)
        pb[xl, y, xh, c, q, :, 128:PAD] = tail.astype(BF16)
    inputs[2].wait()
    inputs[3].wait()

    p1, p2, pm = {}, {}, {}

    def origin(half, s, t):
        u, v = (t, s) if half == 0 else (s, t)
        u = lax.rem(x + 4 - u, 4)
        return pb.at[lax.rem(u, 2), lax.rem(y + 4 - v, 4), lax.div(u, 2), c, half]

    def hop(half, s, t, to):
        block, k = origin(half, s, t), (t + to) % 4
        p2[half, s, k] = remote(
            block, block, p2_ss.at[half, s, k - 1], p2_rs.at[half, s, k - 1],
            at_x(to) if half == 0 else at_y(to),
        )
        p2[half, s, k].start()

    def second(half, s):
        for to in (1, 3):
            hop(half, s, 0, to)

    for half in range(2):
        for s in (1, 3, 2):
            block = origin(half, 0, 0)
            p1[half, s] = remote(
                block, block, p1_ss.at[half, s - 1], p1_rs.at[half, s - 1],
                at_y(s) if half == 0 else at_x(s),
            )
            p1[half, s].start()
    for half in range(2):
        second(half, 0)
    lcp = {}
    for s in (1, 3, 2):
        lcp[s] = remote(lists.at[0], lists.at[s], list_ss.at[s - 1], list_rs.at[s - 1], at_z(s))
        lcp[s].start()

    late = (z == 0) & (c == 0)
    order = (3, lax.select(late, 2, 1), lax.select(late, 1, 2), 0)

    def spread(place, s, p):
        past = lax.broadcasted_iota(jnp.int32, (ROWS, 128), 1) - (CH - 128)
        ones = jnp.where((past >= 0) & (past < 3), 1.0, 0.0)
        rows = pl.ds(pl.multiple_of(place * ROWS, ROWS), ROWS)
        piece = img[s, p].astype(F32)
        for k in range(4):
            j = p * 4 + k
            chunk = piece[:, k * CH : (k + 1) * CH]
            xb[j, rows, 128:PAD] = ones.astype(BF16)
            xb[j, rows, 0:CH] = chunk.astype(BF16)
            full = xb[j, rows, :].astype(F32)
            wb[j, rows, :] = (full * nwp[j]).astype(BF16)

    for p in range(2):
        own[p].wait()
        spread(3, 0, p)

    def mate_copy(half, t):
        u = lax.rem((x if half == 0 else y) + 4 - t, 4)
        if half == 0:
            block = pb.at[lax.rem(u, 2), :, lax.div(u, 2), c, 0]
        else:
            block = pb.at[:, u, :, c, 1]
        pm[half, t] = remote(block, block, pm_ss.at[half, t], pm_rs.at[half, t], mate)
        pm[half, t].start()

    for s in (1, 3, 2):
        for half in range(2):
            p1[half, s].wait_recv()
            second(half, s)
        if s == 1:
            image(lead, 1).start()
            image(3, 1).start()
    image(3 - lead, 0).start()
    for half in range(2):
        mate_copy(half, 0)
    for s in (0, 1, 3, 2):
        for half in range(2):
            way = 1 if s % 2 == 0 else 3
            p2[half, s, way].wait_recv()
            hop(half, s, way, way)
    image(3 - lead, 1).start()

    for t in (1, 3, 2):
        for half in range(2):
            for s in range(4):
                if t == 2 or t != (1 if s % 2 == 0 else 3):
                    p2[half, s, t].wait_recv()
            mate_copy(half, t)
    for s in (1, 2, 3):
        lcp[s].wait_recv()

    def early(k, carry):
        s, p = lax.select(k == 1, order[1], order[0]), lax.div(k, 2)
        image(s, p).wait_recv()
        spread(lax.rem(k, 2), s, p)
        return carry

    lax.fori_loop(0, 3, early, 0)
    for t in range(4):
        for half in range(2):
            pm[half, t].wait_recv()

    def score_copy(s):
        return remote(sbuf.at[s], srecv.at[s - 1], s_ss.at[s - 1], s_rs.at[s - 1], at_z(4 - s))

    def scores(s, n, lanes):
        def body(i, carry):
            start = pl.multiple_of(i * 16, 16)
            listed = [jnp.broadcast_to(lists[s, t : t + 1, :], (16, ROWS)) for t in range(2)]
            chosen = [jnp.zeros((16, ROWS), F32)] * 2
            for k in range(8):
                rows = pl.ds(k * R + start, 16)
                part = cross[n, 0, rows, lanes] + cross[n, 1, rows, lanes]
                for t in range(2):
                    chosen[t] = jnp.where(listed[t] == k, part, chosen[t])
            for t in range(2):
                sbuf[s, t, pl.ds(start, 16), :] = chosen[t]
            return carry

        lax.fori_loop(0, R // 16, body, 0)

    def pair(k, carry):
        i, p = lax.div(k, 2), lax.rem(k, 2)

        @pl.when(k > 0)
        def _():
            s = lax.select(i == 0, order[1], order[2])
            image(s, p).wait_recv()
            spread(1 + i, s, p)

        left = jnp.concatenate([pb[p, t].reshape(8 * R, PAD) for t in range(4)], axis=1)
        rows = pl.ds(pl.multiple_of(2 * i * ROWS, ROWS), 2 * ROWS)
        right = jnp.concatenate([wb[p * 4 + t, rows, :] for t in range(4)], axis=1)
        cross[i, p] = lax.dot_general(
            left, right, (((1,), (1,)), ((), ())), preferred_element_type=F32
        )

        @pl.when(p == 1)
        def _():
            first = lax.select(i == 0, order[0], order[2])
            second = lax.select(i == 0, order[1], order[3])
            scores(first, i, slice(0, ROWS))
            score_copy(first).start()
            scores(second, i, slice(ROWS, 2 * ROWS))

            @pl.when(i == 0)
            def _():
                score_copy(second).start()

        return carry

    lax.fori_loop(0, 4, pair, 0)

    for s in (1, 3, 2):
        score_copy(s).wait_recv()
    score = []
    for slot in range(2):
        prior = jnp.ones((1, ROWS), F32)
        for k in range(8):
            prior = jnp.where(lists[0, slot : slot + 1, :] == k, prior_ref[k], prior)
        total = (sbuf[0, slot] + srecv[0, slot]) + (srecv[1, slot] + srecv[2, slot])
        score.append(total + jnp.log(prior))
    top = jnp.maximum(
        jnp.max(score[0], axis=0, keepdims=True), jnp.max(score[1], axis=0, keepdims=True)
    )
    mass = jnp.sum(jnp.exp(score[0] - top), axis=0, keepdims=True) + jnp.sum(
        jnp.exp(score[1] - top), axis=0, keepdims=True
    )
    evid = top + jnp.log(mass)
    evid_ref[...] = evid
    for slot in range(2):
        post[0, slot] = jnp.exp(score[slot] - evid).astype(BF16)

    def post_copy(s):
        return remote(post.at[0], post.at[s], q_ss.at[s - 1], q_rs.at[s - 1], at_z(s))

    for s in (2, 1, 3):
        post_copy(s).start()

    def expand(place, s):
        lanes = pl.ds(pl.multiple_of(place * ROWS, ROWS), ROWS)

        def body(k, carry):
            kh, kc, kq = lax.div(k, 4), lax.rem(lax.div(k, 2), 2), lax.rem(k, 2)
            value = jnp.zeros((R, ROWS), F32)
            for slot in range(2):
                hit = jnp.broadcast_to(lists[s, slot : slot + 1, :] == k, (R, ROWS))
                value = jnp.where(hit, post[s, slot].astype(F32), value)
            pt[lax.rem(kc + c, 2), kh, kq, :, lanes] = value.astype(BF16)
            return carry

        lax.fori_loop(0, 8, body, 0)

    expand(3, 0)

    def take(place, carry):
        s = lax.select(place == 0, order[0], lax.select(place == 1, order[1], order[2]))
        post_copy(s).wait_recv()
        expand(place, s)
        return carry

    lax.fori_loop(0, 3, take, 0)

    def far(i):
        i = lax.div(i, 2)
        t = lax.rem(3 * i + 2, 4)
        return lax.select(i < 2, t, 3 - t)

    def chunk_of(i):
        return lax.rem(xl + lax.rem(i, 2), 2), lax.rem(y + far(i), 4)

    def mate_sum(i):
        jl, jy = chunk_of(i)
        return remote(mb.at[jl, jy], mr.at[jl, jy], m_ss.at[i], m_rs.at[i], mate)

    def block_x(v, s):
        t = lax.rem(x + s, 4)
        return sb.at[lax.rem(t, 2), lax.rem(y + v, 4), lax.div(t, 2), 0]

    def block_y(v, u, h):
        return sb.at[lax.rem(xl + u, 2), lax.rem(y + v, 4), lax.rem(xh + h, 2), 1]

    def along_x(i, part):
        way = 1 + 2 * lax.rem(i, 2)
        v = far(2 * i)
        shift = (way, 4 - way, 2)[part]
        return remote(
            block_x(v, shift), ra.at[part, i], xa_ss.at[part, i], xa_rs.at[part, i],
            at_x((way, 4 - way, way)[part]),
        )

    def along_y(u, h, part):
        way = 1 + 2 * u
        shift = (way, 4 - way, 2)[part]
        return remote(
            block_y(shift, u, h), rb.at[part, u, h], yb_ss.at[part, u, h], yb_rs.at[part, u, h],
            at_y((way, 4 - way, way)[part]),
        )

    def pass_x(i):
        along_x(i, 2).wait_recv()
        block = block_x(far(2 * i), 1 + 2 * lax.rem(i, 2))
        block[...] = (block[...].astype(F32) + ra[2, i].astype(F32)).astype(BF16)
        along_x(i, 0).start()

    def pass_y(u, h):
        along_y(u, h, 2).wait_recv()
        block = block_y(1 + 2 * u, u, h)
        block[...] = (block[...].astype(F32) + rb[2, u, h].astype(F32)).astype(BF16)
        along_y(u, h, 0).start()

    def product(i):
        jl, jy = chunk_of(i)
        left = pt[...].reshape(8 * R, 4 * ROWS)
        both = jnp.dot(left, xb[jl * 4 + jy], preferred_element_type=F32)
        both = both.reshape(2, 2, 2, R, PAD).astype(BF16)
        mb[jl, jy] = both[1]
        sb[jl, jy] = both[0]
        mate_sum(i).start()

    def join(i):
        jl, jy = chunk_of(i)
        mate_sum(i).wait_recv()
        sb[jl, jy] = (sb[jl, jy].astype(F32) + mr[jl, jy].astype(F32)).astype(BF16)

    def ahead(i, carry):
        product(i)
        return carry

    def steady(i, carry):
        for u in range(2):

            @pl.when(i < 3)
            def _():
                product(2 * i + 2 + u)

            join(2 * i + u)
            for step, part in ((0, 2), (1 + u, u), (2 - u, 1 - u)):
                if part:

                    @pl.when(i == step)
                    def _():
                        along_y(u, 1, part).start()
                        along_y(u, 0, part).start()

            along_x(i, 2 - u).start()
        return carry

    lax.fori_loop(0, 2, ahead, 0)
    lax.fori_loop(0, 4, steady, 0)

    def last_y(v):
        return remote(t2a.at[v], fa.at[v - 1], r2_ss.at[0, v - 1], r2_rs.at[0, v - 1], at_y(v))

    def last_x(s):
        return remote(
            t2b.at[s - 1], fb.at[s - 1], r2_ss.at[1, s - 1], r2_rs.at[1, s - 1], at_x(s)
        )

    def add_x(i):
        along_x(i, 1).wait_recv()
        along_x(i, 0).wait_recv()
        total = block_x(far(2 * i), 0)[...].astype(F32)
        return total + (ra[0, i].astype(F32) + ra[1, i].astype(F32))

    def leave_y(i):
        v = far(2 * i)
        t2a[v] = add_x(i).astype(BF16)
        last_y(v).start()

    def add_y(u, h):
        along_y(u, h, 1).wait_recv()
        along_y(u, h, 0).wait_recv()
        total = block_y(0, u, h)[...].astype(F32)
        return total + (rb[0, u, h].astype(F32) + rb[1, u, h].astype(F32))

    def leave_x(u, h):
        s = 2 if u == 0 else 1 + 2 * lax.rem(xl + h, 2)
        t2b[s - 1] = add_y(u, h).astype(BF16)
        last_x(s).start()

    pass_y(0, 1)
    pass_y(1, 1)
    pass_x(0)
    pass_y(1, 0)
    pass_x(1)
    pass_y(0, 0)
    pass_x(2)
    pass_x(3)
    leave_y(0)
    leave_x(0, 1)
    leave_x(1, 1)
    leave_y(1)
    leave_x(1, 0)
    leave_y(2)
    gb[...] = add_y(0, 0)
    ga[...] = add_x(3)

    for v in (1, 2, 3):
        last_y(v).wait_recv()
    out_ref[0] = (ga[...] + fa[0].astype(F32)) + (fa[1].astype(F32) + fa[2].astype(F32))
    for s in (1, 2, 3):
        last_x(s).wait_recv()
    out_ref[1] = (gb[...] + fb[0].astype(F32)) + (fb[1].astype(F32) + fb[2].astype(F32))

    for group in (p1, lcp, p2, pm):
        for cp in group.values():
            cp.wait_send()
    for s in (1, 2, 3):
        score_copy(s).wait_send()
        post_copy(s).wait_send()
        for p in range(2):
            image(s, p).wait_send()

    def mate_done(i, carry):
        mate_sum(i).wait_send()
        return carry

    lax.fori_loop(0, 8, mate_done, 0)
    for part in range(3):
        for i in range(4):
            along_x(i, part).wait_send()
        for u in range(2):
            for h in range(2):
                along_y(u, h, part).wait_send()
    for s in (1, 2, 3):
        last_y(s).wait_send()
        last_x(s).wait_send()


def finish(sums_ref, evid_ref, out_ref, total_ref, out_evid_ref):
    for q in range(2):
        out_ref[q] = sums_ref[q, :, 0:CH]
        total_ref[q : q + 1, :] = sums_ref[q, :, 128:PAD].T[CH - 128 : CH - 127, :]
    out_evid_ref[...] = evid_ref[...]


def local(images, projections, noise_weights, class_prior, class_lists):
    dma = pltpu.SemaphoreType.DMA
    vmem = pl.BlockSpec(memory_space=pltpu.VMEM)
    sums, evidence = pl.pallas_call(
        kernel,
        name="estep",
        out_shape=(
            jax.ShapeDtypeStruct((2, R, PAD), F32),
            jax.ShapeDtypeStruct((1, ROWS), F32),
        ),
        in_specs=[pl.BlockSpec(memory_space=pl.ANY)] * 5,
        out_specs=(vmem, vmem),
        scratch_shapes=[
            pltpu.VMEM((4, 2, ROWS, PIECE), BF16),
            pltpu.VMEM((4, 2, ROWS), jnp.int32),
            pltpu.VMEM((8, 4 * ROWS, PAD), BF16),
            pltpu.VMEM((8, 4 * ROWS, PAD), BF16),
            pltpu.VMEM((8, 1, PAD), F32),
            pltpu.VMEM((2, 4, 2, 2, 2, R, PAD), BF16),
            pltpu.VMEM((2, 2, 8 * R, 2 * ROWS), F32),
            pltpu.VMEM((4, 2, R, ROWS), F32),
            pltpu.VMEM((3, 2, R, ROWS), F32),
            pltpu.VMEM((4, 2, R, ROWS), BF16),
            pltpu.VMEM((2, 2, 2, R, 4 * ROWS), BF16),
            pltpu.VMEM((2, 4, 2, 2, R, PAD), BF16),
            pltpu.VMEM((2, 4, 2, 2, R, PAD), BF16),
            pltpu.VMEM((2, 4, 2, 2, R, PAD), BF16),
            pltpu.VMEM((3, 4, R, PAD), BF16),
            pltpu.VMEM((3, 2, 2, R, PAD), BF16),
            pltpu.VMEM((4, R, PAD), BF16),
            pltpu.VMEM((3, R, PAD), BF16),
            pltpu.VMEM((R, PAD), F32),
            pltpu.VMEM((R, PAD), F32),
            pltpu.VMEM((3, R, PAD), BF16),
            pltpu.VMEM((3, R, PAD), BF16),
            pltpu.VMEM((2, R, CH), BF16),
            pltpu.VMEM((56, 128), F32),
            pltpu.SMEM((8,), F32),
            dma((4,)),
            dma((2,)),
            dma((3, 2)), dma((3, 2)),
            dma((3,)), dma((3,)),
            dma((2, 3)), dma((2, 3)),
            dma((2, 4, 3)), dma((2, 4, 3)),
            dma((2, 4)), dma((2, 4)),
            dma((3,)), dma((3,)),
            dma((3,)), dma((3,)),
            dma((8,)), dma((8,)),
            dma((3, 4)), dma((3, 4)),
            dma((3, 2, 2)), dma((3, 2, 2)),
            dma((2, 3)), dma((2, 3)),
        ],
        compiler_params=pltpu.CompilerParams(
            collective_id=0, has_side_effects=True, vmem_limit_bytes=56 * 2**20
        ),
    )(images, projections, noise_weights.reshape(56, 128), class_prior, class_lists.T)
    sums, totals, evidence = pl.pallas_call(
        finish,
        name="finish",
        out_shape=(
            jax.ShapeDtypeStruct((2, R, CH), F32),
            jax.ShapeDtypeStruct((2, R), F32),
            jax.ShapeDtypeStruct((1, ROWS), F32),
        ),
        in_specs=[vmem] * 2,
        out_specs=(vmem,) * 3,
    )(sums, evidence)
    return sums, totals, evidence.reshape(ROWS)


def solution(mesh):
    finer = Mesh(mesh.devices.reshape(2, 2, 2, 4, 4), AXES)
    rows, cls, prt = P(AXES, None), ("xh", "c"), ("xl", "z", "y")
    return jax.shard_map(
        local,
        mesh=finer,
        in_specs=(rows, P(cls, None, prt), P(), P(), rows),
        out_specs=(P(cls, None, prt), P(cls, None), P(AXES)),
        check_vma=False,
    )
```
